32 devices in a mesh: section: 2 (over y), fsdp: 4 (over x, core), dp: 4 (over z).
Axes of the slice: x: 2, y: 2, z: 4, core: 2. Of those that a mesh axis runs over, the one named last changes fastest.
Arguments:
- images: bfloat16 [32, 65, 384], P(('fsdp', 'dp')), may hold values from -6 to 6
- slot_image: int32 [16, 2], P(('fsdp', 'dp')), may hold values from 0 to 1, each once within a row
- cotangent: bfloat16 [32, 65, 384], P(('fsdp', 'dp')), may hold values from -6 to 6
- pre_gain: bfloat16 [2, 384], P('section', 'fsdp'), may hold values from 0.099609375 to 1.8984375
- pre_shift: bfloat16 [2, 384], P('section', 'fsdp'), may hold values from -1.5 to 1.5
- heads_weight: bfloat16 [2, 384, 1152], P('section', 'fsdp'), may hold values from -0.4375 to 0.4375
- query_bias: bfloat16 [2, 384], P('section', 'fsdp'), may hold values from -1.5 to 1.5
- value_bias: bfloat16 [2, 384], P('section', 'fsdp'), may hold values from -1.5 to 1.5
- merge_weight: bfloat16 [2, 384, 384], P('section', 'fsdp'), may hold values from -0.875 to 0.875
- merge_bias: bfloat16 [2, 384], P('section', 'fsdp'), may hold values from -1.5 to 1.5
- mid_gain: bfloat16 [2, 384], P('section', 'fsdp'), may hold values from 0.099609375 to 1.8984375
- mid_shift: bfloat16 [2, 384], P('section', 'fsdp'), may hold values from -1.5 to 1.5
- up_weight: bfloat16 [2, 384, 1536], P('section', 'fsdp'), may hold values from -0.3125 to 0.3125
- up_bias: bfloat16 [2, 1536], P('section', 'fsdp'), may hold values from -1.5 to 1.5
- down_weight: bfloat16 [2, 1536, 384], P('section', 'fsdp'), may hold values from -0.21875 to 0.21875
- down_bias: bfloat16 [2, 384], P('section', 'fsdp'), may hold values from -1.5 to 1.5
Outputs:
- layer_outputs: bfloat16 [2, 32, 65, 384], P('section', ('fsdp', 'dp'))
- input_grads: float32 [2, 32, 65, 384], P('section', ('fsdp', 'dp'))
- grad_pre_gain: float32 [2, 384], P('section', 'fsdp')
- grad_pre_shift: float32 [2, 384], P('section', 'fsdp')
- grad_heads_weight: float32 [2, 384, 1152], P('section', 'fsdp')
- grad_query_bias: float32 [2, 384], P('section', 'fsdp')
- grad_value_bias: float32 [2, 384], P('section', 'fsdp')
- grad_merge_weight: float32 [2, 384, 384], P('section', 'fsdp')
- grad_merge_bias: float32 [2, 384], P('section', 'fsdp')
- grad_mid_gain: float32 [2, 384], P('section', 'fsdp')
- grad_mid_shift: float32 [2, 384], P('section', 'fsdp')
- grad_up_weight: float32 [2, 384, 1536], P('section', 'fsdp')
- grad_up_bias: float32 [2, 1536], P('section', 'fsdp')
- grad_down_weight: float32 [2, 1536, 384], P('section', 'fsdp')
- grad_down_bias: float32 [2, 384], P('section', 'fsdp')
The draws below stay inside these ranges and needn't reach their ends.
All inputs are finite; a program needn't handle non-finite values.
Results may differ from the reference program's by a relative error of at most 0.024.
Values may be sent and summed in bfloat16 or wider, within the bound.
No kernel may reach another device: no remote copies, remote signals or barrier semaphores. Data moves between devices by JAX's collectives and lax.ppermute only.
A program may use at most 64 MiB of HBM per device.

```python
import jax
import jax.numpy as jnp
from jax import lax

D = 384
HEADS = 6
HD = 64
FF = 1536
SEQ = 65
MICRO = 2
ROWS = 16
IMAGES = 32


def levels(stream_key, shape, cuts, smallest, high):
    level = 1.0
    for axis_at, parts in cuts:
        draws = jax.random.uniform(jax.random.fold_in(jax.random.fold_in(stream_key, 6), axis_at), (parts,), jnp.float32, smallest / len(cuts), high / len(cuts))
        level = level * jnp.repeat(jnp.exp(draws), shape[axis_at] // parts).reshape((-1,) + (1,) * (len(shape) - 1 - axis_at))
    return level


def centred(key, shape, width, reach, cuts=(), held_as=jnp.bfloat16):
    values = width * jax.random.normal(key, shape, jnp.float32)
    if cuts:
        values = values * levels(key, shape, cuts, -0.22, 0.18)
    return jnp.clip(values, -reach, reach).astype(held_as)


def setup_inputs(seed: int = 0) -> dict:
    key_of = jax.random.split(jax.random.key(seed), 17)
    return {
        "images": centred(key_of[0], (IMAGES, SEQ, D), 1.0, 6.0, ((0, 16),)),
        "slot_image": jax.vmap(lambda own: jax.random.permutation(own, MICRO))(jax.random.split(key_of[1], ROWS)).reshape((ROWS, MICRO)).astype(jnp.int32),
        "cotangent": centred(key_of[2], (IMAGES, SEQ, D), 1.0, 6.0, ((0, 16),)),
        "pre_gain": jnp.clip(1.0 + 0.18 * jax.random.normal(key_of[3], (2, D), jnp.float32), 0.099609375, 1.8984375).astype(jnp.bfloat16),
        "pre_shift": centred(key_of[4], (2, D), 0.3, 1.5, ((0, 2), (1, 4))),
        "heads_weight": centred(key_of[5], (2, D, 3 * D), (D // 2) ** -0.5, 0.4375, ((0, 2), (1, 4))),
        "query_bias": centred(key_of[6], (2, D), 0.3, 1.5, ((0, 2), (1, 4))),
        "value_bias": centred(key_of[7], (2, D), 0.3, 1.5, ((0, 2), (1, 4))),
        "merge_weight": centred(key_of[8], (2, D, D), (D // 8) ** -0.5, 0.875, ((0, 2), (1, 4))),
        "merge_bias": centred(key_of[9], (2, D), 0.3, 1.5, ((0, 2), (1, 4))),
        "mid_gain": jnp.clip(1.0 + 0.18 * jax.random.normal(key_of[10], (2, D), jnp.float32), 0.099609375, 1.8984375).astype(jnp.bfloat16),
        "mid_shift": centred(key_of[11], (2, D), 0.3, 1.5, ((0, 2), (1, 4))),
        "up_weight": centred(key_of[12], (2, D, FF), D ** -0.5, 0.3125, ((0, 2), (1, 4))),
        "up_bias": centred(key_of[13], (2, FF), 0.3, 1.5, ((0, 2), (1, 4))),
        "down_weight": centred(key_of[14], (2, FF, D), (FF // 2) ** -0.5, 0.21875, ((0, 2), (1, 4))),
        "down_bias": centred(key_of[15], (2, D), 0.3, 1.5, ((0, 2), (1, 4))),
    }


EPS = 1e-06
HIGH = lax.Precision.HIGHEST

@jax.custom_vjp
def low(v):
    return lax.optimization_barrier(v.astype(jnp.bfloat16)).astype(jnp.float32)

@jax.custom_vjp
def low_back(v):
    return v

def low_keep(v):
    return (low(v), None)

def low_pass(kept, grad):
    return (grad,)

def back_keep(v):
    return (v, None)

def back_low(kept, grad):
    return (low(grad),)
low.defvjp(low_keep, low_pass)
low_back.defvjp(back_keep, back_low)

def norm_rows(rows_in, gain_vec, shift_vec):
    row_mean = lax.optimization_barrier(jnp.mean(rows_in, axis=-1, keepdims=True))
    centered = rows_in - row_mean
    row_var = lax.optimization_barrier(jnp.mean(centered * centered, axis=-1, keepdims=True))
    return centered * lax.rsqrt(row_var + EPS) * gain_vec + shift_vec

def one_layer(inputs, weights):
    pre_gain, pre_shift, heads_weight, query_bias, value_bias, merge_weight, merge_bias, mid_gain, mid_shift, up_weight, up_bias, down_weight, down_bias = weights
    count = inputs.shape[0]
    normed_one = low(norm_rows(inputs, pre_gain, pre_shift))
    bias_all = jnp.concatenate([query_bias, jnp.zeros_like(query_bias), value_bias])
    packed = jnp.einsum('isd,de->ise', normed_one, heads_weight, precision=HIGH) + bias_all
    packed = low_back(low(packed)).reshape(count, SEQ, 3, HEADS, HD)
    queries = packed[:, :, 0]
    key_rows = packed[:, :, 1]
    values = packed[:, :, 2]
    scores = low_back(jnp.einsum('iqhd,ikhd->ihqk', queries, key_rows, precision=HIGH) * HD ** (-0.5))
    attn_probs = low(jax.nn.softmax(scores, axis=-1))
    mixed_heads = jnp.einsum('ihqk,ikhd->iqhd', attn_probs, values, precision=HIGH).reshape(count, SEQ, D)
    mixed_heads = low_back(low(mixed_heads))
    branch_out = low_back(jnp.einsum('isd,de->ise', mixed_heads, merge_weight, precision=HIGH) + merge_bias)
    middle = inputs + branch_out
    normed_two = low(norm_rows(middle, mid_gain, mid_shift))
    hidden = low_back(jnp.einsum('isd,df->isf', normed_two, up_weight, precision=HIGH) + up_bias)
    activated = low(jax.nn.gelu(hidden, approximate=False))
    mlp_out = low_back(jnp.einsum('isf,fd->isd', activated, down_weight, precision=HIGH) + down_bias)
    return middle + mlp_out

def forward(picked, section_bump, layer_zero, layer_one):
    group_size = 16

    def group(carried, pieces):
        part_in, part_bump = pieces
        out_first = one_layer(part_in, layer_zero)
        out_second = one_layer(low_back(low(out_first) + part_bump), layer_one)
        return (carried, (out_second, low(out_first)))
    grouped = (picked.reshape(-1, group_size, SEQ, D), section_bump.reshape(-1, group_size, SEQ, D))
    _, (second_out, first_out) = lax.scan(jax.checkpoint(group), jnp.float32(0.0), grouped)
    return (second_out.reshape(IMAGES, SEQ, D), first_out.reshape(IMAGES, SEQ, D))

def reference(images, slot_image, cotangent, pre_gain, pre_shift, heads_weight, query_bias, value_bias, merge_weight, merge_bias, mid_gain, mid_shift, up_weight, up_bias, down_weight, down_bias):
    row_count = slot_image.shape[0]
    per_device = images.astype(jnp.float32).reshape(row_count, MICRO, SEQ, D)
    index_table = slot_image.astype(jnp.int32)[:, :, None, None]
    picked = jnp.take_along_axis(per_device, index_table, axis=1).reshape(IMAGES, SEQ, D)
    stacked = (pre_gain, pre_shift, heads_weight, query_bias, value_bias, merge_weight, merge_bias, mid_gain, mid_shift, up_weight, up_bias, down_weight, down_bias)
    layer_zero = tuple((member[0].astype(jnp.float32) for member in stacked))
    layer_one = tuple((member[1].astype(jnp.float32) for member in stacked))
    section_bump = jnp.zeros((IMAGES, SEQ, D), jnp.float32)
    out_second, vjp_fn, out_first = jax.vjp(forward, picked, section_bump, layer_zero, layer_one, has_aux=True)
    grad_picked, grad_bump, grads_zero, grads_one = vjp_fn(cotangent.astype(jnp.float32))
    layer_outputs = jnp.stack([out_first, out_second]).astype(jnp.bfloat16)
    input_grads = jnp.stack([grad_picked, grad_bump])
    weight_grads = tuple((jnp.stack([first_grad, second_grad]) for first_grad, second_grad in zip(grads_zero, grads_one)))
    return (layer_outputs, input_grads, weight_grads[0], weight_grads[1], weight_grads[2], weight_grads[3], weight_grads[4], weight_grads[5], weight_grads[6], weight_grads[7], weight_grads[8], weight_grads[9], weight_grads[10], weight_grads[11], weight_grads[12])
```

```python
import functools

import jax
import jax.numpy as jnp
from jax import lax
from jax.experimental import pallas as pl
from jax.experimental.pallas import tpu as pltpu
from jax.sharding import PartitionSpec as P

HD = 64
PAIR = 2 * HD
EPS = 1e-06
SQRT_HALF = 0.7071067811865476
INV_ROOT_TAU = 0.3989422804014327
BF = jnp.bfloat16
F32 = jnp.float32
VMEM_BYTES = 28 * 1024 * 1024

PRE_GAIN, PRE_SHIFT, QUERY_BIAS, VALUE_BIAS, MERGE_BIAS, MID_GAIN, MID_SHIFT, DOWN_BIAS = range(8)


def padded_length(length):
    return -(-length // 16) * 16


def dot(a, b):
    return jnp.dot(a, b, preferred_element_type=F32)


def dot_nt(a, b):
    return lax.dot_general(a, b, (((1,), (1,)), ((), ())), preferred_element_type=F32)


def dot_tn(a, b):
    return lax.dot_general(a, b, (((0,), (0,)), ((), ())), preferred_element_type=F32)


def fetch(pieces, dest, sems, first, me):
    copies = []
    for k, piece in enumerate(pieces):
        rows = piece.shape[0]
        start = pl.multiple_of(jnp.bitwise_xor(me, k) * rows, rows)
        copies.append(pltpu.make_async_copy(piece, dest.at[pl.ds(start, rows)], sems.at[first + k]))
    for copy in copies:
        copy.start()
    return copies


def arrive(copies):
    for copy in copies:
        copy.wait()


def pad_images(images, scratch):
    length = images[0].shape[0]
    step = padded_length(length)
    scratch[...] = jnp.zeros_like(scratch)
    for n, image in enumerate(images):
        scratch[n * step : n * step + length, :] = image.astype(F32)
    return scratch[...]


def unpad(ref, rows, kind):
    count, length, _ = ref.shape
    step = padded_length(length)
    for n in range(count):
        ref[n] = rows[n * step : n * step + length, :].astype(kind)


def norm_parts(rows):
    mean = jnp.mean(rows, axis=-1, keepdims=True)
    centered = rows - mean
    inverse = lax.rsqrt(jnp.mean(centered * centered, axis=-1, keepdims=True) + EPS)
    return centered * inverse, inverse


def norm_backward(grad_rows, normed, inverse, gain):
    scaled = grad_rows * gain
    mean_one = jnp.mean(scaled, axis=-1, keepdims=True)
    mean_two = jnp.mean(scaled * normed, axis=-1, keepdims=True)
    return inverse * (scaled - mean_one - normed * mean_two)


def column_sum(rows):
    return jnp.sum(rows, axis=0, keepdims=True)


def half_masks():
    lane = lax.broadcasted_iota(jnp.int32, (1, PAIR), 1)
    low = (lane < HD).astype(F32)
    return low.astype(BF), (1.0 - low).astype(BF)


def both_heads(rows):
    low, high = half_masks()
    return jnp.concatenate([rows * low, rows * high], axis=0)


def beside(stacked):
    half = stacked.shape[0] // 2
    lane = lax.broadcasted_iota(jnp.int32, (half, PAIR), 1)
    return jnp.where(lane < HD, stacked[:half], stacked[half:])


def qkv(packed, n, pair, step, width):
    rows = slice(n * step, (n + 1) * step)
    return tuple(packed[rows, part * width + pair * PAIR : part * width + (pair + 1) * PAIR] for part in range(3))


def head_probs(queries, keys, length):
    stacked = both_heads(queries)
    scores = dot_nt(stacked, keys) * HD**-0.5
    lane = lax.broadcasted_iota(jnp.int32, scores.shape, 1)
    scores = jnp.where(lane < length, scores, -1e30)
    grown = jnp.exp(scores - jnp.max(scores, axis=-1, keepdims=True))
    return grown * (1.0 / jnp.sum(grown, axis=-1, keepdims=True)), stacked


def attention_forward(packed, mixed, count, length, width):
    step = padded_length(length)
    for n in range(count):
        for pair in range(width // PAIR):
            queries, keys, values = qkv(packed, n, pair, step, width)
            probs, _ = head_probs(queries, keys, length)
            out = beside(dot(probs.astype(BF), values)).astype(BF)
            mixed[n * step : (n + 1) * step, pair * PAIR : (pair + 1) * PAIR] = out


def attention_backward(packed, grad_mixed, grad_packed, count, length, width):
    step = padded_length(length)
    for n in range(count):
        for pair in range(width // PAIR):
            queries, keys, values = qkv(packed, n, pair, step, width)
            probs, stacked = head_probs(queries, keys, length)
            rows = slice(n * step, (n + 1) * step)
            incoming = both_heads(grad_mixed[rows, pair * PAIR : (pair + 1) * PAIR])
            grad_probs = dot_nt(incoming, values)
            inner = jnp.sum(probs * grad_probs, axis=-1, keepdims=True)
            grad_scores = (probs * (grad_probs - inner)).astype(BF)
            parts = (
                beside(dot(grad_scores, keys)) * HD**-0.5,
                dot_tn(grad_scores, stacked) * HD**-0.5,
                dot_tn(probs.astype(BF), incoming),
            )
            for part, value in enumerate(parts):
                column = part * width + pair * PAIR
                grad_packed[rows, column : column + PAIR] = value.astype(BF)


def entry_rows(rows, small):
    normed, inverse = norm_parts(rows)
    return (normed * small[PRE_GAIN : PRE_GAIN + 1] + small[PRE_SHIFT : PRE_SHIFT + 1]).astype(BF), normed, inverse


def mid_rows(middle, small):
    normed, inverse = norm_parts(middle)
    return (normed * small[MID_GAIN : MID_GAIN + 1] + small[MID_SHIFT : MID_SHIFT + 1]).astype(BF), normed, inverse


def packed_bias(small):
    query = small[QUERY_BIAS : QUERY_BIAS + 1]
    return jnp.concatenate([query, jnp.zeros_like(query), small[VALUE_BIAS : VALUE_BIAS + 1]], axis=1)


def attention_half(rows, small, heads, merge, packed, mixed, count, length, waits):
    width = rows.shape[1]
    entry, _, _ = entry_rows(rows, small)
    arrive(waits[0])
    packed[...] = (dot(entry, heads[...]) + packed_bias(small)).astype(BF)
    attention_forward(packed, mixed, count, length, width)
    arrive(waits[1])
    return rows + dot(mixed[...], merge[...]) + small[MERGE_BIAS : MERGE_BIAS + 1]


def gelu_parts(hidden):
    bell = 0.5 * (1.0 + lax.erf(hidden * SQRT_HALF))
    return hidden * bell, bell


def gelu_slope(hidden, bell):
    return bell + hidden * jnp.exp(-0.5 * hidden * hidden) * INV_ROOT_TAU


def picked_images(info, images):
    return [
        jnp.where(info[2 + n] == 0, images[0], images[1]) for n in range(images.shape[0])
    ]


def attend_kernel(shards, info, images, small, *refs):
    heads_pieces, merge_pieces = refs[:shards], refs[shards : 2 * shards]
    middle_ref, mid_ref, heads, merge, rows_ref, packed, mixed, sems = refs[2 * shards :]
    me = info[0]
    waits = (fetch(heads_pieces, heads, sems, 0, me), fetch(merge_pieces, merge, sems, shards, me))
    count, length, _ = images.shape
    rows = pad_images(picked_images(info, images), rows_ref)
    middle = attention_half(rows, small, heads, merge, packed, mixed, count, length, waits)
    middle_ref[...] = middle
    mid_ref[...] = mid_rows(middle, small)[0]


def widen_kernel(shards, info, mid_ref, up_bias, *refs):
    act_ref, up, sems = refs[shards:]
    arrive(fetch(refs[:shards], up, sems, 0, info[0]))
    hidden = dot(mid_ref[...], up[...]) + up_bias[...]
    act_ref[...] = gelu_parts(hidden)[0].astype(BF)


def narrow_kernel(shards, info, act_ref, middle_ref, small, *refs):
    out_ref, down, sems = refs[shards:]
    arrive(fetch(refs[:shards], down, sems, 0, info[0]))
    out = middle_ref[...] + dot(act_ref[...], down[...]) + small[DOWN_BIAS : DOWN_BIAS + 1]
    unpad(out_ref, out, BF)


def both_ways_kernel(shards, info, images, arrived, cotangent, small, up_bias, *refs):
    pieces = [refs[n * shards : (n + 1) * shards] for n in range(4)]
    out_ref, sent_ref, packed, mixed, middle_ref, act_ref = refs[4 * shards : 4 * shards + 6]
    heads, merge, up, down, rows_ref, grad_ref, grad_packed, sems = refs[4 * shards + 6 :]
    me, leading = info[0], info[1] == 0
    waits = [
        fetch(piece, dest, sems, n * shards, me) for n, (piece, dest) in enumerate(zip(pieces, (heads, merge, up, down)))
    ]
    count, length, width = images.shape
    source = [jnp.where(leading, image, arrived[n]) for n, image in enumerate(picked_images(info, images))]
    rows = pad_images(source, rows_ref)
    middle = attention_half(rows, small, heads, merge, packed, mixed, count, length, waits)
    middle_ref[...] = middle
    mid, unit_two, inverse_two = mid_rows(middle, small)
    arrive(waits[2])
    hidden = dot(mid, up[...]) + up_bias[...]
    act, bell = gelu_parts(hidden)
    slope = gelu_slope(hidden, bell)
    act_ref[...] = act.astype(BF)
    arrive(waits[3])
    out = middle + dot(act_ref[...], down[...]) + small[DOWN_BIAS : DOWN_BIAS + 1]
    unpad(out_ref, out, BF)
    incoming = pad_images([cotangent[n] for n in range(count)], grad_ref)
    grad_hidden = (dot_nt(incoming.astype(BF), down[...]) * slope).astype(BF)
    grad_mid = dot_nt(grad_hidden, up[...])
    grad_middle = incoming + norm_backward(grad_mid, unit_two, inverse_two, small[MID_GAIN : MID_GAIN + 1])
    grad_mixed = dot_nt(grad_middle.astype(BF), merge[...]).astype(BF)
    attention_backward(packed, grad_mixed, grad_packed, count, length, width)
    grad_entry = dot_nt(grad_packed[...], heads[...])
    _, unit_one, inverse_one = entry_rows(rows, small)
    grad_in = grad_middle + norm_backward(grad_entry, unit_one, inverse_one, small[PRE_GAIN : PRE_GAIN + 1])
    unpad(sent_ref, grad_in, BF)


def own_gradient(info, returned, cotangent, scratch):
    leading = info[1] == 0
    return pad_images(
        [jnp.where(leading, returned[n], cotangent[n]) for n in range(cotangent.shape[0])], scratch
    )


def down_grad_kernel(shards, info, returned, cotangent, act_ref, *refs):
    outs, grad_ref = refs[:shards], refs[shards]
    incoming = own_gradient(info, returned, cotangent, grad_ref).astype(BF)
    rows = outs[0].shape[0]
    for k in range(shards):
        start = pl.multiple_of(jnp.bitwise_xor(info[0], k) * rows, rows)
        outs[k][...] = dot_tn(act_ref[:, pl.ds(start, rows)], incoming).astype(BF)


def up_grad_kernel(shards, info, returned, cotangent, middle_ref, small, up_bias, *refs):
    pieces = (refs[:shards], refs[shards : 2 * shards])
    outs = refs[2 * shards : 3 * shards]
    hidden_ref, up, down, grad_ref, whole, sems = refs[3 * shards :]
    me = info[0]
    waits = [fetch(piece, dest, sems, n * shards, me) for n, (piece, dest) in enumerate(zip(pieces, (up, down)))]
    incoming = own_gradient(info, returned, cotangent, grad_ref).astype(BF)
    mid, _, _ = mid_rows(middle_ref[...], small)
    arrive(waits[0])
    hidden = dot(mid, up[...]) + up_bias[...]
    slope = gelu_slope(hidden, gelu_parts(hidden)[1])
    arrive(waits[1])
    hidden_ref[...] = (dot_nt(incoming, down[...]) * slope).astype(BF)
    whole[...] = dot_tn(mid, hidden_ref[...]).astype(BF)
    rows = outs[0].shape[0]
    for k in range(shards):
        start = pl.multiple_of(jnp.bitwise_xor(me, k) * rows, rows)
        outs[k][...] = whole[pl.ds(start, rows), :]


def rest_grad_kernel(
    shards, info, returned, cotangent, images, arrived, middle_ref, grad_hidden, packed, mixed, small, *refs
):
    pieces = [refs[n * shards : (n + 1) * shards] for n in range(3)]
    outs = refs[3 * shards : 4 * shards]
    grad_in_ref, heads, merge, up, rows_ref, grad_ref, grad_packed, whole_heads, whole_merge, extra, sems = refs[4 * shards :]
    me, leading = info[0], info[1] == 0
    waits = [
        fetch(piece, dest, sems, n * shards, me) for n, (piece, dest) in enumerate(zip(pieces, (heads, merge, up)))
    ]
    count, length, width = images.shape
    incoming = own_gradient(info, returned, cotangent, grad_ref)
    extra[...] = jnp.zeros_like(extra)
    extra[DOWN_BIAS : DOWN_BIAS + 1, :] = column_sum(incoming)
    wide_sum = column_sum(grad_hidden[...].astype(F32))
    for n in range(wide_sum.shape[1] // width):
        extra[8 + n : 9 + n, :] = wide_sum[:, n * width : (n + 1) * width]
    _, unit_two, inverse_two = mid_rows(middle_ref[...], small)
    arrive(waits[2])
    grad_mid = dot_nt(grad_hidden[...], up[...])
    extra[MID_GAIN : MID_GAIN + 1, :] = column_sum(grad_mid * unit_two)
    extra[MID_SHIFT : MID_SHIFT + 1, :] = column_sum(grad_mid)
    grad_middle = incoming + norm_backward(grad_mid, unit_two, inverse_two, small[MID_GAIN : MID_GAIN + 1])
    grad_branch = grad_middle.astype(BF)
    extra[MERGE_BIAS : MERGE_BIAS + 1, :] = column_sum(grad_branch.astype(F32))
    whole_merge[...] = dot_tn(mixed[...], grad_branch).astype(BF)
    arrive(waits[1])
    grad_mixed = dot_nt(grad_branch, merge[...]).astype(BF)
    attention_backward(packed, grad_mixed, grad_packed, count, length, width)
    packed_sum = column_sum(grad_packed[...].astype(F32))
    extra[QUERY_BIAS : QUERY_BIAS + 1, :] = packed_sum[:, :width]
    extra[VALUE_BIAS : VALUE_BIAS + 1, :] = packed_sum[:, 2 * width :]
    source = [jnp.where(leading, image, arrived[n]) for n, image in enumerate(picked_images(info, images))]
    entry, unit_one, inverse_one = entry_rows(pad_images(source, rows_ref), small)
    whole_heads[...] = dot_tn(entry, grad_packed[...]).astype(BF)
    arrive(waits[0])
    grad_entry = dot_nt(grad_packed[...], heads[...])
    extra[PRE_GAIN : PRE_GAIN + 1, :] = column_sum(grad_entry * unit_one)
    extra[PRE_SHIFT : PRE_SHIFT + 1, :] = column_sum(grad_entry)
    grad_in = grad_middle + norm_backward(grad_entry, unit_one, inverse_one, small[PRE_GAIN : PRE_GAIN + 1])
    rounded = grad_in.astype(BF).astype(F32)
    unpad(grad_in_ref, jnp.where(leading, grad_in, rounded), F32)
    rows = pieces[0][0].shape[0]
    wide = whole_heads.shape[1]
    for k in range(shards):
        start = pl.multiple_of(jnp.bitwise_xor(me, k) * rows, rows)
        outs[k][:rows, :wide] = whole_heads[pl.ds(start, rows), :]
        outs[k][:rows, wide:] = whole_merge[pl.ds(start, rows), :]
        outs[k][rows:, :wide] = jnp.zeros((16, wide), BF)
        outs[k][rows:, wide:] = extra[...].astype(BF)


def call(kernel, name, info, blocks, pieces, outs, scratch, flops):
    space = lambda kind, many: [pl.BlockSpec(memory_space=kind)] * many
    nbytes = sum(a.size * a.dtype.itemsize for a in (*blocks, *pieces, *outs))
    return pl.pallas_call(
        kernel,
        out_shape=outs,
        in_specs=space(pltpu.SMEM, 1) + space(pltpu.VMEM, len(blocks)) + space(pl.ANY, len(pieces)),
        out_specs=space(pltpu.VMEM, len(outs)),
        scratch_shapes=scratch,
        compiler_params=pltpu.CompilerParams(vmem_limit_bytes=VMEM_BYTES),
        cost_estimate=pl.CostEstimate(flops=flops, bytes_accessed=nbytes, transcendentals=0),
        name=name,
    )(info, *blocks, *pieces)


def swapped(block, axis, bit):
    return lax.ppermute(block, axis, [(i, i ^ bit) for i in range(lax.axis_size(axis))])


def bits_of(size):
    return [1 << n for n in range(size.bit_length() - 1)]


def gather_pieces(shard, axis):
    pieces = {0: shard}
    for bit in reversed(bits_of(lax.axis_size(axis))):
        pieces.update({k ^ bit: swapped(piece, axis, bit) for k, piece in list(pieces.items())})
    return [pieces[k] for k in range(len(pieces))]


def in_order(pieces, me):
    stacked = jnp.stack(pieces)
    for bit in bits_of(len(pieces)):
        split = stacked.reshape(-1, 2, bit, *stacked.shape[1:])
        stacked = jnp.where((me & bit) != 0, split[:, ::-1], split).reshape(stacked.shape)
    return stacked


def added(*terms):
    return sum(term.astype(F32) for term in terms).astype(BF)


def scatter_pieces(pieces, axis):
    for bit in bits_of(lax.axis_size(axis)):
        kept = [k for k in range(len(pieces)) if pieces[k] is not None and not k & bit]
        for k in sorted(kept, reverse=True):
            pieces[k] = added(pieces[k], swapped(pieces[k ^ bit], axis, bit))
            pieces[k ^ bit] = None
    return pieces[0]


def total_over(shard, axis):
    if lax.axis_size(axis) != 4:
        return lax.psum(shard, axis).astype(F32)
    at = lax.axis_index(axis)
    inward = added(shard, lax.ppermute(shard, axis, [(0, 1), (3, 2)]))
    across = inward.astype(F32) + lax.ppermute(inward, axis, [(1, 2), (2, 1)]).astype(F32)
    across = lax.reduce_precision(across, 8, 7).astype(BF)
    outward = lax.ppermute(across, axis, [(1, 0), (2, 3)])
    return jnp.where((at == 0) | (at == 3), outward, across).astype(F32)


def local(
    images,
    slot_image,
    cotangent,
    pre_gain,
    pre_shift,
    heads_weight,
    query_bias,
    value_bias,
    merge_weight,
    merge_bias,
    mid_gain,
    mid_shift,
    up_weight,
    up_bias,
    down_weight,
    down_bias,
):
    me = lax.axis_index("fsdp").astype(jnp.int32)
    section = lax.axis_index("section").astype(jnp.int32)
    shards = lax.axis_size("fsdp")
    info = jnp.concatenate([jnp.stack([me, section]), slot_image[0]])
    count, length, width = images.shape
    tall = count * padded_length(length)
    part = width // shards
    wide = heads_weight.shape[2]
    hidden_width = up_weight.shape[2]

    vectors = jnp.concatenate(
        [pre_gain, pre_shift, query_bias, value_bias, merge_bias, mid_gain, mid_shift, down_bias, up_bias.reshape(-1, part)]
    )
    vector_pieces = gather_pieces(vectors, "fsdp")
    heads_pieces = gather_pieces(heads_weight[0], "fsdp")
    merge_pieces = gather_pieces(merge_weight[0], "fsdp")
    up_pieces = gather_pieces(up_weight[0], "fsdp")
    down_pieces = gather_pieces(down_weight[0], "fsdp")
    ordered = in_order(vector_pieces, me).astype(F32)
    small = ordered[:, :8].transpose(1, 0, 2).reshape(8, width)
    wide_bias = ordered[:, 8:].reshape(1, hidden_width)

    shape = jax.ShapeDtypeStruct
    scratch_heads = pltpu.VMEM((width, wide), BF)
    scratch_merge = pltpu.VMEM((width, width), BF)
    scratch_up = pltpu.VMEM((width, hidden_width), BF)
    scratch_down = pltpu.VMEM((hidden_width, width), BF)
    scratch_rows = pltpu.VMEM((tall, width), F32)
    scratch_packed = pltpu.VMEM((tall, wide), BF)
    scratch_mixed = pltpu.VMEM((tall, width), BF)
    sems = lambda many: pltpu.SemaphoreType.DMA((many * shards,))
    bind = lambda kernel: functools.partial(kernel, shards)
    work = 2 * tall * width

    middle, mid = call(
        bind(attend_kernel),
        "attend",
        info,
        (images, small),
        (*heads_pieces, *merge_pieces),
        (shape((tall, width), F32), shape((tall, width), BF)),
        [scratch_heads, scratch_merge, scratch_rows, scratch_packed, scratch_mixed, sems(2)],
        work * (wide + width),
    )
    (act,) = call(
        bind(widen_kernel),
        "widen",
        info,
        (mid, wide_bias),
        up_pieces,
        (shape((tall, hidden_width), BF),),
        [scratch_up, sems(1)],
        work * hidden_width,
    )
    (first_out,) = call(
        bind(narrow_kernel),
        "narrow",
        info,
        (act, middle, small),
        down_pieces,
        (shape(images.shape, BF),),
        [scratch_down, sems(1)],
        work * hidden_width,
    )
    arrived = lax.ppermute(first_out, "section", [(0, 1)])

    layer_out, sent, packed, mixed, middle, act = call(
        bind(both_ways_kernel),
        "both_ways",
        info,
        (images, arrived, cotangent, small, wide_bias),
        (*heads_pieces, *merge_pieces, *up_pieces, *down_pieces),
        (
            shape(images.shape, BF),
            shape(images.shape, BF),
            shape((tall, wide), BF),
            shape((tall, width), BF),
            shape((tall, width), F32),
            shape((tall, hidden_width), BF),
        ),
        [scratch_heads, scratch_merge, scratch_up, scratch_down, scratch_rows, scratch_rows, scratch_packed, sems(4)],
        2 * work * (wide + width + 2 * hidden_width),
    )
    returned = lax.ppermute(sent, "section", [(1, 0)])

    down_grads = call(
        bind(down_grad_kernel),
        "down_grad",
        info,
        (returned, cotangent, act),
        (),
        (shape((hidden_width // shards, width), BF),) * shards,
        [scratch_rows],
        work * hidden_width,
    )
    *up_grads, grad_hidden = call(
        bind(up_grad_kernel),
        "up_grad",
        info,
        (returned, cotangent, middle, small, wide_bias),
        (*up_pieces, *down_pieces),
        (shape((part, hidden_width), BF),) * shards + (shape((tall, hidden_width), BF),),
        [scratch_up, scratch_down, scratch_rows, scratch_up, sems(2)],
        3 * work * hidden_width,
    )
    *rest_grads, grad_in = call(
        bind(rest_grad_kernel),
        "rest_grad",
        info,
        (returned, cotangent, images, arrived, middle, grad_hidden, packed, mixed, small),
        (*heads_pieces, *merge_pieces, *up_pieces),
        (shape((part + 16, wide + width), BF),) * shards + (shape(images.shape, F32),),
        [
            scratch_heads,
            scratch_merge,
            scratch_up,
            scratch_rows,
            scratch_rows,
            scratch_packed,
            scratch_heads,
            scratch_merge,
            pltpu.VMEM((16, width), F32),
            sems(3),
        ],
        work * (2 * wide + 2 * width + hidden_width),
    )
    down_total = total_over(scatter_pieces(list(down_grads), "fsdp"), "dp")
    up_total = total_over(scatter_pieces(list(up_grads), "fsdp"), "dp")
    rest_total = total_over(scatter_pieces(list(rest_grads), "fsdp"), "dp")

    heads_total = rest_total[:part, :wide]
    merge_total = rest_total[:part, wide:]
    vector_total = lax.dynamic_slice(rest_total, (part, wide + me * part), (8, part))
    up_bias_total = lax.dynamic_slice(rest_total, (part + 8 + me, wide), (1, width))
    row = lambda n: vector_total[n : n + 1]
    return (
        layer_out[None],
        grad_in[None],
        row(PRE_GAIN),
        row(PRE_SHIFT),
        heads_total[None],
        row(QUERY_BIAS),
        row(VALUE_BIAS),
        merge_total[None],
        row(MERGE_BIAS),
        row(MID_GAIN),
        row(MID_SHIFT),
        up_total[None],
        up_bias_total,
        down_total[None],
        row(DOWN_BIAS),
    )


def solution(mesh):
    vector, matrix = P("section", "fsdp"), P("section", "fsdp", None)
    rows = P("section", ("fsdp", "dp"), None, None)
    weights = (
        vector,
        vector,
        matrix,
        vector,
        vector,
        matrix,
        vector,
        vector,
        vector,
        matrix,
        vector,
        matrix,
        vector,
    )
    blocks = P(("fsdp", "dp"), None, None)
    return jax.shard_map(
        local,
        mesh=mesh,
        in_specs=(blocks, P(("fsdp", "dp"), None), blocks, *weights),
        out_specs=(rows, rows, *weights),
        check_vma=False,
    )
```

```python
import functools

import jax
import jax.numpy as jnp
from jax import lax
from jax.experimental import pallas as pl
from jax.experimental.pallas import tpu as pltpu
from jax.sharding import PartitionSpec as P

HD = 64
PAIR = 2 * HD
EPS = 1e-06
SQRT_HALF = 0.7071067811865476
INV_ROOT_TAU = 0.3989422804014327
BF = jnp.bfloat16
F32 = jnp.float32
VMEM_BYTES = 20 * 1024 * 1024

PRE_GAIN, PRE_SHIFT, QUERY_BIAS, VALUE_BIAS, MERGE_BIAS, MID_GAIN, MID_SHIFT, DOWN_BIAS = range(8)


def padded_length(length):
    return -(-length // 16) * 16


def dot(a, b):
    return jnp.dot(a, b, preferred_element_type=F32)


def dot_nt(a, b):
    return lax.dot_general(a, b, (((1,), (1,)), ((), ())), preferred_element_type=F32)


def dot_tn(a, b):
    return lax.dot_general(a, b, (((0,), (0,)), ((), ())), preferred_element_type=F32)


def fetch(pieces, dest, sems, first, me, rows=None, column=0):
    copies = []
    for k, piece in enumerate(pieces):
        if rows is not None:
            piece = piece.at[pl.ds(0, rows), pl.ds(column, dest.shape[1])]
        count = piece.shape[0]
        start = pl.multiple_of(jnp.bitwise_xor(me, k) * count, count)
        copies.append(pltpu.make_async_copy(piece, dest.at[pl.ds(start, count)], sems.at[first + k]))
    for copy in copies:
        copy.start()
    return copies


def arrive(copies):
    for copy in copies:
        copy.wait()


def pad_images(images, scratch):
    length = images[0].shape[0]
    step = padded_length(length)
    scratch[...] = jnp.zeros_like(scratch)
    for n, image in enumerate(images):
        scratch[n * step : n * step + length, :] = image.astype(F32)
    return scratch[...]


def unpad(ref, rows, kind):
    count, length, _ = ref.shape
    step = padded_length(length)
    for n in range(count):
        ref[n] = rows[n * step : n * step + length, :].astype(kind)


def norm_parts(rows):
    mean = jnp.mean(rows, axis=-1, keepdims=True)
    centered = rows - mean
    inverse = lax.rsqrt(jnp.mean(centered * centered, axis=-1, keepdims=True) + EPS)
    return centered * inverse, inverse


def norm_backward(grad_rows, normed, inverse, gain):
    scaled = grad_rows * gain
    mean_one = jnp.mean(scaled, axis=-1, keepdims=True)
    mean_two = jnp.mean(scaled * normed, axis=-1, keepdims=True)
    return inverse * (scaled - mean_one - normed * mean_two)


def column_sum(rows):
    return jnp.sum(rows, axis=0, keepdims=True)


def half_masks():
    lane = lax.broadcasted_iota(jnp.int32, (1, PAIR), 1)
    low = (lane < HD).astype(F32)
    return low.astype(BF), (1.0 - low).astype(BF)


def both_heads(rows):
    low, high = half_masks()
    return jnp.concatenate([rows * low, rows * high], axis=0)


def beside(stacked):
    half = stacked.shape[0] // 2
    lane = lax.broadcasted_iota(jnp.int32, (half, PAIR), 1)
    return jnp.where(lane < HD, stacked[:half], stacked[half:])


def qkv(packed, n, pair, step, width):
    rows = slice(n * step, (n + 1) * step)
    return tuple(packed[rows, part * width + pair * PAIR : part * width + (pair + 1) * PAIR] for part in range(3))


def head_pairs(packed, count, length, width):
    step = padded_length(length)
    parts = [qkv(packed, n, pair, step, width) for n in range(count) for pair in range(width // PAIR)]
    return [both_heads(queries) for queries, _, _ in parts], [keys for _, keys, _ in parts], [v for _, _, v in parts]


def block(rows, n, total):
    high = rows.shape[0] // total
    return rows[n * high : (n + 1) * high]


def attention_forward(packed, mixed, count, length, width):
    step = padded_length(length)
    queries, keys, values = head_pairs(packed, count, length, width)
    scores = jnp.concatenate([dot_nt(q, k) for q, k in zip(queries, keys)], axis=0) * HD**-0.5
    lane = lax.broadcasted_iota(jnp.int32, scores.shape, 1)
    scores = jnp.where(lane < length, scores, -1e30)
    grown = jnp.exp(scores - jnp.max(scores, axis=-1, keepdims=True))
    probs = grown * (1.0 / jnp.sum(grown, axis=-1, keepdims=True))
    rounded = probs.astype(BF)
    outs = [beside(dot(block(rounded, at, len(values)), v)).astype(BF) for at, v in enumerate(values)]
    for at, out in enumerate(outs):
        n, pair = divmod(at, width // PAIR)
        mixed[n * step : (n + 1) * step, pair * PAIR : (pair + 1) * PAIR] = out
    return probs


def attention_backward(packed, probs, grad_mixed, grad_packed, count, length, width):
    step = padded_length(length)
    queries, keys, values = head_pairs(packed, count, length, width)
    pairs = width // PAIR
    incoming = [
        both_heads(grad_mixed[n * step : (n + 1) * step, pair * PAIR : (pair + 1) * PAIR])
        for n in range(count)
        for pair in range(pairs)
    ]
    grad_probs = jnp.concatenate([dot_nt(g, v) for g, v in zip(incoming, values)], axis=0)
    inner = jnp.sum(probs * grad_probs, axis=-1, keepdims=True)
    grad_scores = (probs * (grad_probs - inner)).astype(BF)
    rounded = probs.astype(BF)
    total = len(keys)
    parts = [
        (
            beside(dot(block(grad_scores, at, total), keys[at])) * HD**-0.5,
            dot_tn(block(grad_scores, at, total), queries[at]) * HD**-0.5,
            dot_tn(block(rounded, at, total), incoming[at]),
        )
        for at in range(total)
    ]
    for at, three in enumerate(parts):
        n, pair = divmod(at, pairs)
        for part, value in enumerate(three):
            column = part * width + pair * PAIR
            grad_packed[n * step : (n + 1) * step, column : column + PAIR] = value.astype(BF)


def entry_rows(rows, small):
    normed, inverse = norm_parts(rows)
    return (normed * small[PRE_GAIN : PRE_GAIN + 1] + small[PRE_SHIFT : PRE_SHIFT + 1]).astype(BF), normed, inverse


def mid_rows(middle, small):
    normed, inverse = norm_parts(middle)
    return (normed * small[MID_GAIN : MID_GAIN + 1] + small[MID_SHIFT : MID_SHIFT + 1]).astype(BF), normed, inverse


def packed_bias(small):
    query = small[QUERY_BIAS : QUERY_BIAS + 1]
    return jnp.concatenate([query, jnp.zeros_like(query), small[VALUE_BIAS : VALUE_BIAS + 1]], axis=1)


def gelu_parts(hidden):
    bell = 0.5 * (1.0 + lax.erf(hidden * SQRT_HALF))
    return hidden * bell, bell


def gelu_slope(hidden, bell):
    return bell + hidden * jnp.exp(-0.5 * hidden * hidden) * INV_ROOT_TAU


def picked_images(info, images):
    return [
        jnp.where(info[2 + n] == 0, images[0], images[1]) for n in range(images.shape[0])
    ]


def pack_kernel(heads_ref, merge_ref, *refs):
    many = (len(refs) - 3) // 2
    vectors, (out_ref, rows, *held), sems = refs[:many], refs[many : 2 * many + 2], refs[-1]
    part, wide = heads_ref.shape
    copies = [
        pltpu.make_async_copy(heads_ref, out_ref.at[pl.ds(0, part), pl.ds(0, wide)], sems.at[0]),
        pltpu.make_async_copy(merge_ref, out_ref.at[pl.ds(0, part), pl.ds(wide, merge_ref.shape[1])], sems.at[1]),
    ]
    copies += [pltpu.make_async_copy(v, held[n], sems.at[2 + n]) for n, v in enumerate(vectors)]
    for copy in copies:
        copy.start()
    rows[...] = jnp.zeros_like(rows)
    arrive(copies[2:])
    for n, vector in enumerate(held):
        rows[n : n + 1, : vector.shape[1]] = vector[...].astype(F32)
    out_ref[part:, :] = rows[...].astype(BF)
    arrive(copies[:2])


def attend_kernel(shards, info, images, *refs):
    pieces = refs[:shards]
    middle_ref, mid_ref, heads, merge, small, up_bias, rows_ref, packed, mixed, vectors, sems = refs[shards:]
    me = info[0]
    count, length, width = images.shape
    part = width // shards
    first = fetch(pieces, heads, sems, 0, me, part)
    second = fetch(pieces, merge, sems, shards, me, part, heads.shape[1])
    third = []
    for k, piece in enumerate(pieces):
        source = piece.at[pl.ds(part, 16)]
        third.append(pltpu.make_async_copy(source, vectors.at[jnp.bitwise_xor(me, k)], sems.at[2 * shards + k]))
        third[-1].start()
    rows = pad_images(picked_images(info, images), rows_ref)
    unit, _ = norm_parts(rows)
    arrive(third)
    hidden_part = up_bias.shape[1] // shards
    for at in range(shards):
        given = vectors[at].astype(F32)
        small[:, at * part : (at + 1) * part] = given[:8, :part]
        up_bias[:, at * hidden_part : (at + 1) * hidden_part] = given[8:9, :hidden_part]
    entry = (unit * small[PRE_GAIN : PRE_GAIN + 1] + small[PRE_SHIFT : PRE_SHIFT + 1]).astype(BF)
    arrive(first)
    packed[...] = (dot(entry, heads[...]) + packed_bias(small)).astype(BF)
    attention_forward(packed, mixed, count, length, width)
    arrive(second)
    middle = rows + dot(mixed[...], merge[...]) + small[MERGE_BIAS : MERGE_BIAS + 1]
    middle_ref[...] = middle
    mid_ref[...] = mid_rows(middle, small)[0]


def widen_kernel(shards, info, mid_ref, up_bias, *refs):
    act_ref, up, sems = refs[shards:]
    arrive(fetch(refs[:shards], up, sems, 0, info[0]))
    hidden = dot(mid_ref[...], up[...]) + up_bias[...]
    act_ref[...] = gelu_parts(hidden)[0].astype(BF)


def narrow_kernel(shards, info, act_ref, middle_ref, small, *refs):
    out_ref, down, sems = refs[shards:]
    arrive(fetch(refs[:shards], down, sems, 0, info[0]))
    out = middle_ref[...] + dot(act_ref[...], down[...]) + small[DOWN_BIAS : DOWN_BIAS + 1]
    unpad(out_ref, out, BF)


def both_ways_kernel(
    info,
    images,
    arrived,
    cotangent,
    small,
    up_bias,
    heads,
    merge,
    up,
    down,
    out_ref,
    sent_ref,
    packed,
    probs_ref,
    mixed,
    act_ref,
    slope_ref,
    entry_ref,
    unit_one_ref,
    inverse_one_ref,
    mid_ref,
    unit_two_ref,
    inverse_two_ref,
    rows_ref,
    grad_ref,
    grad_packed,
):
    leading = info[1] == 0
    count, length, width = images.shape
    source = [jnp.where(leading, image, arrived[n]) for n, image in enumerate(picked_images(info, images))]
    rows = pad_images(source, rows_ref)
    entry_ref[...], unit_one_ref[...], inverse_one_ref[...] = entry_rows(rows, small)
    packed[...] = (dot(entry_ref[...], heads[...]) + packed_bias(small)).astype(BF)
    probs_ref[...] = attention_forward(packed, mixed, count, length, width)
    middle = rows + dot(mixed[...], merge[...]) + small[MERGE_BIAS : MERGE_BIAS + 1]
    mid_ref[...], unit_two_ref[...], inverse_two_ref[...] = mid_rows(middle, small)
    hidden = dot(mid_ref[...], up[...]) + up_bias[...]
    act, bell = gelu_parts(hidden)
    slope_ref[...] = gelu_slope(hidden, bell)
    act_ref[...] = act.astype(BF)
    out = middle + dot(act_ref[...], down[...]) + small[DOWN_BIAS : DOWN_BIAS + 1]
    unpad(out_ref, out, BF)
    incoming = pad_images([cotangent[n] for n in range(count)], grad_ref)
    grad_hidden = (dot_nt(incoming.astype(BF), down[...]) * slope_ref[...]).astype(BF)
    grad_mid = dot_nt(grad_hidden, up[...])
    grad_middle = incoming + norm_backward(
        grad_mid, unit_two_ref[...], inverse_two_ref[...], small[MID_GAIN : MID_GAIN + 1]
    )
    grad_mixed = dot_nt(grad_middle.astype(BF), merge[...]).astype(BF)
    attention_backward(packed, probs_ref[...], grad_mixed, grad_packed, count, length, width)
    grad_entry = dot_nt(grad_packed[...], heads[...])
    grad_in = grad_middle + norm_backward(
        grad_entry, unit_one_ref[...], inverse_one_ref[...], small[PRE_GAIN : PRE_GAIN + 1]
    )
    unpad(sent_ref, grad_in, BF)


def own_gradient(info, returned, cotangent, scratch):
    leading = info[1] == 0
    return pad_images(
        [jnp.where(leading, returned[n], cotangent[n]) for n in range(cotangent.shape[0])], scratch
    )


def down_grad_kernel(shards, info, returned, cotangent, act_ref, *refs):
    outs, grad_ref = refs[:shards], refs[shards]
    incoming = own_gradient(info, returned, cotangent, grad_ref).astype(BF)
    rows = outs[0].shape[0]
    for k in range(shards):
        start = pl.multiple_of(jnp.bitwise_xor(info[0], k) * rows, rows)
        outs[k][...] = dot_tn(act_ref[:, pl.ds(start, rows)], incoming).astype(BF)


def rest_grad_kernel(
    shards,
    info,
    returned,
    cotangent,
    small,
    heads,
    merge,
    up,
    down,
    packed,
    probs_ref,
    mixed,
    slope_ref,
    entry_ref,
    unit_one_ref,
    inverse_one_ref,
    mid_ref,
    unit_two_ref,
    inverse_two_ref,
    *refs,
):
    up_outs, rest_outs = refs[:shards], refs[shards : 2 * shards]
    grad_in_ref, grad_ref, grad_packed, whole_up, whole_heads, whole_merge, extra = refs[2 * shards :]
    me, leading = info[0], info[1] == 0
    count, length, width = cotangent.shape
    part = width // shards
    incoming = own_gradient(info, returned, cotangent, grad_ref)
    extra[...] = jnp.zeros_like(extra)
    extra[DOWN_BIAS : DOWN_BIAS + 1, :] = column_sum(incoming)
    grad_hidden = (dot_nt(incoming.astype(BF), down[...]) * slope_ref[...]).astype(BF)
    whole_up[...] = dot_tn(mid_ref[...], grad_hidden).astype(BF)
    wide_sum = column_sum(grad_hidden.astype(F32))
    for n in range(wide_sum.shape[1] // width):
        extra[8 + n : 9 + n, :] = wide_sum[:, n * width : (n + 1) * width]
    grad_mid = dot_nt(grad_hidden, up[...])
    extra[MID_GAIN : MID_GAIN + 1, :] = column_sum(grad_mid * unit_two_ref[...])
    extra[MID_SHIFT : MID_SHIFT + 1, :] = column_sum(grad_mid)
    grad_middle = incoming + norm_backward(
        grad_mid, unit_two_ref[...], inverse_two_ref[...], small[MID_GAIN : MID_GAIN + 1]
    )
    grad_branch = grad_middle.astype(BF)
    extra[MERGE_BIAS : MERGE_BIAS + 1, :] = column_sum(grad_branch.astype(F32))
    whole_merge[...] = dot_tn(mixed[...], grad_branch).astype(BF)
    grad_mixed = dot_nt(grad_branch, merge[...]).astype(BF)
    attention_backward(packed, probs_ref[...], grad_mixed, grad_packed, count, length, width)
    packed_sum = column_sum(grad_packed[...].astype(F32))
    extra[QUERY_BIAS : QUERY_BIAS + 1, :] = packed_sum[:, :width]
    extra[VALUE_BIAS : VALUE_BIAS + 1, :] = packed_sum[:, 2 * width :]
    whole_heads[...] = dot_tn(entry_ref[...], grad_packed[...]).astype(BF)
    grad_entry = dot_nt(grad_packed[...], heads[...])
    extra[PRE_GAIN : PRE_GAIN + 1, :] = column_sum(grad_entry * unit_one_ref[...])
    extra[PRE_SHIFT : PRE_SHIFT + 1, :] = column_sum(grad_entry)
    grad_in = grad_middle + norm_backward(
        grad_entry, unit_one_ref[...], inverse_one_ref[...], small[PRE_GAIN : PRE_GAIN + 1]
    )
    rounded = grad_in.astype(BF).astype(F32)
    unpad(grad_in_ref, jnp.where(leading, grad_in, rounded), F32)
    wide = whole_heads.shape[1]
    for k in range(shards):
        rows = pl.ds(pl.multiple_of(jnp.bitwise_xor(me, k) * part, part), part)
        up_outs[k][...] = whole_up[rows, :]
        rest_outs[k][:part, :wide] = whole_heads[rows, :]
        rest_outs[k][:part, wide:] = whole_merge[rows, :]
        rest_outs[k][part:, :wide] = jnp.zeros((16, wide), BF)
        rest_outs[k][part:, wide:] = extra[...].astype(BF)


def column_blocks_kernel(at, *refs):
    outs = [ref for ref in refs if ref.shape != refs[0].shape]
    wide = outs[0].shape[1]
    for k, out in enumerate(outs):
        columns = pl.ds(pl.multiple_of(jnp.bitwise_xor(at[0], k) * wide, wide), wide)
        out[...] = sum(ref[:, columns].astype(F32) for ref in refs[: len(refs) - len(outs)]).astype(BF)


def call(kernel, name, info, blocks, pieces, outs, scratch, flops, earlier=(), room=VMEM_BYTES):
    space = lambda kind, many: [pl.BlockSpec(memory_space=kind)] * many
    nbytes = sum(a.size * a.dtype.itemsize for a in (*blocks, *pieces, *outs))
    scalars = () if info is None else (info,)
    used = len(scalars) + len(blocks) + len(pieces)
    return pl.pallas_call(
        lambda *refs: kernel(*refs[:used], *refs[used + len(earlier) :]),
        out_shape=outs,
        in_specs=space(pltpu.SMEM, len(scalars)) + space(pltpu.VMEM, len(blocks)) + space(pl.ANY, len(pieces) + len(earlier)),
        out_specs=space(pltpu.VMEM, len(outs)),
        scratch_shapes=scratch,
        compiler_params=pltpu.CompilerParams(vmem_limit_bytes=room),
        cost_estimate=pl.CostEstimate(flops=flops, bytes_accessed=nbytes, transcendentals=0),
        name=name,
    )(*scalars, *blocks, *pieces, *earlier)


def after(value, *others):
    return lax.optimization_barrier((value, *others))[0]


def swapped(block, axis, bit):
    return lax.ppermute(block, axis, [(i, i ^ bit) for i in range(lax.axis_size(axis))])


def bits_of(size):
    return [1 << n for n in range(size.bit_length() - 1)]


def gather_pieces(shard, axis, *earlier):
    pieces = {0: shard}
    for bit in reversed(bits_of(lax.axis_size(axis))):
        pieces.update({k ^ bit: swapped(piece if k == 0 else after(piece, *earlier), axis, bit) for k, piece in list(pieces.items())})
    return [pieces[k] for k in range(len(pieces))]


def added(*terms):
    return sum(term.astype(F32) for term in terms).astype(BF)


def scatter_steps(pieces, axis):
    pieces = dict(enumerate(pieces))
    *nearer, last = bits_of(lax.axis_size(axis))
    for bit in nearer:
        for k in sorted((k for k in pieces if not k & bit), reverse=True):
            received = swapped(pieces.pop(k ^ bit), axis, bit)
            pieces[k] = added(pieces[k], received) if k & last else (pieces[k], received)
    yield pieces[last]
    kept = pieces[0] if isinstance(pieces[0], tuple) else (pieces[0],)
    yield (*kept, swapped(pieces[last], axis, last))


def together(*values):
    return lax.optimization_barrier(values)


def rounded(*terms):
    return lax.reduce_precision(sum(term.astype(F32) for term in terms), 8, 7).astype(BF)


def chosen(at, options):
    while len(options) > 1:
        options = [jnp.where((at & 1) != 0, odd, even) for even, odd in zip(options[::2], options[1::2])]
        at = at >> 1
    return options[0]


def column_blocks(at, terms, count):
    high, wide = terms[0].shape
    shapes = (jax.ShapeDtypeStruct((high, wide // count), BF),) * count
    return call(column_blocks_kernel, "column_blocks", at.reshape(1), terms, (), shapes, [], 1)


def totals_over_line(down_sum, up_steps, rest_steps, axis):
    at = lax.axis_index(axis).astype(jnp.int32)
    size = lax.axis_size(axis)
    inwards = lambda block: lax.ppermute(block, axis, [(0, 1), (3, 2)])
    across = lambda block: lax.ppermute(block, axis, [(1, 2), (2, 1)])
    outwards = lambda block: lax.ppermute(block, axis, [(1, 0), (2, 3)])
    finished = lambda kept, received: jnp.where((at == 0) | (at == 3), received, kept).astype(F32)
    others = lambda blocks: [swapped(blocks[k], axis, k) for k in range(1, size)]

    rest_first = next(rest_steps)
    *up_terms, up_last = next(up_steps)
    up_last, down_in, rest_first = together(up_last, inwards(down_sum), rest_first)
    up_sum, down_half = added(*up_terms, up_last), added(down_sum, down_in)

    *rest_terms, rest_last = next(rest_steps)
    rest_last, down_across, up_in = together(rest_last, across(down_half), inwards(up_sum))
    blocks = column_blocks(at, (*rest_terms, rest_last), size)
    down_full, up_half = rounded(down_half, down_across), added(up_sum, up_in)

    down_out, up_across, *received = together(outwards(down_full), across(up_half), *others(blocks))
    own, up_full = rounded(blocks[0], *received), rounded(up_half, up_across)

    full = [own, *others([own] * size)]
    rest_total = [chosen(at, [full[n ^ k] for k in range(size)]).astype(F32) for n in range(size)]
    return (
        finished(down_full, down_out),
        finished(up_full, outwards(up_full)),
        rest_total,
        up_sum,
    )


def totals_over(down_sum, up_steps, rest_steps, axis):
    if lax.axis_size(axis) == 4:
        return totals_over_line(down_sum, up_steps, rest_steps, axis)
    next(rest_steps)
    up_sum, rest_sum = added(*next(up_steps)), added(*next(rest_steps))
    down, up, rest = (total.astype(F32) for total in lax.psum((down_sum, up_sum, rest_sum), axis))
    return down, up, jnp.split(rest, 4, axis=1), up_sum


def local(
    images,
    slot_image,
    cotangent,
    pre_gain,
    pre_shift,
    heads_weight,
    query_bias,
    value_bias,
    merge_weight,
    merge_bias,
    mid_gain,
    mid_shift,
    up_weight,
    up_bias,
    down_weight,
    down_bias,
):
    me = lax.axis_index("fsdp").astype(jnp.int32)
    section = lax.axis_index("section").astype(jnp.int32)
    shards = lax.axis_size("fsdp")
    info = jnp.concatenate([jnp.stack([me, section]), slot_image[0]])
    count, length, width = images.shape
    tall = count * padded_length(length)
    part = width // shards
    wide = heads_weight.shape[2]
    hidden_width = up_weight.shape[2]

    shape = jax.ShapeDtypeStruct
    scratch_rows = pltpu.VMEM((tall, width), F32)
    scratch_packed = pltpu.VMEM((tall, wide), BF)
    scratch_mixed = pltpu.VMEM((tall, width), BF)
    sems = lambda many: pltpu.SemaphoreType.DMA((many * shards,))
    bind = lambda kernel: functools.partial(kernel, shards)
    work = 2 * tall * width
    full_heads, full_merge = shape((width, wide), BF), shape((width, width), BF)
    full_up, full_down = shape((width, hidden_width), BF), shape((hidden_width, width), BF)
    rows_wide, rows_bf, column = shape((tall, width), F32), shape((tall, width), BF), shape((tall, 1), F32)

    (mix,) = call(
        pack_kernel,
        "pack",
        None,
        (),
        (
            heads_weight[0],
            merge_weight[0],
            pre_gain,
            pre_shift,
            query_bias,
            value_bias,
            merge_bias,
            mid_gain,
            mid_shift,
            down_bias,
            up_bias,
        ),
        (shape((part + 16, wide + width), BF),),
        [pltpu.VMEM((16, wide + width), F32)]
        + [pltpu.VMEM((1, part), BF)] * 8
        + [pltpu.VMEM(up_bias.shape, BF), pltpu.SemaphoreType.DMA((11,))],
        1,
        room=56 * 1024 * 1024,
    )
    up_pieces = gather_pieces(up_weight[0], "fsdp")
    mix_pieces = gather_pieces(mix, "fsdp", up_pieces[shards // 2])

    middle, mid, heads, merge, small, wide_bias = call(
        bind(attend_kernel),
        "attend",
        info,
        (images,),
        mix_pieces,
        (rows_wide, rows_bf, full_heads, full_merge, shape((8, width), F32), shape((1, hidden_width), F32)),
        [
            scratch_rows,
            scratch_packed,
            scratch_mixed,
            pltpu.VMEM((shards, 16, wide + width), BF),
            sems(3),
        ],
        work * (wide + width),
    )
    down_pieces = gather_pieces(down_weight[0], "fsdp", mid)
    act, up = call(
        bind(widen_kernel),
        "widen",
        info,
        (mid, wide_bias),
        up_pieces,
        (shape((tall, hidden_width), BF), full_up),
        [sems(1)],
        work * hidden_width,
        (down_pieces[shards // 2],),
    )
    first_out, down = call(
        bind(narrow_kernel),
        "narrow",
        info,
        (act, middle, small),
        down_pieces,
        (shape(images.shape, BF), full_down),
        [sems(1)],
        work * hidden_width,
    )
    arrived = lax.ppermute(first_out, "section", [(0, 1)])

    layer_out, sent, packed, probs, mixed, act, slope, *kept = call(
        both_ways_kernel,
        "both_ways",
        info,
        (images, arrived, cotangent, small, wide_bias, heads, merge, up, down),
        (),
        (
            shape(images.shape, BF),
            shape(images.shape, BF),
            shape((tall, wide), BF),
            shape((2 * tall * (width // PAIR), tall // count), F32),
            rows_bf,
            shape((tall, hidden_width), BF),
            shape((tall, hidden_width), F32),
            rows_bf,
            rows_wide,
            column,
            rows_bf,
            rows_wide,
            column,
        ),
        [scratch_rows, scratch_rows, scratch_packed],
        2 * work * (wide + width + 2 * hidden_width),
    )
    returned = lax.ppermute(sent, "section", [(1, 0)])

    down_grads = call(
        bind(down_grad_kernel),
        "down_grad",
        info,
        (returned, cotangent, act),
        (),
        (shape((hidden_width // shards, width), BF),) * shards,
        [scratch_rows],
        work * hidden_width,
    )
    down_chain = scatter_steps(down_grads, "fsdp")
    down_first = next(down_chain)
    *grads, grad_in = call(
        bind(rest_grad_kernel),
        "rest_grad",
        info,
        (returned, cotangent, small, heads, merge, up, down, packed, probs, mixed, slope, *kept),
        (),
        (shape((part, hidden_width), BF),) * shards
        + (shape((part + 16, wide + width), BF),) * shards
        + (shape(images.shape, F32),),
        [
            scratch_rows,
            scratch_packed,
            pltpu.VMEM((width, hidden_width), BF),
            pltpu.VMEM((width, wide), BF),
            pltpu.VMEM((width, width), BF),
            pltpu.VMEM((16, width), F32),
        ],
        2 * work * (wide + width + 2 * hidden_width),
        (down_first,),
    )
    down_sum = added(*next(down_chain))
    up_chain = scatter_steps([after(one, down_sum) for one in grads[:shards]], "fsdp")
    up_first = next(up_chain)
    rest_chain = scatter_steps([after(one, down_sum, up_first) for one in grads[shards:]], "fsdp")
    down_total, up_total, rest_total, up_sum = totals_over(down_sum, up_chain, rest_chain, "dp")
    layer_out, grad_in = after(layer_out, up_sum), after(grad_in, up_sum)

    heads_total = jnp.concatenate([block[:part] for block in rest_total[:3]], axis=1)
    merge_total = rest_total[3][:part]
    vector_total = lax.dynamic_slice(rest_total[3], (part, me * part), (8, part))
    up_bias_total = lax.dynamic_slice(rest_total[3], (part + 8 + me, 0), (1, width))
    row = lambda n: vector_total[n : n + 1]
    return (
        layer_out[None],
        grad_in[None],
        row(PRE_GAIN),
        row(PRE_SHIFT),
        heads_total[None],
        row(QUERY_BIAS),
        row(VALUE_BIAS),
        merge_total[None],
        row(MERGE_BIAS),
        row(MID_GAIN),
        row(MID_SHIFT),
        up_total[None],
        up_bias_total,
        down_total[None],
        row(DOWN_BIAS),
    )


def solution(mesh):
    vector, matrix = P("section", "fsdp"), P("section", "fsdp", None)
    rows = P("section", ("fsdp", "dp"), None, None)
    weights = (
        vector,
        vector,
        matrix,
        vector,
        vector,
        matrix,
        vector,
        vector,
        vector,
        matrix,
        vector,
        matrix,
        vector,
    )
    blocks = P(("fsdp", "dp"), None, None)
    return jax.shard_map(
        local,
        mesh=mesh,
        in_specs=(blocks, P(("fsdp", "dp"), None), blocks, *weights),
        out_specs=(rows, rows, *weights),
        check_vma=False,
    )
```

```python
import functools

import jax
import jax.numpy as jnp
from jax import lax
from jax.experimental import pallas as pl
from jax.experimental.pallas import tpu as pltpu
from jax.sharding import PartitionSpec as P

HD = 64
PAIR = 2 * HD
EPS = 1e-06
SQRT_HALF = 0.7071067811865476
INV_ROOT_TAU = 0.3989422804014327
BF = jnp.bfloat16
F32 = jnp.float32
VMEM_BYTES = 20 * 1024 * 1024

PRE_GAIN, PRE_SHIFT, QUERY_BIAS, VALUE_BIAS, MERGE_BIAS, MID_GAIN, MID_SHIFT, DOWN_BIAS = range(8)


def padded_length(length):
    return -(-length // 16) * 16


def dot(a, b):
    return jnp.dot(a, b, preferred_element_type=F32)


def dot_nt(a, b):
    return lax.dot_general(a, b, (((1,), (1,)), ((), ())), preferred_element_type=F32)


def dot_tn(a, b):
    return lax.dot_general(a, b, (((0,), (0,)), ((), ())), preferred_element_type=F32)


def fetch(pieces, dest, sems, first, me, rows=None, column=0, half=0):
    copies = []
    for k, piece in enumerate(pieces):
        if rows is not None:
            piece = piece.at[pl.ds(0, rows), pl.ds(column, dest.shape[1])]
        blocks = piece if isinstance(piece, tuple) else (piece,)
        count, wide = blocks[0].shape
        start = pl.multiple_of(jnp.bitwise_xor(me, k) * count, count)
        for n, one in enumerate(blocks):
            target = dest.at[pl.ds(start, count)]
            if len(blocks) > 1:
                target = dest.at[pl.ds(start, count), pl.ds(pl.multiple_of(jnp.bitwise_xor(half, n) * wide, wide), wide)]
            copies.append(pltpu.make_async_copy(one, target, sems.at[first + len(copies)]))
    for copy in copies:
        copy.start()
    return copies


def arrive(copies):
    for copy in copies:
        copy.wait()


def pad_images(images, scratch):
    length = images[0].shape[0]
    step = padded_length(length)
    scratch[...] = jnp.zeros_like(scratch)
    for n, image in enumerate(images):
        scratch[n * step : n * step + length, :] = image.astype(F32)
    return scratch[...]


def unpad(ref, rows, kind):
    count, length, _ = ref.shape
    step = padded_length(length)
    for n in range(count):
        ref[n] = rows[n * step : n * step + length, :].astype(kind)


def norm_parts(rows):
    mean = jnp.mean(rows, axis=-1, keepdims=True)
    centered = rows - mean
    inverse = lax.rsqrt(jnp.mean(centered * centered, axis=-1, keepdims=True) + EPS)
    return centered * inverse, inverse


def norm_backward(grad_rows, normed, inverse, gain):
    scaled = grad_rows * gain
    mean_one = jnp.mean(scaled, axis=-1, keepdims=True)
    mean_two = jnp.mean(scaled * normed, axis=-1, keepdims=True)
    return inverse * (scaled - mean_one - normed * mean_two)


def column_sum(rows):
    return jnp.sum(rows, axis=0, keepdims=True)


def half_masks():
    lane = lax.broadcasted_iota(jnp.int32, (1, PAIR), 1)
    low = (lane < HD).astype(F32)
    return low.astype(BF), (1.0 - low).astype(BF)


def both_heads(rows):
    low, high = half_masks()
    return jnp.concatenate([rows * low, rows * high], axis=0)


def beside(stacked):
    half = stacked.shape[0] // 2
    lane = lax.broadcasted_iota(jnp.int32, (half, PAIR), 1)
    return jnp.where(lane < HD, stacked[:half], stacked[half:])


def qkv(packed, n, pair, step, width):
    rows = slice(n * step, (n + 1) * step)
    return tuple(packed[rows, part * width + pair * PAIR : part * width + (pair + 1) * PAIR] for part in range(3))


def head_pairs(packed, count, length, width):
    step = padded_length(length)
    parts = [qkv(packed, n, pair, step, width) for n in range(count) for pair in range(width // PAIR)]
    return [both_heads(queries) for queries, _, _ in parts], [keys for _, keys, _ in parts], [v for _, _, v in parts]


def block(rows, n, total):
    high = rows.shape[0] // total
    return rows[n * high : (n + 1) * high]


def attention_forward(packed, mixed, count, length, width):
    step = padded_length(length)
    queries, keys, values = head_pairs(packed, count, length, width)
    scores = jnp.concatenate([dot_nt(q, k) for q, k in zip(queries, keys)], axis=0) * HD**-0.5
    lane = lax.broadcasted_iota(jnp.int32, scores.shape, 1)
    scores = jnp.where(lane < length, scores, -1e30)
    grown = jnp.exp(scores - jnp.max(scores, axis=-1, keepdims=True))
    probs = grown * (1.0 / jnp.sum(grown, axis=-1, keepdims=True))
    rounded = probs.astype(BF)
    outs = [beside(dot(block(rounded, at, len(values)), v)).astype(BF) for at, v in enumerate(values)]
    for at, out in enumerate(outs):
        n, pair = divmod(at, width // PAIR)
        mixed[n * step : (n + 1) * step, pair * PAIR : (pair + 1) * PAIR] = out
    return probs


def attention_backward(packed, probs, grad_mixed, grad_packed, count, length, width):
    step = padded_length(length)
    queries, keys, values = head_pairs(packed, count, length, width)
    pairs = width // PAIR
    incoming = [
        both_heads(grad_mixed[n * step : (n + 1) * step, pair * PAIR : (pair + 1) * PAIR])
        for n in range(count)
        for pair in range(pairs)
    ]
    grad_probs = jnp.concatenate([dot_nt(g, v) for g, v in zip(incoming, values)], axis=0)
    inner = jnp.sum(probs * grad_probs, axis=-1, keepdims=True)
    grad_scores = (probs * (grad_probs - inner)).astype(BF)
    rounded = probs.astype(BF)
    total = len(keys)
    parts = [
        (
            beside(dot(block(grad_scores, at, total), keys[at])) * HD**-0.5,
            dot_tn(block(grad_scores, at, total), queries[at]) * HD**-0.5,
            dot_tn(block(rounded, at, total), incoming[at]),
        )
        for at in range(total)
    ]
    for at, three in enumerate(parts):
        n, pair = divmod(at, pairs)
        for part, value in enumerate(three):
            column = part * width + pair * PAIR
            grad_packed[n * step : (n + 1) * step, column : column + PAIR] = value.astype(BF)


def entry_rows(rows, small):
    normed, inverse = norm_parts(rows)
    return (normed * small[PRE_GAIN : PRE_GAIN + 1] + small[PRE_SHIFT : PRE_SHIFT + 1]).astype(BF), normed, inverse


def mid_rows(middle, small):
    normed, inverse = norm_parts(middle)
    return (normed * small[MID_GAIN : MID_GAIN + 1] + small[MID_SHIFT : MID_SHIFT + 1]).astype(BF), normed, inverse


def packed_bias(small):
    query = small[QUERY_BIAS : QUERY_BIAS + 1]
    return jnp.concatenate([query, jnp.zeros_like(query), small[VALUE_BIAS : VALUE_BIAS + 1]], axis=1)


def gelu_parts(hidden):
    bell = 0.5 * (1.0 + lax.erf(hidden * SQRT_HALF))
    return hidden * bell, bell


def gelu_slope(hidden, bell):
    return bell + hidden * jnp.exp(-0.5 * hidden * hidden) * INV_ROOT_TAU


def picked_images(info, images):
    return [
        jnp.where(info[2 + n] == 0, images[0], images[1]) for n in range(images.shape[0])
    ]


def pack_kernel(info, heads_ref, merge_ref, up_ref, *refs):
    many = (len(refs) - 4) // 2
    vectors, (out_ref, half_ref, rows, *held), sems = refs[:many], refs[many : 2 * many + 3], refs[-1]
    part, wide = heads_ref.shape
    half = half_ref.shape[1]
    columns = pl.ds(pl.multiple_of(info[0] * half, half), half)
    copies = [
        pltpu.make_async_copy(heads_ref, out_ref.at[pl.ds(0, part), pl.ds(0, wide)], sems.at[0]),
        pltpu.make_async_copy(merge_ref, out_ref.at[pl.ds(0, part), pl.ds(wide, merge_ref.shape[1])], sems.at[1]),
        pltpu.make_async_copy(up_ref.at[:, columns], half_ref, sems.at[2]),
    ]
    copies += [pltpu.make_async_copy(v, held[n], sems.at[3 + n]) for n, v in enumerate(vectors)]
    for copy in copies:
        copy.start()
    rows[...] = jnp.zeros_like(rows)
    arrive(copies[3:])
    for n, vector in enumerate(held):
        rows[n : n + 1, : vector.shape[1]] = vector[...].astype(F32)
    out_ref[part:, :] = rows[...].astype(BF)
    arrive(copies[:3])


def pick_kernel(info, images, rows_ref, unit_ref):
    unit_ref[...], _ = norm_parts(pad_images(picked_images(info, images), rows_ref))


def attend_kernel(shards, count, length, info, rows_ref, unit_ref, *refs):
    pieces = refs[:shards]
    middle_ref, mid_ref, heads, merge, small, up_bias, packed, mixed, vectors, sems = refs[shards:]
    me = info[0]
    width = rows_ref.shape[1]
    part = width // shards
    first = fetch(pieces, heads, sems, 0, me, part)
    second = fetch(pieces, merge, sems, shards, me, part, heads.shape[1])
    third = []
    for k, piece in enumerate(pieces):
        source = piece.at[pl.ds(part, 16)]
        third.append(pltpu.make_async_copy(source, vectors.at[jnp.bitwise_xor(me, k)], sems.at[2 * shards + k]))
        third[-1].start()
    arrive(third)
    hidden_part = up_bias.shape[1] // shards
    for at in range(shards):
        given = vectors[at].astype(F32)
        small[:, at * part : (at + 1) * part] = given[:8, :part]
        up_bias[:, at * hidden_part : (at + 1) * hidden_part] = given[8:9, :hidden_part]
    entry = (unit_ref[...] * small[PRE_GAIN : PRE_GAIN + 1] + small[PRE_SHIFT : PRE_SHIFT + 1]).astype(BF)
    arrive(first)
    packed[...] = (dot(entry, heads[...]) + packed_bias(small)).astype(BF)
    attention_forward(packed, mixed, count, length, width)
    arrive(second)
    middle = rows_ref[...] + dot(mixed[...], merge[...]) + small[MERGE_BIAS : MERGE_BIAS + 1]
    middle_ref[...] = middle
    mid_ref[...] = mid_rows(middle, small)[0]


def widen_kernel(shards, info, mid_ref, up_bias, *refs):
    act_ref, up, sems = refs[shards * 3 // 2 :]
    near, far = refs[: shards // 2], refs[shards // 2 : shards * 3 // 2]
    pieces = (*near, *zip(far[::2], far[1::2]))
    arrive(fetch(pieces, up, sems, 0, info[0], half=info[4]))
    hidden = dot(mid_ref[...], up[...]) + up_bias[...]
    act_ref[...] = gelu_parts(hidden)[0].astype(BF)


def narrow_kernel(shards, info, act_ref, middle_ref, small, *refs):
    out_ref, down, sems = refs[shards:]
    arrive(fetch(refs[:shards], down, sems, 0, info[0]))
    out = middle_ref[...] + dot(act_ref[...], down[...]) + small[DOWN_BIAS : DOWN_BIAS + 1]
    unpad(out_ref, out, BF)


def both_ways_kernel(
    info,
    first_rows,
    arrived,
    cotangent,
    small,
    up_bias,
    heads,
    merge,
    up,
    down,
    out_ref,
    sent_ref,
    packed,
    probs_ref,
    mixed,
    act_ref,
    slope_ref,
    entry_ref,
    unit_one_ref,
    inverse_one_ref,
    mid_ref,
    unit_two_ref,
    inverse_two_ref,
    rows_ref,
    grad_ref,
    grad_packed,
):
    leading = info[1] == 0
    count, length, width = arrived.shape
    rows = jnp.where(leading, first_rows[...], pad_images([arrived[n] for n in range(count)], rows_ref))
    entry_ref[...], unit_one_ref[...], inverse_one_ref[...] = entry_rows(rows, small)
    packed[...] = (dot(entry_ref[...], heads[...]) + packed_bias(small)).astype(BF)
    probs_ref[...] = attention_forward(packed, mixed, count, length, width)
    middle = rows + dot(mixed[...], merge[...]) + small[MERGE_BIAS : MERGE_BIAS + 1]
    mid_ref[...], unit_two_ref[...], inverse_two_ref[...] = mid_rows(middle, small)
    hidden = dot(mid_ref[...], up[...]) + up_bias[...]
    act, bell = gelu_parts(hidden)
    slope_ref[...] = gelu_slope(hidden, bell)
    act_ref[...] = act.astype(BF)
    out = middle + dot(act_ref[...], down[...]) + small[DOWN_BIAS : DOWN_BIAS + 1]
    unpad(out_ref, out, BF)
    incoming = pad_images([cotangent[n] for n in range(count)], grad_ref)
    grad_hidden = (dot_nt(incoming.astype(BF), down[...]) * slope_ref[...]).astype(BF)
    grad_mid = dot_nt(grad_hidden, up[...])
    grad_middle = incoming + norm_backward(
        grad_mid, unit_two_ref[...], inverse_two_ref[...], small[MID_GAIN : MID_GAIN + 1]
    )
    grad_mixed = dot_nt(grad_middle.astype(BF), merge[...]).astype(BF)
    attention_backward(packed, probs_ref[...], grad_mixed, grad_packed, count, length, width)
    grad_entry = dot_nt(grad_packed[...], heads[...])
    grad_in = grad_middle + norm_backward(
        grad_entry, unit_one_ref[...], inverse_one_ref[...], small[PRE_GAIN : PRE_GAIN + 1]
    )
    unpad(sent_ref, grad_in, BF)


def own_gradient(info, returned, cotangent, scratch):
    leading = info[1] == 0
    return pad_images(
        [jnp.where(leading, returned[n], cotangent[n]) for n in range(cotangent.shape[0])], scratch
    )


def rest_grad_kernel(
    shards,
    info,
    returned,
    cotangent,
    small,
    heads,
    merge,
    up,
    down,
    packed,
    probs_ref,
    mixed,
    act_ref,
    slope_ref,
    entry_ref,
    unit_one_ref,
    inverse_one_ref,
    mid_ref,
    unit_two_ref,
    inverse_two_ref,
    *refs,
):
    down_outs, up_outs, rest_outs = (refs[n * shards : (n + 1) * shards] for n in range(3))
    grad_in_ref, grad_ref, grad_packed, whole_up, whole_heads, whole_merge, extra = refs[3 * shards :]
    me, leading = info[0], info[1] == 0
    count, length, width = cotangent.shape
    part = width // shards
    incoming = own_gradient(info, returned, cotangent, grad_ref)
    extra[...] = jnp.zeros_like(extra)
    extra[DOWN_BIAS : DOWN_BIAS + 1, :] = column_sum(incoming)
    grad_out = incoming.astype(BF)
    high = act_ref.shape[1] // shards
    for k in range(shards):
        columns = pl.ds(pl.multiple_of(jnp.bitwise_xor(me, k) * high, high), high)
        down_outs[k][:high, :] = dot_tn(act_ref[:, columns], grad_out).astype(BF)
    grad_hidden = (dot_nt(grad_out, down[...]) * slope_ref[...]).astype(BF)
    whole_up[...] = dot_tn(mid_ref[...], grad_hidden).astype(BF)
    wide_sum = column_sum(grad_hidden.astype(F32))
    for n in range(wide_sum.shape[1] // width):
        extra[8 + n : 9 + n, :] = wide_sum[:, n * width : (n + 1) * width]
    grad_mid = dot_nt(grad_hidden, up[...])
    extra[MID_GAIN : MID_GAIN + 1, :] = column_sum(grad_mid * unit_two_ref[...])
    extra[MID_SHIFT : MID_SHIFT + 1, :] = column_sum(grad_mid)
    grad_middle = incoming + norm_backward(
        grad_mid, unit_two_ref[...], inverse_two_ref[...], small[MID_GAIN : MID_GAIN + 1]
    )
    grad_branch = grad_middle.astype(BF)
    extra[MERGE_BIAS : MERGE_BIAS + 1, :] = column_sum(grad_branch.astype(F32))
    whole_merge[...] = dot_tn(mixed[...], grad_branch).astype(BF)
    grad_mixed = dot_nt(grad_branch, merge[...]).astype(BF)
    attention_backward(packed, probs_ref[...], grad_mixed, grad_packed, count, length, width)
    packed_sum = column_sum(grad_packed[...].astype(F32))
    extra[QUERY_BIAS : QUERY_BIAS + 1, :] = packed_sum[:, :width]
    extra[VALUE_BIAS : VALUE_BIAS + 1, :] = packed_sum[:, 2 * width :]
    whole_heads[...] = dot_tn(entry_ref[...], grad_packed[...]).astype(BF)
    grad_entry = dot_nt(grad_packed[...], heads[...])
    extra[PRE_GAIN : PRE_GAIN + 1, :] = column_sum(grad_entry * unit_one_ref[...])
    extra[PRE_SHIFT : PRE_SHIFT + 1, :] = column_sum(grad_entry)
    grad_in = grad_middle + norm_backward(
        grad_entry, unit_one_ref[...], inverse_one_ref[...], small[PRE_GAIN : PRE_GAIN + 1]
    )
    rounded = grad_in.astype(BF).astype(F32)
    unpad(grad_in_ref, jnp.where(leading, grad_in, rounded), F32)
    wide = whole_heads.shape[1]
    for k in range(shards):
        rows = pl.ds(pl.multiple_of(jnp.bitwise_xor(me, k) * part, part), part)
        up_outs[k][...] = whole_up[rows, :]
        rest_outs[k][:, :wide] = whole_heads[rows, :]
        rest_outs[k][:, wide:] = whole_merge[rows, :]
        down_outs[k][high:, :] = extra[...].astype(BF)


def column_blocks_kernel(at, *refs):
    outs = [ref for ref in refs if ref.shape != refs[0].shape]
    wide = outs[0].shape[1]
    for k, out in enumerate(outs):
        columns = pl.ds(pl.multiple_of(jnp.bitwise_xor(at[0], k) * wide, wide), wide)
        out[...] = sum(ref[:, columns].astype(F32) for ref in refs[: len(refs) - len(outs)]).astype(BF)


def call(kernel, name, info, blocks, pieces, outs, scratch, flops, earlier=(), room=VMEM_BYTES):
    space = lambda kind, many: [pl.BlockSpec(memory_space=kind)] * many
    nbytes = sum(a.size * a.dtype.itemsize for a in (*blocks, *pieces, *outs))
    scalars = () if info is None else (info,)
    used = len(scalars) + len(blocks) + len(pieces)
    return pl.pallas_call(
        lambda *refs: kernel(*refs[:used], *refs[used + len(earlier) :]),
        out_shape=outs,
        in_specs=space(pltpu.SMEM, len(scalars)) + space(pltpu.VMEM, len(blocks)) + space(pl.ANY, len(pieces) + len(earlier)),
        out_specs=space(pltpu.VMEM, len(outs)),
        scratch_shapes=scratch,
        compiler_params=pltpu.CompilerParams(vmem_limit_bytes=room),
        cost_estimate=pl.CostEstimate(flops=flops, bytes_accessed=nbytes, transcendentals=0),
        name=name,
    )(*scalars, *blocks, *pieces, *earlier)


def after(value, *others):
    return lax.optimization_barrier((value, *others))[0]


def swapped(block, axis, bit):
    return lax.ppermute(block, axis, [(i, i ^ bit) for i in range(lax.axis_size(axis))])


def bits_of(size):
    return [1 << n for n in range(size.bit_length() - 1)]


def gather_nearer(pieces, axis):
    for bit in bits_of(lax.axis_size(axis))[:-1]:
        pieces = pieces + [swapped(piece, axis, bit) for piece in pieces]
    return pieces


def gather_pieces(shard, axis, *earlier):
    pieces = {0: shard}
    for bit in reversed(bits_of(lax.axis_size(axis))):
        pieces.update({k ^ bit: swapped(piece if k == 0 else after(piece, *earlier), axis, bit) for k, piece in list(pieces.items())})
    return [pieces[k] for k in range(len(pieces))]


def added(*terms):
    return sum(term.astype(F32) for term in terms).astype(BF)


def nearer_sums(pieces, axis):
    terms = {k: (piece,) for k, piece in enumerate(pieces)}
    *nearer, last = bits_of(lax.axis_size(axis))
    for bit in nearer:
        for k in sorted((k for k in terms if not k & bit), reverse=True):
            terms[k] += (swapped(added(*terms.pop(k ^ bit)), axis, bit),)
    return added(*terms[last]), terms[0]


def together(*values):
    return lax.optimization_barrier(values)


def rounded(*terms):
    return lax.reduce_precision(sum(term.astype(F32) for term in terms), 8, 7).astype(BF)


def chosen(at, options):
    while len(options) > 1:
        options = [jnp.where((at & 1) != 0, odd, even) for even, odd in zip(options[::2], options[1::2])]
        at = at >> 1
    return options[0]


def column_blocks(at, terms, count):
    high, wide = terms[0].shape
    shapes = (jax.ShapeDtypeStruct((high, wide // count), BF),) * count
    return call(column_blocks_kernel, "column_blocks", at.reshape(1), terms, (), shapes, [], 1)


def totals_over_line(leaving, kept, axes):
    scattered, axis = axes
    at = lax.axis_index(axis).astype(jnp.int32)
    size = lax.axis_size(axis)
    odd = (at & 1) != 0
    far = lambda block: swapped(block, scattered, lax.axis_size(scattered) // 2)
    others = lambda blocks: [swapped(blocks[k], axis, k) for k in range(1, size)]
    lower = lambda block: block[: block.shape[0] // 2]
    upper = lambda block: block[block.shape[0] // 2 :]
    own_half = lambda block: jnp.where(odd, upper(block), lower(block))
    whole = lambda own, other: jnp.concatenate([jnp.where(odd, other, own), jnp.where(odd, own, other)]).astype(F32)

    down_far, *leaving = together(far(leaving[0]), *leaving[1:])
    down = added(*kept[0], down_far)

    up_far, down_near = together(far(leaving[0]), swapped(down, axis, 1))
    up, down = added(*kept[1], up_far), added(down, down_near)

    rest_far, up_near, down_next = together(far(leaving[1]), swapped(up, axis, 1), swapped(own_half(down), axis, 2))
    blocks = column_blocks(at, (*kept[2], rest_far), size)
    pair = added(up, up_near)
    down = rounded(own_half(down), down_next)

    down_back, up_next, *received = together(swapped(down, axis, 1), swapped(own_half(pair), axis, 2), *others(blocks))
    own, up_full = rounded(blocks[0], *received), rounded(own_half(pair), up_next)

    up_total = whole(up_full, swapped(up_full, axis, 1))
    full = [own, *after(tuple(others([own] * size)), up_total)]
    rest_total = [chosen(at, [full[n ^ k] for k in range(size)]).astype(F32) for n in range(size)]
    return whole(down, down_back), up_total, rest_total, up


def totals_over(grads, axes):
    scattered, axis = axes
    leaving, kept = zip(*(nearer_sums(pieces, scattered) for pieces in grads))
    if lax.axis_size(axis) == 4:
        return totals_over_line(leaving, kept, axes)
    last = lax.axis_size(scattered) // 2
    sums = tuple(added(*terms, swapped(one, scattered, last)) for one, terms in zip(leaving, kept))
    down, up, rest = (total.astype(F32) for total in lax.psum(sums, axis))
    return down, up, jnp.split(rest, 4, axis=1), sums[1]


def local(
    images,
    slot_image,
    cotangent,
    pre_gain,
    pre_shift,
    heads_weight,
    query_bias,
    value_bias,
    merge_weight,
    merge_bias,
    mid_gain,
    mid_shift,
    up_weight,
    up_bias,
    down_weight,
    down_bias,
):
    me = lax.axis_index("fsdp").astype(jnp.int32)
    section = lax.axis_index("section").astype(jnp.int32)
    shards = lax.axis_size("fsdp")
    half = lax.axis_index("dp").astype(jnp.int32) & 1
    info = jnp.concatenate([jnp.stack([me, section]), slot_image[0], half[None]])
    count, length, width = images.shape
    tall = count * padded_length(length)
    part = width // shards
    wide = heads_weight.shape[2]
    hidden_width = up_weight.shape[2]

    shape = jax.ShapeDtypeStruct
    scratch_rows = pltpu.VMEM((tall, width), F32)
    scratch_packed = pltpu.VMEM((tall, wide), BF)
    scratch_mixed = pltpu.VMEM((tall, width), BF)
    sems = lambda many: pltpu.SemaphoreType.DMA((many * shards,))
    bind = lambda kernel: functools.partial(kernel, shards)
    work = 2 * tall * width
    full_heads, full_merge = shape((width, wide), BF), shape((width, width), BF)
    full_up, full_down = shape((width, hidden_width), BF), shape((hidden_width, width), BF)
    rows_wide, rows_bf, column = shape((tall, width), F32), shape((tall, width), BF), shape((tall, 1), F32)

    mix, up_half = call(
        pack_kernel,
        "pack",
        half.reshape(1),
        (),
        (
            heads_weight[0],
            merge_weight[0],
            up_weight[0],
            pre_gain,
            pre_shift,
            query_bias,
            value_bias,
            merge_bias,
            mid_gain,
            mid_shift,
            down_bias,
            up_bias,
        ),
        (shape((part + 16, wide + width), BF), shape((part, hidden_width // 2), BF)),
        [pltpu.VMEM((16, wide + width), F32)]
        + [pltpu.VMEM((1, part), BF)] * 8
        + [pltpu.VMEM(up_bias.shape, BF), pltpu.SemaphoreType.DMA((12,))],
        1,
        room=56 * 1024 * 1024,
    )
    first_rows, first_unit = call(pick_kernel, "pick", info, (images,), (), (rows_wide, rows_wide), [], 1)
    farthest = shards // 2
    up_far = swapped(up_half, "fsdp", farthest)
    mix_pieces = gather_pieces(mix, "fsdp", up_far, first_rows)
    up_other = swapped(after(up_far, mix_pieces[-1]), "dp", 1)
    up_near = gather_nearer([up_weight[0]], "fsdp")
    up_halves = (gather_nearer([one], "fsdp") for one in (up_far, up_other))

    middle, mid, heads, merge, small, wide_bias = call(
        functools.partial(attend_kernel, shards, count, length),
        "attend",
        info,
        (first_rows, first_unit),
        mix_pieces,
        (rows_wide, rows_bf, full_heads, full_merge, shape((8, width), F32), shape((1, hidden_width), F32)),
        [
            scratch_packed,
            scratch_mixed,
            pltpu.VMEM((shards, 16, wide + width), BF),
            sems(3),
        ],
        work * (wide + width),
    )
    down_pieces = gather_pieces(down_weight[0], "fsdp", mid)
    act, up = call(
        bind(widen_kernel),
        "widen",
        info,
        (mid, wide_bias),
        (*up_near, *(one for two in zip(*up_halves) for one in two)),
        (shape((tall, hidden_width), BF), full_up),
        [sems(2)],
        work * hidden_width,
        (down_pieces[shards // 2],),
    )
    first_out, down = call(
        bind(narrow_kernel),
        "narrow",
        info,
        (act, middle, small),
        down_pieces,
        (shape(images.shape, BF), full_down),
        [sems(1)],
        work * hidden_width,
    )
    arrived = lax.ppermute(first_out, "section", [(0, 1)])

    layer_out, sent, packed, probs, mixed, act, slope, *kept = call(
        both_ways_kernel,
        "both_ways",
        info,
        (first_rows, arrived, cotangent, small, wide_bias, heads, merge, up, down),
        (),
        (
            shape(images.shape, BF),
            shape(images.shape, BF),
            shape((tall, wide), BF),
            shape((2 * tall * (width // PAIR), tall // count), F32),
            rows_bf,
            shape((tall, hidden_width), BF),
            shape((tall, hidden_width), F32),
            rows_bf,
            rows_wide,
            column,
            rows_bf,
            rows_wide,
            column,
        ),
        [scratch_rows, scratch_rows, scratch_packed],
        2 * work * (wide + width + 2 * hidden_width),
    )
    returned = lax.ppermute(sent, "section", [(1, 0)])

    *grads, grad_in = call(
        bind(rest_grad_kernel),
        "rest_grad",
        info,
        (returned, cotangent, small, heads, merge, up, down, packed, probs, mixed, act, slope, *kept),
        (),
        (shape((hidden_width // shards + 16, width), BF),) * shards
        + (shape((part, hidden_width), BF),) * shards
        + (shape((part, wide + width), BF),) * shards
        + (shape(images.shape, F32),),
        [
            scratch_rows,
            scratch_packed,
            pltpu.VMEM((width, hidden_width), BF),
            pltpu.VMEM((width, wide), BF),
            pltpu.VMEM((width, width), BF),
            pltpu.VMEM((16, width), F32),
        ],
        2 * work * (wide + width + 2 * hidden_width),
    )
    down_total, up_total, rest_total, up_sum = totals_over(
        [grads[n * shards : (n + 1) * shards] for n in range(3)], ("fsdp", "dp")
    )
    layer_out, grad_in = after(layer_out, up_sum), after(grad_in, up_sum)

    vectors, down_total = down_total[-16:], down_total[:-16]
    heads_total, merge_total = jnp.concatenate(rest_total[:3], axis=1), rest_total[3]
    vector_total = lax.dynamic_slice(vectors, (0, me * part), (8, part))
    up_bias_total = lax.dynamic_slice(vectors, (8 + me, 0), (1, width))
    row = lambda n: vector_total[n : n + 1]
    return (
        layer_out[None],
        grad_in[None],
        row(PRE_GAIN),
        row(PRE_SHIFT),
        heads_total[None],
        row(QUERY_BIAS),
        row(VALUE_BIAS),
        merge_total[None],
        row(MERGE_BIAS),
        row(MID_GAIN),
        row(MID_SHIFT),
        up_total[None],
        up_bias_total,
        down_total[None],
        row(DOWN_BIAS),
    )


def solution(mesh):
    vector, matrix = P("section", "fsdp"), P("section", "fsdp", None)
    rows = P("section", ("fsdp", "dp"), None, None)
    weights = (
        vector,
        vector,
        matrix,
        vector,
        vector,
        matrix,
        vector,
        vector,
        vector,
        matrix,
        vector,
        matrix,
        vector,
    )
    blocks = P(("fsdp", "dp"), None, None)
    return jax.shard_map(
        local,
        mesh=mesh,
        in_specs=(blocks, P(("fsdp", "dp"), None), blocks, *weights),
        out_specs=(rows, rows, *weights),
        check_vma=False,
    )
```

```python
import functools

import jax
import jax.numpy as jnp
from jax import lax
from jax.experimental import pallas as pl
from jax.experimental.pallas import tpu as pltpu
from jax.sharding import PartitionSpec as P

HD = 64
PAIR = 2 * HD
EPS = 1e-06
SQRT_HALF = 0.7071067811865476
INV_ROOT_TAU = 0.3989422804014327
BF = jnp.bfloat16
F32 = jnp.float32
VMEM_BYTES = 20 * 1024 * 1024

PRE_GAIN, PRE_SHIFT, QUERY_BIAS, VALUE_BIAS, MERGE_BIAS, MID_GAIN, MID_SHIFT, DOWN_BIAS = range(8)


def padded_length(length):
    return -(-length // 16) * 16


def dot(a, b):
    return jnp.dot(a, b, preferred_element_type=F32)


def dot_nt(a, b):
    return lax.dot_general(a, b, (((1,), (1,)), ((), ())), preferred_element_type=F32)


def dot_tn(a, b):
    return lax.dot_general(a, b, (((0,), (0,)), ((), ())), preferred_element_type=F32)


def fetch(pieces, dest, sems, first, me, rows=None, column=0, half=0):
    copies = []
    for k, piece in enumerate(pieces):
        if rows is not None:
            piece = piece.at[pl.ds(0, rows), pl.ds(column, dest.shape[1])]
        blocks = piece if isinstance(piece, tuple) else (piece,)
        count, wide = blocks[0].shape
        start = pl.multiple_of(jnp.bitwise_xor(me, k) * count, count)
        for n, one in enumerate(blocks):
            target = dest.at[pl.ds(start, count)]
            if len(blocks) > 1:
                target = dest.at[pl.ds(start, count), pl.ds(pl.multiple_of(jnp.bitwise_xor(half, n) * wide, wide), wide)]
            copies.append(pltpu.make_async_copy(one, target, sems.at[first + len(copies)]))
    for copy in copies:
        copy.start()
    return copies


def arrive(copies):
    for copy in copies:
        copy.wait()


def pad_images(images, scratch):
    length = images[0].shape[0]
    step = padded_length(length)
    scratch[...] = jnp.zeros_like(scratch)
    for n, image in enumerate(images):
        scratch[n * step : n * step + length, :] = image.astype(F32)
    return scratch[...]


def unpad(ref, rows, kind):
    count, length, _ = ref.shape
    step = padded_length(length)
    for n in range(count):
        ref[n] = rows[n * step : n * step + length, :].astype(kind)


def norm_parts(rows):
    mean = jnp.mean(rows, axis=-1, keepdims=True)
    centered = rows - mean
    inverse = lax.rsqrt(jnp.mean(centered * centered, axis=-1, keepdims=True) + EPS)
    return centered * inverse, inverse


def norm_backward(grad_rows, normed, inverse, gain):
    scaled = grad_rows * gain
    mean_one = jnp.mean(scaled, axis=-1, keepdims=True)
    mean_two = jnp.mean(scaled * normed, axis=-1, keepdims=True)
    return inverse * (scaled - mean_one - normed * mean_two)


def column_sum(rows):
    return jnp.sum(rows, axis=0, keepdims=True)


def half_masks():
    lane = lax.broadcasted_iota(jnp.int32, (1, PAIR), 1)
    low = (lane < HD).astype(F32)
    return low.astype(BF), (1.0 - low).astype(BF)


def both_heads(rows):
    low, high = half_masks()
    return jnp.concatenate([rows * low, rows * high], axis=0)


def beside(stacked):
    half = stacked.shape[0] // 2
    lane = lax.broadcasted_iota(jnp.int32, (half, PAIR), 1)
    return jnp.where(lane < HD, stacked[:half], stacked[half:])


def qkv(packed, n, pair, step, width):
    rows = slice(n * step, (n + 1) * step)
    return tuple(packed[rows, part * width + pair * PAIR : part * width + (pair + 1) * PAIR] for part in range(3))


def head_pairs(packed, count, length, width):
    step = padded_length(length)
    parts = [qkv(packed, n, pair, step, width) for n in range(count) for pair in range(width // PAIR)]
    return [both_heads(queries) for queries, _, _ in parts], [keys for _, keys, _ in parts], [v for _, _, v in parts]


def block(rows, n, total):
    high = rows.shape[0] // total
    return rows[n * high : (n + 1) * high]


def attention_forward(packed, mixed, count, length, width):
    step = padded_length(length)
    queries, keys, values = head_pairs(packed, count, length, width)
    scores = jnp.concatenate([dot_nt(q, k) for q, k in zip(queries, keys)], axis=0) * HD**-0.5
    lane = lax.broadcasted_iota(jnp.int32, scores.shape, 1)
    scores = jnp.where(lane < length, scores, -1e30)
    grown = jnp.exp(scores - jnp.max(scores, axis=-1, keepdims=True))
    probs = grown * (1.0 / jnp.sum(grown, axis=-1, keepdims=True))
    rounded = probs.astype(BF)
    outs = [beside(dot(block(rounded, at, len(values)), v)).astype(BF) for at, v in enumerate(values)]
    for at, out in enumerate(outs):
        n, pair = divmod(at, width // PAIR)
        mixed[n * step : (n + 1) * step, pair * PAIR : (pair + 1) * PAIR] = out
    return probs


def attention_backward(packed, probs, grad_mixed, grad_packed, count, length, width):
    step = padded_length(length)
    queries, keys, values = head_pairs(packed, count, length, width)
    pairs = width // PAIR
    incoming = [
        both_heads(grad_mixed[n * step : (n + 1) * step, pair * PAIR : (pair + 1) * PAIR])
        for n in range(count)
        for pair in range(pairs)
    ]
    grad_probs = jnp.concatenate([dot_nt(g, v) for g, v in zip(incoming, values)], axis=0)
    inner = jnp.sum(probs * grad_probs, axis=-1, keepdims=True)
    grad_scores = (probs * (grad_probs - inner)).astype(BF)
    rounded = probs.astype(BF)
    total = len(keys)
    parts = [
        (
            beside(dot(block(grad_scores, at, total), keys[at])) * HD**-0.5,
            dot_tn(block(grad_scores, at, total), queries[at]) * HD**-0.5,
            dot_tn(block(rounded, at, total), incoming[at]),
        )
        for at in range(total)
    ]
    for at, three in enumerate(parts):
        n, pair = divmod(at, pairs)
        for part, value in enumerate(three):
            column = part * width + pair * PAIR
            grad_packed[n * step : (n + 1) * step, column : column + PAIR] = value.astype(BF)


def entry_rows(rows, small):
    normed, inverse = norm_parts(rows)
    return (normed * small[PRE_GAIN : PRE_GAIN + 1] + small[PRE_SHIFT : PRE_SHIFT + 1]).astype(BF), normed, inverse


def mid_rows(middle, small):
    normed, inverse = norm_parts(middle)
    return (normed * small[MID_GAIN : MID_GAIN + 1] + small[MID_SHIFT : MID_SHIFT + 1]).astype(BF), normed, inverse


def packed_bias(small):
    query = small[QUERY_BIAS : QUERY_BIAS + 1]
    return jnp.concatenate([query, jnp.zeros_like(query), small[VALUE_BIAS : VALUE_BIAS + 1]], axis=1)


def gelu_parts(hidden):
    bell = 0.5 * (1.0 + lax.erf(hidden * SQRT_HALF))
    return hidden * bell, bell


def gelu_slope(hidden, bell):
    return bell + hidden * jnp.exp(-0.5 * hidden * hidden) * INV_ROOT_TAU


def picked_images(info, images):
    return [
        jnp.where(info[2 + n] == 0, images[0], images[1]) for n in range(images.shape[0])
    ]


def pack_kernel(info, heads_ref, merge_ref, up_ref, *refs):
    many = (len(refs) - 4) // 2
    vectors, (out_ref, half_ref, rows, *held), sems = refs[:many], refs[many : 2 * many + 3], refs[-1]
    part, wide = heads_ref.shape
    half = half_ref.shape[1]
    columns = pl.ds(pl.multiple_of(info[0] * half, half), half)
    copies = [
        pltpu.make_async_copy(heads_ref, out_ref.at[pl.ds(0, part), pl.ds(0, wide)], sems.at[0]),
        pltpu.make_async_copy(merge_ref, out_ref.at[pl.ds(0, part), pl.ds(wide, merge_ref.shape[1])], sems.at[1]),
        pltpu.make_async_copy(up_ref.at[:, columns], half_ref, sems.at[2]),
    ]
    copies += [pltpu.make_async_copy(v, held[n], sems.at[3 + n]) for n, v in enumerate(vectors)]
    for copy in copies:
        copy.start()
    rows[...] = jnp.zeros_like(rows)
    arrive(copies[3:])
    for n, vector in enumerate(held):
        rows[n : n + 1, : vector.shape[1]] = vector[...].astype(F32)
    out_ref[part:, :] = rows[...].astype(BF)
    arrive(copies[:3])


def pick_kernel(info, images, rows_ref, unit_ref):
    unit_ref[...], _ = norm_parts(pad_images(picked_images(info, images), rows_ref))


def attend_kernel(shards, count, length, info, rows_ref, unit_ref, *refs):
    pieces = refs[:shards]
    middle_ref, mid_ref, heads, merge, small, up_bias, packed, mixed, vectors, sems = refs[shards:]
    me = info[0]
    width = rows_ref.shape[1]
    part = width // shards
    first = fetch(pieces, heads, sems, 0, me, part)
    second = fetch(pieces, merge, sems, shards, me, part, heads.shape[1])
    third = []
    for k, piece in enumerate(pieces):
        source = piece.at[pl.ds(part, 16)]
        third.append(pltpu.make_async_copy(source, vectors.at[jnp.bitwise_xor(me, k)], sems.at[2 * shards + k]))
        third[-1].start()
    arrive(third)
    hidden_part = up_bias.shape[1] // shards
    for at in range(shards):
        given = vectors[at].astype(F32)
        small[:, at * part : (at + 1) * part] = given[:8, :part]
        up_bias[:, at * hidden_part : (at + 1) * hidden_part] = given[8:9, :hidden_part]
    arrive(first)
    arrive(second)

    @pl.when(info[1] == 0)
    def _():
        entry = (unit_ref[...] * small[PRE_GAIN : PRE_GAIN + 1] + small[PRE_SHIFT : PRE_SHIFT + 1]).astype(BF)
        packed[...] = (dot(entry, heads[...]) + packed_bias(small)).astype(BF)
        attention_forward(packed, mixed, count, length, width)
        middle = rows_ref[...] + dot(mixed[...], merge[...]) + small[MERGE_BIAS : MERGE_BIAS + 1]
        middle_ref[...] = middle
        mid_ref[...] = mid_rows(middle, small)[0]


def feed_forward_kernel(shards, info, mid_ref, middle_ref, small, up_bias, *refs):
    near, far = refs[: shards // 2], refs[shards // 2 : shards * 3 // 2]
    down_pieces = refs[shards * 3 // 2 : shards * 5 // 2]
    out_ref, up, down, sems = refs[shards * 5 // 2 :]
    me = info[0]
    first = fetch((*near, *zip(far[::2], far[1::2])), up, sems, 0, me, half=info[4])
    second = fetch(down_pieces, down, sems, 2 * shards, me)
    arrive(first)
    arrive(second)

    @pl.when(info[1] == 0)
    def _():
        hidden = dot(mid_ref[...], up[...]) + up_bias[...]
        act = gelu_parts(hidden)[0].astype(BF)
        out = middle_ref[...] + dot(act, down[...]) + small[DOWN_BIAS : DOWN_BIAS + 1]
        unpad(out_ref, out, BF)


def act_gradient_kernel(cotangent, down, grad_act_ref, grad_ref):
    incoming = pad_images([cotangent[n] for n in range(cotangent.shape[0])], grad_ref)
    grad_act_ref[...] = dot_nt(incoming.astype(BF), down[...])


def both_ways_kernel(
    info,
    first_rows,
    arrived,
    cotangent,
    grad_act,
    small,
    up_bias,
    heads,
    merge,
    up,
    down,
    out_ref,
    sent_ref,
    packed,
    probs_ref,
    mixed,
    act_ref,
    slope_ref,
    entry_ref,
    unit_one_ref,
    inverse_one_ref,
    mid_ref,
    unit_two_ref,
    inverse_two_ref,
    rows_ref,
    grad_ref,
    grad_packed,
):
    leading = info[1] == 0
    count, length, width = arrived.shape
    rows = jnp.where(leading, first_rows[...], pad_images([arrived[n] for n in range(count)], rows_ref))
    entry_ref[...], unit_one_ref[...], inverse_one_ref[...] = entry_rows(rows, small)
    packed[...] = (dot(entry_ref[...], heads[...]) + packed_bias(small)).astype(BF)
    probs_ref[...] = attention_forward(packed, mixed, count, length, width)
    middle = rows + dot(mixed[...], merge[...]) + small[MERGE_BIAS : MERGE_BIAS + 1]
    mid_ref[...], unit_two_ref[...], inverse_two_ref[...] = mid_rows(middle, small)
    hidden = dot(mid_ref[...], up[...]) + up_bias[...]
    act, bell = gelu_parts(hidden)
    slope_ref[...] = gelu_slope(hidden, bell)
    act_ref[...] = act.astype(BF)
    out = middle + dot(act_ref[...], down[...]) + small[DOWN_BIAS : DOWN_BIAS + 1]
    unpad(out_ref, out, BF)
    incoming = pad_images([cotangent[n] for n in range(count)], grad_ref)
    grad_hidden = (grad_act[...] * slope_ref[...]).astype(BF)
    grad_mid = dot_nt(grad_hidden, up[...])
    grad_middle = incoming + norm_backward(
        grad_mid, unit_two_ref[...], inverse_two_ref[...], small[MID_GAIN : MID_GAIN + 1]
    )
    grad_mixed = dot_nt(grad_middle.astype(BF), merge[...]).astype(BF)
    attention_backward(packed, probs_ref[...], grad_mixed, grad_packed, count, length, width)
    grad_entry = dot_nt(grad_packed[...], heads[...])
    grad_in = grad_middle + norm_backward(
        grad_entry, unit_one_ref[...], inverse_one_ref[...], small[PRE_GAIN : PRE_GAIN + 1]
    )
    unpad(sent_ref, grad_in, BF)


def own_gradient(info, returned, cotangent, scratch):
    leading = info[1] == 0
    return pad_images(
        [jnp.where(leading, returned[n], cotangent[n]) for n in range(cotangent.shape[0])], scratch
    )


def rest_grad_kernel(
    shards,
    info,
    returned,
    cotangent,
    small,
    heads,
    merge,
    up,
    down,
    packed,
    probs_ref,
    mixed,
    act_ref,
    slope_ref,
    entry_ref,
    unit_one_ref,
    inverse_one_ref,
    mid_ref,
    unit_two_ref,
    inverse_two_ref,
    *refs,
):
    down_outs, up_outs, rest_outs = (refs[n * shards : (n + 1) * shards] for n in range(3))
    grad_in_ref, grad_ref, grad_packed, whole_up, whole_heads, whole_merge, extra = refs[3 * shards :]
    me, leading = info[0], info[1] == 0
    count, length, width = cotangent.shape
    part = width // shards
    incoming = own_gradient(info, returned, cotangent, grad_ref)
    extra[...] = jnp.zeros_like(extra)
    extra[DOWN_BIAS : DOWN_BIAS + 1, :] = column_sum(incoming)
    grad_out = incoming.astype(BF)
    high = act_ref.shape[1] // shards
    for k in range(shards):
        columns = pl.ds(pl.multiple_of(jnp.bitwise_xor(me, k) * high, high), high)
        down_outs[k][:high, :] = dot_tn(act_ref[:, columns], grad_out).astype(BF)
    grad_hidden = (dot_nt(grad_out, down[...]) * slope_ref[...]).astype(BF)
    whole_up[...] = dot_tn(mid_ref[...], grad_hidden).astype(BF)
    wide_sum = column_sum(grad_hidden.astype(F32))
    for n in range(wide_sum.shape[1] // width):
        extra[8 + n : 9 + n, :] = wide_sum[:, n * width : (n + 1) * width]
    grad_mid = dot_nt(grad_hidden, up[...])
    extra[MID_GAIN : MID_GAIN + 1, :] = column_sum(grad_mid * unit_two_ref[...])
    extra[MID_SHIFT : MID_SHIFT + 1, :] = column_sum(grad_mid)
    grad_middle = incoming + norm_backward(
        grad_mid, unit_two_ref[...], inverse_two_ref[...], small[MID_GAIN : MID_GAIN + 1]
    )
    grad_branch = grad_middle.astype(BF)
    extra[MERGE_BIAS : MERGE_BIAS + 1, :] = column_sum(grad_branch.astype(F32))
    whole_merge[...] = dot_tn(mixed[...], grad_branch).astype(BF)
    grad_mixed = dot_nt(grad_branch, merge[...]).astype(BF)
    attention_backward(packed, probs_ref[...], grad_mixed, grad_packed, count, length, width)
    packed_sum = column_sum(grad_packed[...].astype(F32))
    extra[QUERY_BIAS : QUERY_BIAS + 1, :] = packed_sum[:, :width]
    extra[VALUE_BIAS : VALUE_BIAS + 1, :] = packed_sum[:, 2 * width :]
    whole_heads[...] = dot_tn(entry_ref[...], grad_packed[...]).astype(BF)
    grad_entry = dot_nt(grad_packed[...], heads[...])
    extra[PRE_GAIN : PRE_GAIN + 1, :] = column_sum(grad_entry * unit_one_ref[...])
    extra[PRE_SHIFT : PRE_SHIFT + 1, :] = column_sum(grad_entry)
    grad_in = grad_middle + norm_backward(
        grad_entry, unit_one_ref[...], inverse_one_ref[...], small[PRE_GAIN : PRE_GAIN + 1]
    )
    rounded = grad_in.astype(BF).astype(F32)
    unpad(grad_in_ref, jnp.where(leading, grad_in, rounded), F32)
    wide = whole_heads.shape[1]
    for k in range(shards):
        rows = pl.ds(pl.multiple_of(jnp.bitwise_xor(me, k) * part, part), part)
        up_outs[k][...] = whole_up[rows, :]
        rest_outs[k][:, :wide] = whole_heads[rows, :]
        rest_outs[k][:, wide:] = whole_merge[rows, :]
        down_outs[k][high:, :] = extra[...].astype(BF)


def column_blocks_kernel(at, *refs):
    outs = [ref for ref in refs if ref.shape != refs[0].shape]
    wide = outs[0].shape[1]
    for k, out in enumerate(outs):
        columns = pl.ds(pl.multiple_of(jnp.bitwise_xor(at[0], k) * wide, wide), wide)
        out[...] = sum(ref[:, columns].astype(F32) for ref in refs[: len(refs) - len(outs)]).astype(BF)


def call(kernel, name, info, blocks, pieces, outs, scratch, flops, earlier=(), room=VMEM_BYTES):
    space = lambda kind, many: [pl.BlockSpec(memory_space=kind)] * many
    nbytes = sum(a.size * a.dtype.itemsize for a in (*blocks, *pieces, *outs))
    scalars = () if info is None else (info,)
    used = len(scalars) + len(blocks) + len(pieces)
    return pl.pallas_call(
        lambda *refs: kernel(*refs[:used], *refs[used + len(earlier) :]),
        out_shape=outs,
        in_specs=space(pltpu.SMEM, len(scalars)) + space(pltpu.VMEM, len(blocks)) + space(pl.ANY, len(pieces) + len(earlier)),
        out_specs=space(pltpu.VMEM, len(outs)),
        scratch_shapes=scratch,
        compiler_params=pltpu.CompilerParams(vmem_limit_bytes=room),
        cost_estimate=pl.CostEstimate(flops=flops, bytes_accessed=nbytes, transcendentals=0),
        name=name,
    )(*scalars, *blocks, *pieces, *earlier)


def after(value, *others):
    return lax.optimization_barrier((value, *others))[0]


def swapped(block, axis, bit):
    return lax.ppermute(block, axis, [(i, i ^ bit) for i in range(lax.axis_size(axis))])


def bits_of(size):
    return [1 << n for n in range(size.bit_length() - 1)]


def gather_nearer(pieces, axis):
    for bit in bits_of(lax.axis_size(axis))[:-1]:
        pieces = pieces + [swapped(piece, axis, bit) for piece in pieces]
    return pieces


def gather_pieces(shard, axis, *earlier):
    pieces = {0: shard}
    for bit in reversed(bits_of(lax.axis_size(axis))):
        pieces.update({k ^ bit: swapped(piece if k == 0 else after(piece, *earlier), axis, bit) for k, piece in list(pieces.items())})
    return [pieces[k] for k in range(len(pieces))]


def added(*terms):
    return sum(term.astype(F32) for term in terms).astype(BF)


def nearer_sums(pieces, axis):
    terms = {k: (piece,) for k, piece in enumerate(pieces)}
    *nearer, last = bits_of(lax.axis_size(axis))
    for bit in nearer:
        for k in sorted((k for k in terms if not k & bit), reverse=True):
            terms[k] += (swapped(added(*terms.pop(k ^ bit)), axis, bit),)
    return added(*terms[last]), terms[0]


def together(*values):
    return lax.optimization_barrier(values)


def rounded(*terms):
    return lax.reduce_precision(sum(term.astype(F32) for term in terms), 8, 7).astype(BF)


def chosen(at, options):
    while len(options) > 1:
        options = [jnp.where((at & 1) != 0, odd, even) for even, odd in zip(options[::2], options[1::2])]
        at = at >> 1
    return options[0]


def column_blocks(at, terms, count):
    high, wide = terms[0].shape
    shapes = (jax.ShapeDtypeStruct((high, wide // count), BF),) * count
    return call(column_blocks_kernel, "column_blocks", at.reshape(1), terms, (), shapes, [], 1)


def totals_over_line(leaving, kept, axes):
    scattered, axis = axes
    at = lax.axis_index(axis).astype(jnp.int32)
    size = lax.axis_size(axis)
    odd = (at & 1) != 0
    far = lambda block: swapped(block, scattered, lax.axis_size(scattered) // 2)
    others = lambda blocks: [swapped(blocks[k], axis, k) for k in range(1, size)]
    lower = lambda block: block[: block.shape[0] // 2]
    upper = lambda block: block[block.shape[0] // 2 :]
    own_half = lambda block: jnp.where(odd, upper(block), lower(block))
    other_half = lambda block: jnp.where(odd, lower(block), upper(block))
    whole = lambda own, other: jnp.concatenate([jnp.where(odd, other, own), jnp.where(odd, own, other)]).astype(F32)

    down_far, *leaving = together(far(leaving[0]), *leaving[1:])
    down = added(*kept[0], down_far)

    up_far, down_near, rest = together(far(leaving[0]), swapped(other_half(down), axis, 1), leaving[1])
    up, down = added(*kept[1], up_far), added(own_half(down), down_near)

    rest_far, up_near, down_next = together(far(rest), swapped(other_half(up), axis, 1), swapped(down, axis, 2))
    blocks = column_blocks(at, (*kept[2], rest_far), size)
    up, down = added(own_half(up), up_near), rounded(down, down_next)

    down_back, up_next, *received = together(swapped(down, axis, 1), swapped(up, axis, 2), *others(blocks))
    own, up_full = rounded(blocks[0], *received), rounded(up, up_next)

    up_total = whole(up_full, swapped(up_full, axis, 1))
    full = [own, *after(tuple(others([own] * size)), up_total)]
    rest_total = [chosen(at, [full[n ^ k] for k in range(size)]).astype(F32) for n in range(size)]
    return whole(down, down_back), up_total, rest_total, up


def totals_over(grads, axes):
    scattered, axis = axes
    leaving, kept = [], []
    for pieces in grads:
        one, terms = nearer_sums([after(piece, *leaving[:1]) for piece in pieces], scattered)
        leaving.append(one)
        kept.append(terms)
    if lax.axis_size(axis) == 4:
        return totals_over_line(leaving, kept, axes)
    last = lax.axis_size(scattered) // 2
    sums = tuple(added(*terms, swapped(one, scattered, last)) for one, terms in zip(leaving, kept))
    down, up, rest = (total.astype(F32) for total in lax.psum(sums, axis))
    return down, up, jnp.split(rest, 4, axis=1), sums[1]


def local(
    images,
    slot_image,
    cotangent,
    pre_gain,
    pre_shift,
    heads_weight,
    query_bias,
    value_bias,
    merge_weight,
    merge_bias,
    mid_gain,
    mid_shift,
    up_weight,
    up_bias,
    down_weight,
    down_bias,
):
    me = lax.axis_index("fsdp").astype(jnp.int32)
    section = lax.axis_index("section").astype(jnp.int32)
    shards = lax.axis_size("fsdp")
    half = lax.axis_index("dp").astype(jnp.int32) & 1
    info = jnp.concatenate([jnp.stack([me, section]), slot_image[0], half[None]])
    count, length, width = images.shape
    tall = count * padded_length(length)
    part = width // shards
    wide = heads_weight.shape[2]
    hidden_width = up_weight.shape[2]

    shape = jax.ShapeDtypeStruct
    scratch_rows = pltpu.VMEM((tall, width), F32)
    scratch_packed = pltpu.VMEM((tall, wide), BF)
    scratch_mixed = pltpu.VMEM((tall, width), BF)
    sems = lambda many: pltpu.SemaphoreType.DMA((many * shards,))
    bind = lambda kernel: functools.partial(kernel, shards)
    work = 2 * tall * width
    full_heads, full_merge = shape((width, wide), BF), shape((width, width), BF)
    full_up, full_down = shape((width, hidden_width), BF), shape((hidden_width, width), BF)
    rows_wide, rows_bf, column = shape((tall, width), F32), shape((tall, width), BF), shape((tall, 1), F32)

    mix, up_half = call(
        pack_kernel,
        "pack",
        half.reshape(1),
        (),
        (
            heads_weight[0],
            merge_weight[0],
            up_weight[0],
            pre_gain,
            pre_shift,
            query_bias,
            value_bias,
            merge_bias,
            mid_gain,
            mid_shift,
            down_bias,
            up_bias,
        ),
        (shape((part + 16, wide + width), BF), shape((part, hidden_width // 2), BF)),
        [pltpu.VMEM((16, wide + width), F32)]
        + [pltpu.VMEM((1, part), BF)] * 8
        + [pltpu.VMEM(up_bias.shape, BF), pltpu.SemaphoreType.DMA((12,))],
        1,
        room=56 * 1024 * 1024,
    )
    first_rows, first_unit = call(pick_kernel, "pick", info, (images,), (), (rows_wide, rows_wide), [], 1)
    farthest = shards // 2
    up_far = swapped(up_half, "fsdp", farthest)
    mix_pieces = gather_pieces(mix, "fsdp", up_far, first_rows)
    up_other = swapped(after(up_far, mix_pieces[-1]), "dp", 1)
    up_near = gather_nearer([up_weight[0]], "fsdp")
    up_halves = (gather_nearer([one], "fsdp") for one in (up_far, up_other))

    middle, mid, heads, merge, small, wide_bias = call(
        functools.partial(attend_kernel, shards, count, length),
        "attend",
        info,
        (first_rows, first_unit),
        mix_pieces,
        (rows_wide, rows_bf, full_heads, full_merge, shape((8, width), F32), shape((1, hidden_width), F32)),
        [
            scratch_packed,
            scratch_mixed,
            pltpu.VMEM((shards, 16, wide + width), BF),
            sems(3),
        ],
        work * (wide + width),
    )
    down_pieces = gather_pieces(down_weight[0], "fsdp", mid)
    first_out, up, down = call(
        bind(feed_forward_kernel),
        "feed_forward",
        info,
        (mid, middle, small, wide_bias),
        (*up_near, *(one for two in zip(*up_halves) for one in two), *down_pieces),
        (shape(images.shape, BF), full_up, full_down),
        [sems(3)],
        2 * work * hidden_width,
    )
    arrived = lax.ppermute(first_out, "section", [(0, 1)])

    (grad_act,) = call(
        act_gradient_kernel,
        "act_gradient",
        None,
        (cotangent, down),
        (),
        (shape((tall, hidden_width), F32),),
        [scratch_rows],
        work * hidden_width,
    )

    layer_out, sent, packed, probs, mixed, act, slope, *kept = call(
        both_ways_kernel,
        "both_ways",
        info,
        (first_rows, arrived, cotangent, grad_act, small, wide_bias, heads, merge, up, down),
        (),
        (
            shape(images.shape, BF),
            shape(images.shape, BF),
            shape((tall, wide), BF),
            shape((2 * tall * (width // PAIR), tall // count), F32),
            rows_bf,
            shape((tall, hidden_width), BF),
            shape((tall, hidden_width), F32),
            rows_bf,
            rows_wide,
            column,
            rows_bf,
            rows_wide,
            column,
        ),
        [scratch_rows, scratch_rows, scratch_packed],
        2 * work * (wide + width + 2 * hidden_width),
    )
    returned = lax.ppermute(sent, "section", [(1, 0)])

    *grads, grad_in = call(
        bind(rest_grad_kernel),
        "rest_grad",
        info,
        (returned, cotangent, small, heads, merge, up, down, packed, probs, mixed, act, slope, *kept),
        (),
        (shape((hidden_width // shards + 16, width), BF),) * shards
        + (shape((part, hidden_width), BF),) * shards
        + (shape((part, wide + width), BF),) * shards
        + (shape(images.shape, F32),),
        [
            scratch_rows,
            scratch_packed,
            pltpu.VMEM((width, hidden_width), BF),
            pltpu.VMEM((width, wide), BF),
            pltpu.VMEM((width, width), BF),
            pltpu.VMEM((16, width), F32),
        ],
        2 * work * (wide + width + 2 * hidden_width),
    )
    down_total, up_total, rest_total, up_sum = totals_over(
        [grads[n * shards : (n + 1) * shards] for n in range(3)], ("fsdp", "dp")
    )
    layer_out, grad_in = after(layer_out, up_sum), after(grad_in, up_sum)

    vectors, down_total = down_total[-16:], down_total[:-16]
    heads_total, merge_total = jnp.concatenate(rest_total[:3], axis=1), rest_total[3]
    vector_total = lax.dynamic_slice(vectors, (0, me * part), (8, part))
    up_bias_total = lax.dynamic_slice(vectors, (8 + me, 0), (1, width))
    row = lambda n: vector_total[n : n + 1]
    return (
        layer_out[None],
        grad_in[None],
        row(PRE_GAIN),
        row(PRE_SHIFT),
        heads_total[None],
        row(QUERY_BIAS),
        row(VALUE_BIAS),
        merge_total[None],
        row(MERGE_BIAS),
        row(MID_GAIN),
        row(MID_SHIFT),
        up_total[None],
        up_bias_total,
        down_total[None],
        row(DOWN_BIAS),
    )


def solution(mesh):
    vector, matrix = P("section", "fsdp"), P("section", "fsdp", None)
    rows = P("section", ("fsdp", "dp"), None, None)
    weights = (
        vector,
        vector,
        matrix,
        vector,
        vector,
        matrix,
        vector,
        vector,
        vector,
        matrix,
        vector,
        matrix,
        vector,
    )
    blocks = P(("fsdp", "dp"), None, None)
    return jax.shard_map(
        local,
        mesh=mesh,
        in_specs=(blocks, P(("fsdp", "dp"), None), blocks, *weights),
        out_specs=(rows, rows, *weights),
        check_vma=False,
    )
```

```python
import functools

import jax
import jax.numpy as jnp
from jax import lax
from jax.experimental import pallas as pl
from jax.experimental.pallas import tpu as pltpu
from jax.sharding import PartitionSpec as P

HD = 64
PAIR = 2 * HD
EPS = 1e-06
SQRT_HALF = 0.7071067811865476
INV_ROOT_TAU = 0.3989422804014327
BF = jnp.bfloat16
F32 = jnp.float32
VMEM_BYTES = 20 * 1024 * 1024

PRE_GAIN, PRE_SHIFT, QUERY_BIAS, VALUE_BIAS, MERGE_BIAS, MID_GAIN, MID_SHIFT, DOWN_BIAS = range(8)


def padded_length(length):
    return -(-length // 16) * 16


def dot(a, b):
    return jnp.dot(a, b, preferred_element_type=F32)


def dot_nt(a, b):
    return lax.dot_general(a, b, (((1,), (1,)), ((), ())), preferred_element_type=F32)


def dot_tn(a, b):
    return lax.dot_general(a, b, (((0,), (0,)), ((), ())), preferred_element_type=F32)


def fetch(pieces, dest, sems, first, me, rows=None, column=0, half=0):
    copies = []
    for k, piece in enumerate(pieces):
        if rows is not None:
            piece = piece.at[pl.ds(0, rows), pl.ds(column, dest.shape[1])]
        blocks = piece if isinstance(piece, tuple) else (piece,)
        count, wide = blocks[0].shape
        start = pl.multiple_of(jnp.bitwise_xor(me, k) * count, count)
        for n, one in enumerate(blocks):
            target = dest.at[pl.ds(start, count)]
            if len(blocks) > 1:
                target = dest.at[pl.ds(start, count), pl.ds(pl.multiple_of(jnp.bitwise_xor(half, n) * wide, wide), wide)]
            copies.append(pltpu.make_async_copy(one, target, sems.at[first + len(copies)]))
    for copy in copies:
        copy.start()
    return copies


def arrive(copies):
    for copy in copies:
        copy.wait()


def pad_images(images, scratch):
    length = images[0].shape[0]
    step = padded_length(length)
    scratch[...] = jnp.zeros_like(scratch)
    for n, image in enumerate(images):
        scratch[n * step : n * step + length, :] = image.astype(F32)
    return scratch[...]


def unpad(ref, rows, kind):
    count, length, _ = ref.shape
    step = padded_length(length)
    for n in range(count):
        ref[n] = rows[n * step : n * step + length, :].astype(kind)


def norm_parts(rows):
    mean = jnp.mean(rows, axis=-1, keepdims=True)
    centered = rows - mean
    inverse = lax.rsqrt(jnp.mean(centered * centered, axis=-1, keepdims=True) + EPS)
    return centered * inverse, inverse


def norm_backward(grad_rows, normed, inverse, gain):
    scaled = grad_rows * gain
    mean_one = jnp.mean(scaled, axis=-1, keepdims=True)
    mean_two = jnp.mean(scaled * normed, axis=-1, keepdims=True)
    return inverse * (scaled - mean_one - normed * mean_two)


def column_sum(rows):
    return jnp.sum(rows, axis=0, keepdims=True)


def half_masks():
    lane = lax.broadcasted_iota(jnp.int32, (1, PAIR), 1)
    low = (lane < HD).astype(F32)
    return low.astype(BF), (1.0 - low).astype(BF)


def both_heads(rows):
    low, high = half_masks()
    return jnp.concatenate([rows * low, rows * high], axis=0)


def beside(stacked):
    half = stacked.shape[0] // 2
    lane = lax.broadcasted_iota(jnp.int32, (half, PAIR), 1)
    return jnp.where(lane < HD, stacked[:half], stacked[half:])


def qkv(packed, n, pair, step, width):
    rows = slice(n * step, (n + 1) * step)
    return tuple(packed[rows, part * width + pair * PAIR : part * width + (pair + 1) * PAIR] for part in range(3))


def head_pairs(packed, count, length, width):
    step = padded_length(length)
    parts = [qkv(packed, n, pair, step, width) for n in range(count) for pair in range(width // PAIR)]
    return [both_heads(queries) for queries, _, _ in parts], [keys for _, keys, _ in parts], [v for _, _, v in parts]


def block(rows, n, total):
    high = rows.shape[0] // total
    return rows[n * high : (n + 1) * high]


def attention_forward(packed, mixed, count, length, width):
    step = padded_length(length)
    queries, keys, values = head_pairs(packed, count, length, width)
    scores = jnp.concatenate([dot_nt(q, k) for q, k in zip(queries, keys)], axis=0) * HD**-0.5
    lane = lax.broadcasted_iota(jnp.int32, scores.shape, 1)
    scores = jnp.where(lane < length, scores, -1e30)
    grown = jnp.exp(scores - jnp.max(scores, axis=-1, keepdims=True))
    probs = grown * (1.0 / jnp.sum(grown, axis=-1, keepdims=True))
    rounded = probs.astype(BF)
    outs = [beside(dot(block(rounded, at, len(values)), v)).astype(BF) for at, v in enumerate(values)]
    for at, out in enumerate(outs):
        n, pair = divmod(at, width // PAIR)
        mixed[n * step : (n + 1) * step, pair * PAIR : (pair + 1) * PAIR] = out
    return probs


def attention_backward(packed, probs, grad_mixed, grad_packed, count, length, width):
    step = padded_length(length)
    queries, keys, values = head_pairs(packed, count, length, width)
    pairs = width // PAIR
    incoming = [
        both_heads(grad_mixed[n * step : (n + 1) * step, pair * PAIR : (pair + 1) * PAIR])
        for n in range(count)
        for pair in range(pairs)
    ]
    grad_probs = jnp.concatenate([dot_nt(g, v) for g, v in zip(incoming, values)], axis=0)
    inner = jnp.sum(probs * grad_probs, axis=-1, keepdims=True)
    grad_scores = (probs * (grad_probs - inner)).astype(BF)
    rounded = probs.astype(BF)
    total = len(keys)
    parts = [
        (
            beside(dot(block(grad_scores, at, total), keys[at])) * HD**-0.5,
            dot_tn(block(grad_scores, at, total), queries[at]) * HD**-0.5,
            dot_tn(block(rounded, at, total), incoming[at]),
        )
        for at in range(total)
    ]
    for at, three in enumerate(parts):
        n, pair = divmod(at, pairs)
        for part, value in enumerate(three):
            column = part * width + pair * PAIR
            grad_packed[n * step : (n + 1) * step, column : column + PAIR] = value.astype(BF)


def entry_rows(rows, small):
    normed, inverse = norm_parts(rows)
    return (normed * small[PRE_GAIN : PRE_GAIN + 1] + small[PRE_SHIFT : PRE_SHIFT + 1]).astype(BF), normed, inverse


def mid_rows(middle, small):
    normed, inverse = norm_parts(middle)
    return (normed * small[MID_GAIN : MID_GAIN + 1] + small[MID_SHIFT : MID_SHIFT + 1]).astype(BF), normed, inverse


def packed_bias(small):
    query = small[QUERY_BIAS : QUERY_BIAS + 1]
    return jnp.concatenate([query, jnp.zeros_like(query), small[VALUE_BIAS : VALUE_BIAS + 1]], axis=1)


def gelu_parts(hidden):
    bell = 0.5 * (1.0 + lax.erf(hidden * SQRT_HALF))
    return hidden * bell, bell


def gelu_slope(hidden, bell):
    return bell + hidden * jnp.exp(-0.5 * hidden * hidden) * INV_ROOT_TAU


def picked_images(info, images):
    return [
        jnp.where(info[2 + n] == 0, images[0], images[1]) for n in range(images.shape[0])
    ]


def pack_kernel(info, heads_ref, merge_ref, up_ref, *refs):
    many = (len(refs) - 4) // 2
    vectors, (out_ref, half_ref, rows, *held), sems = refs[:many], refs[many : 2 * many + 3], refs[-1]
    part, wide = heads_ref.shape
    half = half_ref.shape[1]
    columns = pl.ds(pl.multiple_of(info[0] * half, half), half)
    copies = [
        pltpu.make_async_copy(heads_ref, out_ref.at[pl.ds(0, part), pl.ds(0, wide)], sems.at[0]),
        pltpu.make_async_copy(merge_ref, out_ref.at[pl.ds(0, part), pl.ds(wide, merge_ref.shape[1])], sems.at[1]),
        pltpu.make_async_copy(up_ref.at[:, columns], half_ref, sems.at[2]),
    ]
    copies += [pltpu.make_async_copy(v, held[n], sems.at[3 + n]) for n, v in enumerate(vectors)]
    for copy in copies:
        copy.start()
    rows[...] = jnp.zeros_like(rows)
    arrive(copies[3:])
    for n, vector in enumerate(held):
        rows[n : n + 1, : vector.shape[1]] = vector[...].astype(F32)
    out_ref[part:, :] = rows[...].astype(BF)
    arrive(copies[:3])


def pick_kernel(info, images, rows_ref, unit_ref):
    unit_ref[...], _ = norm_parts(pad_images(picked_images(info, images), rows_ref))


def attend_kernel(shards, count, length, info, rows_ref, unit_ref, *refs):
    pieces = refs[:shards]
    middle_ref, mid_ref, heads, merge, small, up_bias, packed, mixed, vectors, sems = refs[shards:]
    me = info[0]
    width = rows_ref.shape[1]
    part = width // shards
    first = fetch(pieces, heads, sems, 0, me, part)
    second = fetch(pieces, merge, sems, shards, me, part, heads.shape[1])
    third = []
    for k, piece in enumerate(pieces):
        source = piece.at[pl.ds(part, 16)]
        third.append(pltpu.make_async_copy(source, vectors.at[jnp.bitwise_xor(me, k)], sems.at[2 * shards + k]))
        third[-1].start()
    arrive(third)
    hidden_part = up_bias.shape[1] // shards
    for at in range(shards):
        given = vectors[at].astype(F32)
        small[:, at * part : (at + 1) * part] = given[:8, :part]
        up_bias[:, at * hidden_part : (at + 1) * hidden_part] = given[8:9, :hidden_part]
    arrive(first)
    arrive(second)

    @pl.when(info[1] == 0)
    def _():
        entry = (unit_ref[...] * small[PRE_GAIN : PRE_GAIN + 1] + small[PRE_SHIFT : PRE_SHIFT + 1]).astype(BF)
        packed[...] = (dot(entry, heads[...]) + packed_bias(small)).astype(BF)
        attention_forward(packed, mixed, count, length, width)
        middle = rows_ref[...] + dot(mixed[...], merge[...]) + small[MERGE_BIAS : MERGE_BIAS + 1]
        middle_ref[...] = middle
        mid_ref[...] = mid_rows(middle, small)[0]


def feed_forward_kernel(shards, info, mid_ref, middle_ref, small, up_bias, *refs):
    near, far = refs[: shards // 2], refs[shards // 2 : shards * 3 // 2]
    down_pieces = refs[shards * 3 // 2 : shards * 5 // 2]
    out_ref, up, down, sems = refs[shards * 5 // 2 :]
    me = info[0]
    first = fetch((*near, *zip(far[::2], far[1::2])), up, sems, 0, me, half=info[4])
    second = fetch(down_pieces, down, sems, 2 * shards, me)
    arrive(first)
    arrive(second)

    @pl.when(info[1] == 0)
    def _():
        hidden = dot(mid_ref[...], up[...]) + up_bias[...]
        act = gelu_parts(hidden)[0].astype(BF)
        out = middle_ref[...] + dot(act, down[...]) + small[DOWN_BIAS : DOWN_BIAS + 1]
        unpad(out_ref, out, BF)


def act_gradient_kernel(cotangent, down, grad_act_ref, grad_ref):
    incoming = pad_images([cotangent[n] for n in range(cotangent.shape[0])], grad_ref)
    grad_act_ref[...] = dot_nt(incoming.astype(BF), down[...])


def both_ways_kernel(
    info,
    first_rows,
    arrived,
    cotangent,
    grad_act,
    small,
    up_bias,
    heads,
    merge,
    up,
    down,
    out_ref,
    sent_ref,
    packed,
    probs_ref,
    mixed,
    act_ref,
    slope_ref,
    entry_ref,
    unit_one_ref,
    inverse_one_ref,
    mid_ref,
    unit_two_ref,
    inverse_two_ref,
    rows_ref,
    grad_ref,
    grad_packed,
):
    leading = info[1] == 0
    count, length, width = arrived.shape
    rows = jnp.where(leading, first_rows[...], pad_images([arrived[n] for n in range(count)], rows_ref))
    entry_ref[...], unit_one_ref[...], inverse_one_ref[...] = entry_rows(rows, small)
    packed[...] = (dot(entry_ref[...], heads[...]) + packed_bias(small)).astype(BF)
    probs_ref[...] = attention_forward(packed, mixed, count, length, width)
    middle = rows + dot(mixed[...], merge[...]) + small[MERGE_BIAS : MERGE_BIAS + 1]
    mid_ref[...], unit_two_ref[...], inverse_two_ref[...] = mid_rows(middle, small)
    hidden = dot(mid_ref[...], up[...]) + up_bias[...]
    act, bell = gelu_parts(hidden)
    slope_ref[...] = gelu_slope(hidden, bell)
    act_ref[...] = act.astype(BF)
    out = middle + dot(act_ref[...], down[...]) + small[DOWN_BIAS : DOWN_BIAS + 1]
    unpad(out_ref, out, BF)
    incoming = pad_images([cotangent[n] for n in range(count)], grad_ref)
    grad_hidden = (grad_act[...] * slope_ref[...]).astype(BF)
    grad_mid = dot_nt(grad_hidden, up[...])
    grad_middle = incoming + norm_backward(
        grad_mid, unit_two_ref[...], inverse_two_ref[...], small[MID_GAIN : MID_GAIN + 1]
    )
    grad_mixed = dot_nt(grad_middle.astype(BF), merge[...]).astype(BF)
    attention_backward(packed, probs_ref[...], grad_mixed, grad_packed, count, length, width)
    grad_entry = dot_nt(grad_packed[...], heads[...])
    grad_in = grad_middle + norm_backward(
        grad_entry, unit_one_ref[...], inverse_one_ref[...], small[PRE_GAIN : PRE_GAIN + 1]
    )
    unpad(sent_ref, grad_in, BF)


def own_gradient(info, returned, cotangent, scratch):
    leading = info[1] == 0
    return pad_images(
        [jnp.where(leading, returned[n], cotangent[n]) for n in range(cotangent.shape[0])], scratch
    )


def rest_grad_kernel(
    shards,
    info,
    returned,
    cotangent,
    small,
    heads,
    merge,
    up,
    down,
    packed,
    probs_ref,
    mixed,
    act_ref,
    slope_ref,
    entry_ref,
    unit_one_ref,
    inverse_one_ref,
    mid_ref,
    unit_two_ref,
    inverse_two_ref,
    *refs,
):
    down_outs, up_outs, rest_outs = (refs[n * shards : (n + 1) * shards] for n in range(3))
    grad_in_ref, grad_ref, grad_packed, whole_up, whole_heads, whole_merge, extra = refs[3 * shards :]
    me, leading = info[0], info[1] == 0
    count, length, width = cotangent.shape
    part = width // shards
    incoming = own_gradient(info, returned, cotangent, grad_ref)
    extra[...] = jnp.zeros_like(extra)
    extra[DOWN_BIAS : DOWN_BIAS + 1, :] = column_sum(incoming)
    grad_out = incoming.astype(BF)
    high = act_ref.shape[1] // shards
    for k in range(shards):
        columns = pl.ds(pl.multiple_of(jnp.bitwise_xor(me, k) * high, high), high)
        down_outs[k][:high, :] = dot_tn(act_ref[:, columns], grad_out).astype(BF)
    grad_hidden = (dot_nt(grad_out, down[...]) * slope_ref[...]).astype(BF)
    whole_up[...] = dot_tn(mid_ref[...], grad_hidden).astype(BF)
    wide_sum = column_sum(grad_hidden.astype(F32))
    for n in range(wide_sum.shape[1] // width):
        extra[8 + n : 9 + n, :] = wide_sum[:, n * width : (n + 1) * width]
    grad_mid = dot_nt(grad_hidden, up[...])
    extra[MID_GAIN : MID_GAIN + 1, :] = column_sum(grad_mid * unit_two_ref[...])
    extra[MID_SHIFT : MID_SHIFT + 1, :] = column_sum(grad_mid)
    grad_middle = incoming + norm_backward(
        grad_mid, unit_two_ref[...], inverse_two_ref[...], small[MID_GAIN : MID_GAIN + 1]
    )
    grad_branch = grad_middle.astype(BF)
    extra[MERGE_BIAS : MERGE_BIAS + 1, :] = column_sum(grad_branch.astype(F32))
    whole_merge[...] = dot_tn(mixed[...], grad_branch).astype(BF)
    grad_mixed = dot_nt(grad_branch, merge[...]).astype(BF)
    attention_backward(packed, probs_ref[...], grad_mixed, grad_packed, count, length, width)
    packed_sum = column_sum(grad_packed[...].astype(F32))
    extra[QUERY_BIAS : QUERY_BIAS + 1, :] = packed_sum[:, :width]
    extra[VALUE_BIAS : VALUE_BIAS + 1, :] = packed_sum[:, 2 * width :]
    whole_heads[...] = dot_tn(entry_ref[...], grad_packed[...]).astype(BF)
    grad_entry = dot_nt(grad_packed[...], heads[...])
    extra[PRE_GAIN : PRE_GAIN + 1, :] = column_sum(grad_entry * unit_one_ref[...])
    extra[PRE_SHIFT : PRE_SHIFT + 1, :] = column_sum(grad_entry)
    grad_in = grad_middle + norm_backward(
        grad_entry, unit_one_ref[...], inverse_one_ref[...], small[PRE_GAIN : PRE_GAIN + 1]
    )
    rounded = grad_in.astype(BF).astype(F32)
    unpad(grad_in_ref, jnp.where(leading, grad_in, rounded), F32)
    wide = whole_heads.shape[1]
    for k in range(shards):
        rows = pl.ds(pl.multiple_of(jnp.bitwise_xor(me, k) * part, part), part)
        up_outs[k][...] = whole_up[rows, :]
        rest_outs[k][:, :wide] = whole_heads[rows, :]
        rest_outs[k][:, wide:] = whole_merge[rows, :]
        down_outs[k][high:, :] = extra[...].astype(BF)


def column_blocks_kernel(at, *refs):
    outs = [ref for ref in refs if ref.shape != refs[0].shape]
    wide = outs[0].shape[1]
    for k, out in enumerate(outs):
        columns = pl.ds(pl.multiple_of(jnp.bitwise_xor(at[0], k) * wide, wide), wide)
        out[...] = sum(ref[:, columns].astype(F32) for ref in refs[: len(refs) - len(outs)]).astype(BF)


def call(kernel, name, info, blocks, pieces, outs, scratch, flops, earlier=(), room=VMEM_BYTES):
    space = lambda kind, many: [pl.BlockSpec(memory_space=kind)] * many
    nbytes = sum(a.size * a.dtype.itemsize for a in (*blocks, *pieces, *outs))
    scalars = () if info is None else (info,)
    used = len(scalars) + len(blocks) + len(pieces)
    return pl.pallas_call(
        lambda *refs: kernel(*refs[:used], *refs[used + len(earlier) :]),
        out_shape=outs,
        in_specs=space(pltpu.SMEM, len(scalars)) + space(pltpu.VMEM, len(blocks)) + space(pl.ANY, len(pieces) + len(earlier)),
        out_specs=space(pltpu.VMEM, len(outs)),
        scratch_shapes=scratch,
        compiler_params=pltpu.CompilerParams(vmem_limit_bytes=room),
        cost_estimate=pl.CostEstimate(flops=flops, bytes_accessed=nbytes, transcendentals=0),
        name=name,
    )(*scalars, *blocks, *pieces, *earlier)


def after(value, *others):
    return lax.optimization_barrier((value, *others))[0]


def swapped(block, axis, bit):
    return lax.ppermute(block, axis, [(i, i ^ bit) for i in range(lax.axis_size(axis))])


def bits_of(size):
    return [1 << n for n in range(size.bit_length() - 1)]


def gather_nearer(pieces, axis):
    for bit in bits_of(lax.axis_size(axis))[:-1]:
        pieces = pieces + [swapped(piece, axis, bit) for piece in pieces]
    return pieces


def gather_pieces(shard, axis, *earlier):
    pieces = {0: shard}
    for bit in reversed(bits_of(lax.axis_size(axis))):
        pieces.update({k ^ bit: swapped(piece if k == 0 else after(piece, *earlier), axis, bit) for k, piece in list(pieces.items())})
    return [pieces[k] for k in range(len(pieces))]


def added(*terms):
    return sum(term.astype(F32) for term in terms).astype(BF)


def nearer_sums(pieces, axis):
    terms = {k: (piece,) for k, piece in enumerate(pieces)}
    *nearer, last = bits_of(lax.axis_size(axis))
    for bit in nearer:
        for k in sorted((k for k in terms if not k & bit), reverse=True):
            terms[k] += (swapped(added(*terms.pop(k ^ bit)), axis, bit),)
    return added(*terms[last]), terms[0]


def together(*values):
    return lax.optimization_barrier(values)


def rounded(*terms):
    return lax.reduce_precision(sum(term.astype(F32) for term in terms), 8, 7).astype(BF)


def chosen(at, options):
    while len(options) > 1:
        options = [jnp.where((at & 1) != 0, odd, even) for even, odd in zip(options[::2], options[1::2])]
        at = at >> 1
    return options[0]


def column_blocks(at, terms, count):
    high, wide = terms[0].shape
    shapes = (jax.ShapeDtypeStruct((high, wide // count), BF),) * count
    return call(column_blocks_kernel, "column_blocks", at.reshape(1), terms, (), shapes, [], 1)


def totals_over_line(leaving, kept, axes):
    scattered, axis = axes
    at = lax.axis_index(axis).astype(jnp.int32)
    size = lax.axis_size(axis)
    odd = (at & 1) != 0
    far = lambda block: swapped(block, scattered, lax.axis_size(scattered) // 2)
    others = lambda blocks: [swapped(blocks[k], axis, k) for k in range(1, size)]
    lower = lambda block: block[: block.shape[0] // 2]
    upper = lambda block: block[block.shape[0] // 2 :]
    own_half = lambda block: jnp.where(odd, upper(block), lower(block))
    other_half = lambda block: jnp.where(odd, lower(block), upper(block))
    whole = lambda own, other: jnp.concatenate([jnp.where(odd, other, own), jnp.where(odd, own, other)]).astype(F32)

    down_far, *leaving = together(far(leaving[0]), *leaving[1:])
    down = added(*kept[0], down_far)

    up_far, down_near, rest = together(far(leaving[0]), swapped(other_half(down), axis, 1), leaving[1])
    up, down = added(*kept[1], up_far), added(own_half(down), down_near)

    rest_far, up_near, down_next = together(far(rest), swapped(other_half(up), axis, 1), swapped(down, axis, 2))
    blocks = column_blocks(at, (*kept[2], rest_far), size)
    up, down = added(own_half(up), up_near), rounded(down, down_next)

    down_back = swapped(down, axis, 1)
    up_next, *received = together(swapped(up, axis, 2), *others(blocks))
    own, up_full = rounded(blocks[0], *received), rounded(up, up_next)

    up_total = whole(up_full, swapped(up_full, axis, 1))
    full = [own, *after(tuple(others([own] * size)), up_total)]
    rest_total = [chosen(at, [full[n ^ k] for k in range(size)]).astype(F32) for n in range(size)]
    return whole(down, down_back), up_total, rest_total, up


def totals_over(grads, axes):
    scattered, axis = axes
    leaving, kept = [], []
    for pieces in grads:
        one, terms = nearer_sums([after(piece, *leaving[:1]) for piece in pieces], scattered)
        leaving.append(one)
        kept.append(terms)
    if lax.axis_size(axis) == 4:
        return totals_over_line(leaving, kept, axes)
    last = lax.axis_size(scattered) // 2
    sums = tuple(added(*terms, swapped(one, scattered, last)) for one, terms in zip(leaving, kept))
    down, up, rest = (total.astype(F32) for total in lax.psum(sums, axis))
    return down, up, jnp.split(rest, 4, axis=1), sums[1]


def local(
    images,
    slot_image,
    cotangent,
    pre_gain,
    pre_shift,
    heads_weight,
    query_bias,
    value_bias,
    merge_weight,
    merge_bias,
    mid_gain,
    mid_shift,
    up_weight,
    up_bias,
    down_weight,
    down_bias,
):
    me = lax.axis_index("fsdp").astype(jnp.int32)
    section = lax.axis_index("section").astype(jnp.int32)
    shards = lax.axis_size("fsdp")
    half = lax.axis_index("dp").astype(jnp.int32) & 1
    info = jnp.concatenate([jnp.stack([me, section]), slot_image[0], half[None]])
    count, length, width = images.shape
    tall = count * padded_length(length)
    part = width // shards
    wide = heads_weight.shape[2]
    hidden_width = up_weight.shape[2]

    shape = jax.ShapeDtypeStruct
    scratch_rows = pltpu.VMEM((tall, width), F32)
    scratch_packed = pltpu.VMEM((tall, wide), BF)
    scratch_mixed = pltpu.VMEM((tall, width), BF)
    sems = lambda many: pltpu.SemaphoreType.DMA((many * shards,))
    bind = lambda kernel: functools.partial(kernel, shards)
    work = 2 * tall * width
    full_heads, full_merge = shape((width, wide), BF), shape((width, width), BF)
    full_up, full_down = shape((width, hidden_width), BF), shape((hidden_width, width), BF)
    rows_wide, rows_bf, column = shape((tall, width), F32), shape((tall, width), BF), shape((tall, 1), F32)

    mix, up_half = call(
        pack_kernel,
        "pack",
        half.reshape(1),
        (),
        (
            heads_weight[0],
            merge_weight[0],
            up_weight[0],
            pre_gain,
            pre_shift,
            query_bias,
            value_bias,
            merge_bias,
            mid_gain,
            mid_shift,
            down_bias,
            up_bias,
        ),
        (shape((part + 16, wide + width), BF), shape((part, hidden_width // 2), BF)),
        [pltpu.VMEM((16, wide + width), F32)]
        + [pltpu.VMEM((1, part), BF)] * 8
        + [pltpu.VMEM(up_bias.shape, BF), pltpu.SemaphoreType.DMA((12,))],
        1,
        room=56 * 1024 * 1024,
    )
    first_rows, first_unit = call(pick_kernel, "pick", info, (images,), (), (rows_wide, rows_wide), [], 1)
    farthest = shards // 2
    up_far = swapped(up_half, "fsdp", farthest)
    mix_pieces = gather_pieces(mix, "fsdp", up_far, first_rows)
    up_other = swapped(after(up_far, mix_pieces[-1]), "dp", 1)
    up_near = gather_nearer([up_weight[0]], "fsdp")
    up_halves = (gather_nearer([one], "fsdp") for one in (up_far, up_other))

    middle, mid, heads, merge, small, wide_bias = call(
        functools.partial(attend_kernel, shards, count, length),
        "attend",
        info,
        (first_rows, first_unit),
        mix_pieces,
        (rows_wide, rows_bf, full_heads, full_merge, shape((8, width), F32), shape((1, hidden_width), F32)),
        [
            scratch_packed,
            scratch_mixed,
            pltpu.VMEM((shards, 16, wide + width), BF),
            sems(3),
        ],
        work * (wide + width),
    )
    down_pieces = gather_pieces(down_weight[0], "fsdp", mid)
    first_out, up, down = call(
        bind(feed_forward_kernel),
        "feed_forward",
        info,
        (mid, middle, small, wide_bias),
        (*up_near, *(one for two in zip(*up_halves) for one in two), *down_pieces),
        (shape(images.shape, BF), full_up, full_down),
        [sems(3)],
        2 * work * hidden_width,
    )
    arrived = lax.ppermute(first_out, "section", [(0, 1)])

    (grad_act,) = call(
        act_gradient_kernel,
        "act_gradient",
        None,
        (cotangent, down),
        (),
        (shape((tall, hidden_width), F32),),
        [scratch_rows],
        work * hidden_width,
    )

    layer_out, sent, packed, probs, mixed, act, slope, *kept = call(
        both_ways_kernel,
        "both_ways",
        info,
        (first_rows, arrived, cotangent, grad_act, small, wide_bias, heads, merge, up, down),
        (),
        (
            shape(images.shape, BF),
            shape(images.shape, BF),
            shape((tall, wide), BF),
            shape((2 * tall * (width // PAIR), tall // count), F32),
            rows_bf,
            shape((tall, hidden_width), BF),
            shape((tall, hidden_width), F32),
            rows_bf,
            rows_wide,
            column,
            rows_bf,
            rows_wide,
            column,
        ),
        [scratch_rows, scratch_rows, scratch_packed],
        2 * work * (wide + width + 2 * hidden_width),
    )
    returned = lax.ppermute(sent, "section", [(1, 0)])

    *grads, grad_in = call(
        bind(rest_grad_kernel),
        "rest_grad",
        info,
        (returned, cotangent, small, heads, merge, up, down, packed, probs, mixed, act, slope, *kept),
        (),
        (shape((hidden_width // shards + 16, width), BF),) * shards
        + (shape((part, hidden_width), BF),) * shards
        + (shape((part, wide + width), BF),) * shards
        + (shape(images.shape, F32),),
        [
            scratch_rows,
            scratch_packed,
            pltpu.VMEM((width, hidden_width), BF),
            pltpu.VMEM((width, wide), BF),
            pltpu.VMEM((width, width), BF),
            pltpu.VMEM((16, width), F32),
        ],
        2 * work * (wide + width + 2 * hidden_width),
    )
    down_total, up_total, rest_total, up_sum = totals_over(
        [grads[n * shards : (n + 1) * shards] for n in range(3)], ("fsdp", "dp")
    )
    layer_out, grad_in = after(layer_out, up_sum), after(grad_in, up_sum)

    vectors, down_total = down_total[-16:], down_total[:-16]
    heads_total, merge_total = jnp.concatenate(rest_total[:3], axis=1), rest_total[3]
    vector_total = lax.dynamic_slice(vectors, (0, me * part), (8, part))
    up_bias_total = lax.dynamic_slice(vectors, (8 + me, 0), (1, width))
    row = lambda n: vector_total[n : n + 1]
    return (
        layer_out[None],
        grad_in[None],
        row(PRE_GAIN),
        row(PRE_SHIFT),
        heads_total[None],
        row(QUERY_BIAS),
        row(VALUE_BIAS),
        merge_total[None],
        row(MERGE_BIAS),
        row(MID_GAIN),
        row(MID_SHIFT),
        up_total[None],
        up_bias_total,
        down_total[None],
        row(DOWN_BIAS),
    )


def solution(mesh):
    vector, matrix = P("section", "fsdp"), P("section", "fsdp", None)
    rows = P("section", ("fsdp", "dp"), None, None)
    weights = (
        vector,
        vector,
        matrix,
        vector,
        vector,
        matrix,
        vector,
        vector,
        vector,
        matrix,
        vector,
        matrix,
        vector,
    )
    blocks = P(("fsdp", "dp"), None, None)
    return jax.shard_map(
        local,
        mesh=mesh,
        in_specs=(blocks, P(("fsdp", "dp"), None), blocks, *weights),
        out_specs=(rows, rows, *weights),
        check_vma=False,
    )
```

```python
import functools

import jax
import jax.numpy as jnp
from jax import lax
from jax.experimental import pallas as pl
from jax.experimental.pallas import tpu as pltpu
from jax.sharding import PartitionSpec as P

HD = 64
PAIR = 2 * HD
EPS = 1e-06
SQRT_HALF = 0.7071067811865476
INV_ROOT_TAU = 0.3989422804014327
BF = jnp.bfloat16
F32 = jnp.float32
VMEM_BYTES = 20 * 1024 * 1024

PRE_GAIN, PRE_SHIFT, QUERY_BIAS, VALUE_BIAS, MERGE_BIAS, MID_GAIN, MID_SHIFT, DOWN_BIAS = range(8)


def padded_length(length):
    return -(-length // 16) * 16


def dot(a, b):
    return jnp.dot(a, b, preferred_element_type=F32)


def dot_nt(a, b):
    return lax.dot_general(a, b, (((1,), (1,)), ((), ())), preferred_element_type=F32)


def dot_tn(a, b):
    return lax.dot_general(a, b, (((0,), (0,)), ((), ())), preferred_element_type=F32)


def fetch(pieces, dest, sems, first, me, rows=None, column=0, half=0):
    copies = []
    for k, piece in enumerate(pieces):
        if rows is not None:
            piece = piece.at[pl.ds(0, rows), pl.ds(column, dest.shape[1])]
        blocks = piece if isinstance(piece, tuple) else (piece,)
        count, wide = blocks[0].shape
        start = pl.multiple_of(jnp.bitwise_xor(me, k) * count, count)
        for n, one in enumerate(blocks):
            target = dest.at[pl.ds(start, count)]
            if len(blocks) > 1:
                target = dest.at[pl.ds(start, count), pl.ds(pl.multiple_of(jnp.bitwise_xor(half, n) * wide, wide), wide)]
            copies.append(pltpu.make_async_copy(one, target, sems.at[first + len(copies)]))
    for copy in copies:
        copy.start()
    return copies


def arrive(copies):
    for copy in copies:
        copy.wait()


def pad_images(images, scratch):
    length = images[0].shape[0]
    step = padded_length(length)
    scratch[...] = jnp.zeros_like(scratch)
    for n, image in enumerate(images):
        scratch[n * step : n * step + length, :] = image.astype(F32)
    return scratch[...]


def unpad(ref, rows, kind):
    count, length, _ = ref.shape
    step = padded_length(length)
    for n in range(count):
        ref[n] = rows[n * step : n * step + length, :].astype(kind)


def norm_parts(rows):
    mean = jnp.mean(rows, axis=-1, keepdims=True)
    centered = rows - mean
    inverse = lax.rsqrt(jnp.mean(centered * centered, axis=-1, keepdims=True) + EPS)
    return centered * inverse, inverse


def norm_backward(grad_rows, normed, inverse, gain):
    scaled = grad_rows * gain
    mean_one = jnp.mean(scaled, axis=-1, keepdims=True)
    mean_two = jnp.mean(scaled * normed, axis=-1, keepdims=True)
    return inverse * (scaled - mean_one - normed * mean_two)


def column_sum(rows):
    return jnp.sum(rows, axis=0, keepdims=True)


def half_masks():
    lane = lax.broadcasted_iota(jnp.int32, (1, PAIR), 1)
    low = (lane < HD).astype(F32)
    return low.astype(BF), (1.0 - low).astype(BF)


def both_heads(rows):
    low, high = half_masks()
    return jnp.concatenate([rows * low, rows * high], axis=0)


def beside(stacked):
    half = stacked.shape[0] // 2
    lane = lax.broadcasted_iota(jnp.int32, (half, PAIR), 1)
    return jnp.where(lane < HD, stacked[:half], stacked[half:])


def qkv(packed, n, pair, step, width):
    rows = slice(n * step, (n + 1) * step)
    return tuple(packed[rows, part * width + pair * PAIR : part * width + (pair + 1) * PAIR] for part in range(3))


def head_pairs(packed, count, length, width):
    step = padded_length(length)
    parts = [qkv(packed, n, pair, step, width) for n in range(count) for pair in range(width // PAIR)]
    return [both_heads(queries) for queries, _, _ in parts], [keys for _, keys, _ in parts], [v for _, _, v in parts]


def block(rows, n, total):
    high = rows.shape[0] // total
    return rows[n * high : (n + 1) * high]


def attention_forward(packed, mixed, count, length, width):
    step = padded_length(length)
    queries, keys, values = head_pairs(packed, count, length, width)
    scores = jnp.concatenate([dot_nt(q, k) for q, k in zip(queries, keys)], axis=0) * HD**-0.5
    lane = lax.broadcasted_iota(jnp.int32, scores.shape, 1)
    scores = jnp.where(lane < length, scores, -1e30)
    grown = jnp.exp(scores - jnp.max(scores, axis=-1, keepdims=True))
    probs = grown * (1.0 / jnp.sum(grown, axis=-1, keepdims=True))
    rounded = probs.astype(BF)
    outs = [beside(dot(block(rounded, at, len(values)), v)).astype(BF) for at, v in enumerate(values)]
    for at, out in enumerate(outs):
        n, pair = divmod(at, width // PAIR)
        mixed[n * step : (n + 1) * step, pair * PAIR : (pair + 1) * PAIR] = out
    return probs


def attention_backward(packed, probs, grad_mixed, grad_packed, count, length, width):
    step = padded_length(length)
    queries, keys, values = head_pairs(packed, count, length, width)
    pairs = width // PAIR
    incoming = [
        both_heads(grad_mixed[n * step : (n + 1) * step, pair * PAIR : (pair + 1) * PAIR])
        for n in range(count)
        for pair in range(pairs)
    ]
    grad_probs = jnp.concatenate([dot_nt(g, v) for g, v in zip(incoming, values)], axis=0)
    inner = jnp.sum(probs * grad_probs, axis=-1, keepdims=True)
    grad_scores = (probs * (grad_probs - inner)).astype(BF)
    rounded = probs.astype(BF)
    total = len(keys)
    parts = [
        (
            beside(dot(block(grad_scores, at, total), keys[at])) * HD**-0.5,
            dot_tn(block(grad_scores, at, total), queries[at]) * HD**-0.5,
            dot_tn(block(rounded, at, total), incoming[at]),
        )
        for at in range(total)
    ]
    for at, three in enumerate(parts):
        n, pair = divmod(at, pairs)
        for part, value in enumerate(three):
            column = part * width + pair * PAIR
            grad_packed[n * step : (n + 1) * step, column : column + PAIR] = value.astype(BF)


def entry_rows(rows, small):
    normed, inverse = norm_parts(rows)
    return (normed * small[PRE_GAIN : PRE_GAIN + 1] + small[PRE_SHIFT : PRE_SHIFT + 1]).astype(BF), normed, inverse


def mid_rows(middle, small):
    normed, inverse = norm_parts(middle)
    return (normed * small[MID_GAIN : MID_GAIN + 1] + small[MID_SHIFT : MID_SHIFT + 1]).astype(BF), normed, inverse


def packed_bias(small):
    query = small[QUERY_BIAS : QUERY_BIAS + 1]
    return jnp.concatenate([query, jnp.zeros_like(query), small[VALUE_BIAS : VALUE_BIAS + 1]], axis=1)


def gelu_parts(hidden):
    bell = 0.5 * (1.0 + lax.erf(hidden * SQRT_HALF))
    return hidden * bell, bell


def gelu_slope(hidden, bell):
    return bell + hidden * jnp.exp(-0.5 * hidden * hidden) * INV_ROOT_TAU


def picked_images(info, images):
    return [
        jnp.where(info[2 + n] == 0, images[0], images[1]) for n in range(images.shape[0])
    ]


def pack_kernel(info, heads_ref, merge_ref, up_ref, *refs):
    many = (len(refs) - 4) // 2
    vectors, (out_ref, half_ref, rows, *held), sems = refs[:many], refs[many : 2 * many + 3], refs[-1]
    part, wide = heads_ref.shape
    half = half_ref.shape[1]
    columns = pl.ds(pl.multiple_of(info[0] * half, half), half)
    copies = [
        pltpu.make_async_copy(heads_ref, out_ref.at[pl.ds(0, part), pl.ds(0, wide)], sems.at[0]),
        pltpu.make_async_copy(merge_ref, out_ref.at[pl.ds(0, part), pl.ds(wide, merge_ref.shape[1])], sems.at[1]),
        pltpu.make_async_copy(up_ref.at[:, columns], half_ref, sems.at[2]),
    ]
    copies += [pltpu.make_async_copy(v, held[n], sems.at[3 + n]) for n, v in enumerate(vectors)]
    for copy in copies:
        copy.start()
    rows[...] = jnp.zeros_like(rows)
    arrive(copies[3:])
    for n, vector in enumerate(held):
        rows[n : n + 1, : vector.shape[1]] = vector[...].astype(F32)
    out_ref[part:, :] = rows[...].astype(BF)
    arrive(copies[:3])


def pick_kernel(info, images, mix_ref, rows_ref, unit_ref, own_ref, sem):
    copy = pltpu.make_async_copy(mix_ref, own_ref, sem)
    copy.start()
    unit_ref[...], _ = norm_parts(pad_images(picked_images(info, images), rows_ref))
    copy.wait()


def attend_kernel(shards, count, length, info, rows_ref, unit_ref, *refs):
    pieces = refs[:shards]
    middle_ref, mid_ref, heads, merge, small, up_bias, packed, mixed, vectors, sems = refs[shards:]
    me = info[0]
    width = rows_ref.shape[1]
    part = width // shards
    first = fetch(pieces, heads, sems, 0, me, part)
    second = fetch(pieces, merge, sems, shards, me, part, heads.shape[1])
    third = []
    for k, piece in enumerate(pieces):
        source = piece.at[pl.ds(part, 16)]
        third.append(pltpu.make_async_copy(source, vectors.at[jnp.bitwise_xor(me, k)], sems.at[2 * shards + k]))
        third[-1].start()
    arrive(third)
    hidden_part = up_bias.shape[1] // shards
    for at in range(shards):
        given = vectors[at].astype(F32)
        small[:, at * part : (at + 1) * part] = given[:8, :part]
        up_bias[:, at * hidden_part : (at + 1) * hidden_part] = given[8:9, :hidden_part]
    arrive(first)
    arrive(second)

    @pl.when(info[1] == 0)
    def _():
        entry = (unit_ref[...] * small[PRE_GAIN : PRE_GAIN + 1] + small[PRE_SHIFT : PRE_SHIFT + 1]).astype(BF)
        packed[...] = (dot(entry, heads[...]) + packed_bias(small)).astype(BF)
        attention_forward(packed, mixed, count, length, width)
        middle = rows_ref[...] + dot(mixed[...], merge[...]) + small[MERGE_BIAS : MERGE_BIAS + 1]
        middle_ref[...] = middle
        mid_ref[...] = mid_rows(middle, small)[0]


def feed_forward_kernel(shards, info, mid_ref, middle_ref, small, up_bias, *refs):
    near, far = refs[: shards // 2], refs[shards // 2 : shards * 3 // 2]
    down_pieces = refs[shards * 3 // 2 : shards * 5 // 2]
    out_ref, up, down, sems = refs[shards * 5 // 2 :]
    me = info[0]
    first = fetch((*near, *zip(far[::2], far[1::2])), up, sems, 0, me, half=info[4])
    second = fetch(down_pieces, down, sems, 2 * shards, me)
    arrive(first)
    arrive(second)

    @pl.when(info[1] == 0)
    def _():
        hidden = dot(mid_ref[...], up[...]) + up_bias[...]
        act = gelu_parts(hidden)[0].astype(BF)
        out = middle_ref[...] + dot(act, down[...]) + small[DOWN_BIAS : DOWN_BIAS + 1]
        unpad(out_ref, out, BF)


def act_gradient_kernel(cotangent, down, grad_act_ref, grad_ref):
    incoming = pad_images([cotangent[n] for n in range(cotangent.shape[0])], grad_ref)
    grad_act_ref[...] = dot_nt(incoming.astype(BF), down[...])


def both_ways_kernel(
    info,
    first_rows,
    arrived,
    cotangent,
    grad_act,
    small,
    up_bias,
    heads,
    merge,
    up,
    down,
    out_ref,
    sent_ref,
    packed,
    probs_ref,
    mixed,
    act_ref,
    slope_ref,
    entry_ref,
    unit_one_ref,
    inverse_one_ref,
    mid_ref,
    unit_two_ref,
    inverse_two_ref,
    rows_ref,
    grad_ref,
    grad_packed,
):
    leading = info[1] == 0
    count, length, width = arrived.shape
    rows = jnp.where(leading, first_rows[...], pad_images([arrived[n] for n in range(count)], rows_ref))
    entry_ref[...], unit_one_ref[...], inverse_one_ref[...] = entry_rows(rows, small)
    packed[...] = (dot(entry_ref[...], heads[...]) + packed_bias(small)).astype(BF)
    probs_ref[...] = attention_forward(packed, mixed, count, length, width)
    middle = rows + dot(mixed[...], merge[...]) + small[MERGE_BIAS : MERGE_BIAS + 1]
    mid_ref[...], unit_two_ref[...], inverse_two_ref[...] = mid_rows(middle, small)
    hidden = dot(mid_ref[...], up[...]) + up_bias[...]
    act, bell = gelu_parts(hidden)
    slope_ref[...] = gelu_slope(hidden, bell)
    act_ref[...] = act.astype(BF)
    out = middle + dot(act_ref[...], down[...]) + small[DOWN_BIAS : DOWN_BIAS + 1]
    unpad(out_ref, out, BF)
    incoming = pad_images([cotangent[n] for n in range(count)], grad_ref)
    grad_hidden = (grad_act[...] * slope_ref[...]).astype(BF)
    grad_mid = dot_nt(grad_hidden, up[...])
    grad_middle = incoming + norm_backward(
        grad_mid, unit_two_ref[...], inverse_two_ref[...], small[MID_GAIN : MID_GAIN + 1]
    )
    grad_mixed = dot_nt(grad_middle.astype(BF), merge[...]).astype(BF)
    attention_backward(packed, probs_ref[...], grad_mixed, grad_packed, count, length, width)
    grad_entry = dot_nt(grad_packed[...], heads[...])
    grad_in = grad_middle + norm_backward(
        grad_entry, unit_one_ref[...], inverse_one_ref[...], small[PRE_GAIN : PRE_GAIN + 1]
    )
    unpad(sent_ref, grad_in, BF)


def own_gradient(info, returned, cotangent, scratch):
    leading = info[1] == 0
    return pad_images(
        [jnp.where(leading, returned[n], cotangent[n]) for n in range(cotangent.shape[0])], scratch
    )


def rest_grad_kernel(
    shards,
    info,
    returned,
    cotangent,
    small,
    heads,
    merge,
    up,
    down,
    packed,
    probs_ref,
    mixed,
    act_ref,
    slope_ref,
    entry_ref,
    unit_one_ref,
    inverse_one_ref,
    mid_ref,
    unit_two_ref,
    inverse_two_ref,
    *refs,
):
    down_outs, up_outs, rest_outs = (refs[n * shards : (n + 1) * shards] for n in range(3))
    grad_in_ref, grad_ref, grad_packed, whole_up, whole_heads, whole_merge, extra = refs[3 * shards :]
    me, leading = info[0], info[1] == 0
    count, length, width = cotangent.shape
    part = width // shards
    incoming = own_gradient(info, returned, cotangent, grad_ref)
    extra[...] = jnp.zeros_like(extra)
    extra[DOWN_BIAS : DOWN_BIAS + 1, :] = column_sum(incoming)
    grad_out = incoming.astype(BF)
    high = act_ref.shape[1] // shards
    for k in range(shards):
        columns = pl.ds(pl.multiple_of(jnp.bitwise_xor(me, k) * high, high), high)
        down_outs[k][:high, :] = dot_tn(act_ref[:, columns], grad_out).astype(BF)
    grad_hidden = (dot_nt(grad_out, down[...]) * slope_ref[...]).astype(BF)
    whole_up[...] = dot_tn(mid_ref[...], grad_hidden).astype(BF)
    wide_sum = column_sum(grad_hidden.astype(F32))
    for n in range(wide_sum.shape[1] // width):
        extra[8 + n : 9 + n, :] = wide_sum[:, n * width : (n + 1) * width]
    grad_mid = dot_nt(grad_hidden, up[...])
    extra[MID_GAIN : MID_GAIN + 1, :] = column_sum(grad_mid * unit_two_ref[...])
    extra[MID_SHIFT : MID_SHIFT + 1, :] = column_sum(grad_mid)
    grad_middle = incoming + norm_backward(
        grad_mid, unit_two_ref[...], inverse_two_ref[...], small[MID_GAIN : MID_GAIN + 1]
    )
    grad_branch = grad_middle.astype(BF)
    extra[MERGE_BIAS : MERGE_BIAS + 1, :] = column_sum(grad_branch.astype(F32))
    whole_merge[...] = dot_tn(mixed[...], grad_branch).astype(BF)
    grad_mixed = dot_nt(grad_branch, merge[...]).astype(BF)
    attention_backward(packed, probs_ref[...], grad_mixed, grad_packed, count, length, width)
    packed_sum = column_sum(grad_packed[...].astype(F32))
    extra[QUERY_BIAS : QUERY_BIAS + 1, :] = packed_sum[:, :width]
    extra[VALUE_BIAS : VALUE_BIAS + 1, :] = packed_sum[:, 2 * width :]
    whole_heads[...] = dot_tn(entry_ref[...], grad_packed[...]).astype(BF)
    grad_entry = dot_nt(grad_packed[...], heads[...])
    extra[PRE_GAIN : PRE_GAIN + 1, :] = column_sum(grad_entry * unit_one_ref[...])
    extra[PRE_SHIFT : PRE_SHIFT + 1, :] = column_sum(grad_entry)
    grad_in = grad_middle + norm_backward(
        grad_entry, unit_one_ref[...], inverse_one_ref[...], small[PRE_GAIN : PRE_GAIN + 1]
    )
    rounded = grad_in.astype(BF).astype(F32)
    unpad(grad_in_ref, jnp.where(leading, grad_in, rounded), F32)
    wide = whole_heads.shape[1]
    for k in range(shards):
        rows = pl.ds(pl.multiple_of(jnp.bitwise_xor(me, k) * part, part), part)
        up_outs[k][...] = whole_up[rows, :]
        rest_outs[k][:, :wide] = whole_heads[rows, :]
        rest_outs[k][:, wide:] = whole_merge[rows, :]
        down_outs[k][high:, :] = extra[...].astype(BF)


def column_blocks_kernel(at, *refs):
    outs = [ref for ref in refs if ref.shape != refs[0].shape]
    wide = outs[0].shape[1]
    for k, out in enumerate(outs):
        columns = pl.ds(pl.multiple_of(jnp.bitwise_xor(at[0], k) * wide, wide), wide)
        out[...] = sum(ref[:, columns].astype(F32) for ref in refs[: len(refs) - len(outs)]).astype(BF)


def call(kernel, name, info, blocks, pieces, outs, scratch, flops, earlier=(), room=VMEM_BYTES):
    space = lambda kind, many: [pl.BlockSpec(memory_space=kind)] * many
    nbytes = sum(a.size * a.dtype.itemsize for a in (*blocks, *pieces, *outs))
    scalars = () if info is None else (info,)
    used = len(scalars) + len(blocks) + len(pieces)
    return pl.pallas_call(
        lambda *refs: kernel(*refs[:used], *refs[used + len(earlier) :]),
        out_shape=outs,
        in_specs=space(pltpu.SMEM, len(scalars)) + space(pltpu.VMEM, len(blocks)) + space(pl.ANY, len(pieces) + len(earlier)),
        out_specs=space(pltpu.VMEM, len(outs)),
        scratch_shapes=scratch,
        compiler_params=pltpu.CompilerParams(vmem_limit_bytes=room),
        cost_estimate=pl.CostEstimate(flops=flops, bytes_accessed=nbytes, transcendentals=0),
        name=name,
    )(*scalars, *blocks, *pieces, *earlier)


def after(value, *others):
    return lax.optimization_barrier((value, *others))[0]


def swapped(block, axis, bit):
    return lax.ppermute(block, axis, [(i, i ^ bit) for i in range(lax.axis_size(axis))])


def bits_of(size):
    return [1 << n for n in range(size.bit_length() - 1)]


def gather_nearer(pieces, axis):
    for bit in bits_of(lax.axis_size(axis))[:-1]:
        pieces = pieces + [swapped(piece, axis, bit) for piece in pieces]
    return pieces


def gather_pieces(shard, axis, *earlier):
    pieces = {0: shard}
    for bit in reversed(bits_of(lax.axis_size(axis))):
        pieces.update({k ^ bit: swapped(piece if k == 0 else after(piece, *earlier), axis, bit) for k, piece in list(pieces.items())})
    return [pieces[k] for k in range(len(pieces))]


def added(*terms):
    return sum(term.astype(F32) for term in terms).astype(BF)


def nearer_sums(pieces, axis):
    terms = {k: (piece,) for k, piece in enumerate(pieces)}
    *nearer, last = bits_of(lax.axis_size(axis))
    for bit in nearer:
        for k in sorted((k for k in terms if not k & bit), reverse=True):
            terms[k] += (swapped(added(*terms.pop(k ^ bit)), axis, bit),)
    return added(*terms[last]), terms[0]


def together(*values):
    return lax.optimization_barrier(values)


def rounded(*terms):
    return lax.reduce_precision(sum(term.astype(F32) for term in terms), 8, 7).astype(BF)


def chosen(at, options):
    while len(options) > 1:
        options = [jnp.where((at & 1) != 0, odd, even) for even, odd in zip(options[::2], options[1::2])]
        at = at >> 1
    return options[0]


def column_blocks(at, terms, count):
    high, wide = terms[0].shape
    shapes = (jax.ShapeDtypeStruct((high, wide // count), BF),) * count
    return call(column_blocks_kernel, "column_blocks", at.reshape(1), terms, (), shapes, [], 1)


def totals_over_line(leaving, kept, axes):
    scattered, axis = axes
    at = lax.axis_index(axis).astype(jnp.int32)
    size = lax.axis_size(axis)
    odd = (at & 1) != 0
    far = lambda block: swapped(block, scattered, lax.axis_size(scattered) // 2)
    others = lambda blocks: [swapped(blocks[k], axis, k) for k in range(1, size)]
    lower = lambda block: block[: block.shape[0] // 2]
    upper = lambda block: block[block.shape[0] // 2 :]
    own_half = lambda block: jnp.where(odd, upper(block), lower(block))
    other_half = lambda block: jnp.where(odd, lower(block), upper(block))
    whole = lambda own, other: jnp.concatenate([jnp.where(odd, other, own), jnp.where(odd, own, other)]).astype(F32)

    down_far, *leaving = together(far(leaving[0]), *leaving[1:])
    down = added(*kept[0], down_far)

    down_near = swapped(other_half(down), axis, 1)
    rest = after(leaving[1], down_near)
    up_far, down_near = after(far(leaving[0]), down_near), down_near
    up, down = added(*kept[1], up_far), added(own_half(down), down_near)

    rest_far, up_near, down_next = together(far(rest), swapped(other_half(up), axis, 1), swapped(down, axis, 2))
    blocks = column_blocks(at, (*kept[2], rest_far), size)
    up, down = added(own_half(up), up_near), rounded(down, down_next)

    down_back = swapped(down, axis, 1)
    up_next, *received = together(swapped(up, axis, 2), *others(blocks))
    own, up_full = rounded(blocks[0], *received), rounded(up, up_next)

    up_total = whole(up_full, swapped(up_full, axis, 1))
    full = [own, *after(tuple(others([own] * size)), up_total)]
    rest_total = [chosen(at, [full[n ^ k] for k in range(size)]).astype(F32) for n in range(size)]
    return whole(down, down_back), up_total, rest_total, up


def totals_over(grads, axes):
    scattered, axis = axes
    first, later = grads[0], grads[1:]
    first_leaving, first_kept = nearer_sums(first, scattered)
    first_leaving, *tied = together(first_leaving, *later)
    leaving, kept = zip((first_leaving, first_kept), *(nearer_sums(pieces, scattered) for pieces in tied))
    if lax.axis_size(axis) == 4:
        return totals_over_line(leaving, kept, axes)
    last = lax.axis_size(scattered) // 2
    sums = tuple(added(*terms, swapped(one, scattered, last)) for one, terms in zip(leaving, kept))
    down, up, rest = (total.astype(F32) for total in lax.psum(sums, axis))
    return down, up, jnp.split(rest, 4, axis=1), sums[1]


def local(
    images,
    slot_image,
    cotangent,
    pre_gain,
    pre_shift,
    heads_weight,
    query_bias,
    value_bias,
    merge_weight,
    merge_bias,
    mid_gain,
    mid_shift,
    up_weight,
    up_bias,
    down_weight,
    down_bias,
):
    me = lax.axis_index("fsdp").astype(jnp.int32)
    section = lax.axis_index("section").astype(jnp.int32)
    shards = lax.axis_size("fsdp")
    half = lax.axis_index("dp").astype(jnp.int32) & 1
    info = jnp.concatenate([jnp.stack([me, section]), slot_image[0], half[None]])
    count, length, width = images.shape
    tall = count * padded_length(length)
    part = width // shards
    wide = heads_weight.shape[2]
    hidden_width = up_weight.shape[2]

    shape = jax.ShapeDtypeStruct
    scratch_rows = pltpu.VMEM((tall, width), F32)
    scratch_packed = pltpu.VMEM((tall, wide), BF)
    scratch_mixed = pltpu.VMEM((tall, width), BF)
    sems = lambda many: pltpu.SemaphoreType.DMA((many * shards,))
    bind = lambda kernel: functools.partial(kernel, shards)
    work = 2 * tall * width
    full_heads, full_merge = shape((width, wide), BF), shape((width, width), BF)
    full_up, full_down = shape((width, hidden_width), BF), shape((hidden_width, width), BF)
    rows_wide, rows_bf, column = shape((tall, width), F32), shape((tall, width), BF), shape((tall, 1), F32)

    mix, up_half = call(
        pack_kernel,
        "pack",
        half.reshape(1),
        (),
        (
            heads_weight[0],
            merge_weight[0],
            up_weight[0],
            pre_gain,
            pre_shift,
            query_bias,
            value_bias,
            merge_bias,
            mid_gain,
            mid_shift,
            down_bias,
            up_bias,
        ),
        (shape((part + 16, wide + width), BF), shape((part, hidden_width // 2), BF)),
        [pltpu.VMEM((16, wide + width), F32)]
        + [pltpu.VMEM((1, part), BF)] * 8
        + [pltpu.VMEM(up_bias.shape, BF), pltpu.SemaphoreType.DMA((12,))],
        1,
        room=56 * 1024 * 1024,
    )
    first_rows, first_unit, own_mix = call(
        pick_kernel,
        "pick",
        info,
        (images,),
        (mix,),
        (rows_wide, rows_wide, shape(mix.shape, BF)),
        [pltpu.SemaphoreType.DMA(())],
        1,
    )
    farthest = shards // 2
    up_far = swapped(up_half, "fsdp", farthest)
    mix_pieces = [own_mix, *gather_pieces(mix, "fsdp", up_far, first_rows)[1:]]
    up_other = swapped(after(up_far, mix_pieces[-1]), "dp", 1)
    up_near = gather_nearer([up_weight[0]], "fsdp")
    up_halves = (gather_nearer([one], "fsdp") for one in (up_far, up_other))

    middle, mid, heads, merge, small, wide_bias = call(
        functools.partial(attend_kernel, shards, count, length),
        "attend",
        info,
        (first_rows, first_unit),
        mix_pieces,
        (rows_wide, rows_bf, full_heads, full_merge, shape((8, width), F32), shape((1, hidden_width), F32)),
        [
            scratch_packed,
            scratch_mixed,
            pltpu.VMEM((shards, 16, wide + width), BF),
            sems(3),
        ],
        work * (wide + width),
    )
    down_pieces = gather_pieces(down_weight[0], "fsdp", mid)
    first_out, up, down = call(
        bind(feed_forward_kernel),
        "feed_forward",
        info,
        (mid, middle, small, wide_bias),
        (*up_near, *(one for two in zip(*up_halves) for one in two), *down_pieces),
        (shape(images.shape, BF), full_up, full_down),
        [sems(3)],
        2 * work * hidden_width,
    )
    arrived = lax.ppermute(first_out, "section", [(0, 1)])

    (grad_act,) = call(
        act_gradient_kernel,
        "act_gradient",
        None,
        (cotangent, down),
        (),
        (shape((tall, hidden_width), F32),),
        [scratch_rows],
        work * hidden_width,
    )

    layer_out, sent, packed, probs, mixed, act, slope, *kept = call(
        both_ways_kernel,
        "both_ways",
        info,
        (first_rows, arrived, cotangent, grad_act, small, wide_bias, heads, merge, up, down),
        (),
        (
            shape(images.shape, BF),
            shape(images.shape, BF),
            shape((tall, wide), BF),
            shape((2 * tall * (width // PAIR), tall // count), F32),
            rows_bf,
            shape((tall, hidden_width), BF),
            shape((tall, hidden_width), F32),
            rows_bf,
            rows_wide,
            column,
            rows_bf,
            rows_wide,
            column,
        ),
        [scratch_rows, scratch_rows, scratch_packed],
        2 * work * (wide + width + 2 * hidden_width),
    )
    returned = lax.ppermute(sent, "section", [(1, 0)])

    *grads, grad_in = call(
        bind(rest_grad_kernel),
        "rest_grad",
        info,
        (returned, cotangent, small, heads, merge, up, down, packed, probs, mixed, act, slope, *kept),
        (),
        (shape((hidden_width // shards + 16, width), BF),) * shards
        + (shape((part, hidden_width), BF),) * shards
        + (shape((part, wide + width), BF),) * shards
        + (shape(images.shape, F32),),
        [
            scratch_rows,
            scratch_packed,
            pltpu.VMEM((width, hidden_width), BF),
            pltpu.VMEM((width, wide), BF),
            pltpu.VMEM((width, width), BF),
            pltpu.VMEM((16, width), F32),
        ],
        2 * work * (wide + width + 2 * hidden_width),
    )
    down_total, up_total, rest_total, up_sum = totals_over(
        [grads[n * shards : (n + 1) * shards] for n in range(3)], ("fsdp", "dp")
    )
    layer_out, grad_in = after(layer_out, up_sum), after(grad_in, up_sum)

    vectors, down_total = down_total[-16:], down_total[:-16]
    heads_total, merge_total = jnp.concatenate(rest_total[:3], axis=1), rest_total[3]
    vector_total = lax.dynamic_slice(vectors, (0, me * part), (8, part))
    up_bias_total = lax.dynamic_slice(vectors, (8 + me, 0), (1, width))
    row = lambda n: vector_total[n : n + 1]
    return (
        layer_out[None],
        grad_in[None],
        row(PRE_GAIN),
        row(PRE_SHIFT),
        heads_total[None],
        row(QUERY_BIAS),
        row(VALUE_BIAS),
        merge_total[None],
        row(MERGE_BIAS),
        row(MID_GAIN),
        row(MID_SHIFT),
        up_total[None],
        up_bias_total,
        down_total[None],
        row(DOWN_BIAS),
    )


def solution(mesh):
    vector, matrix = P("section", "fsdp"), P("section", "fsdp", None)
    rows = P("section", ("fsdp", "dp"), None, None)
    weights = (
        vector,
        vector,
        matrix,
        vector,
        vector,
        matrix,
        vector,
        vector,
        vector,
        matrix,
        vector,
        matrix,
        vector,
    )
    blocks = P(("fsdp", "dp"), None, None)
    return jax.shard_map(
        local,
        mesh=mesh,
        in_specs=(blocks, P(("fsdp", "dp"), None), blocks, *weights),
        out_specs=(rows, rows, *weights),
        check_vma=False,
    )
```

```python
import functools

import jax
import jax.numpy as jnp
from jax import lax
from jax.experimental import pallas as pl
from jax.experimental.pallas import tpu as pltpu
from jax.sharding import PartitionSpec as P

HD = 64
PAIR = 2 * HD
EPS = 1e-06
SQRT_HALF = 0.7071067811865476
INV_ROOT_TAU = 0.3989422804014327
BF = jnp.bfloat16
F32 = jnp.float32
VMEM_BYTES = 20 * 1024 * 1024

PRE_GAIN, PRE_SHIFT, QUERY_BIAS, VALUE_BIAS, MERGE_BIAS, MID_GAIN, MID_SHIFT, DOWN_BIAS = range(8)


def padded_length(length):
    return -(-length // 16) * 16


def dot(a, b):
    return jnp.dot(a, b, preferred_element_type=F32)


def dot_nt(a, b):
    return lax.dot_general(a, b, (((1,), (1,)), ((), ())), preferred_element_type=F32)


def dot_tn(a, b):
    return lax.dot_general(a, b, (((0,), (0,)), ((), ())), preferred_element_type=F32)


def fetch(pieces, dest, sems, first, me, rows=None, column=0, half=0):
    copies = []
    for k, piece in enumerate(pieces):
        if rows is not None:
            piece = piece.at[pl.ds(0, rows), pl.ds(column, dest.shape[1])]
        blocks = piece if isinstance(piece, tuple) else (piece,)
        count, wide = blocks[0].shape
        start = pl.multiple_of(jnp.bitwise_xor(me, k) * count, count)
        for n, one in enumerate(blocks):
            target = dest.at[pl.ds(start, count)]
            if len(blocks) > 1:
                target = dest.at[pl.ds(start, count), pl.ds(pl.multiple_of(jnp.bitwise_xor(half, n) * wide, wide), wide)]
            copies.append(pltpu.make_async_copy(one, target, sems.at[first + len(copies)]))
    for copy in copies:
        copy.start()
    return copies


def arrive(copies):
    for copy in copies:
        copy.wait()


def pad_images(images, scratch):
    length = images[0].shape[0]
    step = padded_length(length)
    scratch[...] = jnp.zeros_like(scratch)
    for n, image in enumerate(images):
        scratch[n * step : n * step + length, :] = image.astype(F32)
    return scratch[...]


def unpad(ref, rows, kind):
    count, length, _ = ref.shape
    step = padded_length(length)
    for n in range(count):
        ref[n] = rows[n * step : n * step + length, :].astype(kind)


def norm_parts(rows):
    mean = jnp.mean(rows, axis=-1, keepdims=True)
    centered = rows - mean
    inverse = lax.rsqrt(jnp.mean(centered * centered, axis=-1, keepdims=True) + EPS)
    return centered * inverse, inverse


def norm_backward(grad_rows, normed, inverse, gain):
    scaled = grad_rows * gain
    mean_one = jnp.mean(scaled, axis=-1, keepdims=True)
    mean_two = jnp.mean(scaled * normed, axis=-1, keepdims=True)
    return inverse * (scaled - mean_one - normed * mean_two)


def column_sum(rows):
    return jnp.sum(rows, axis=0, keepdims=True)


def half_masks():
    lane = lax.broadcasted_iota(jnp.int32, (1, PAIR), 1)
    low = (lane < HD).astype(F32)
    return low.astype(BF), (1.0 - low).astype(BF)


def both_heads(rows):
    low, high = half_masks()
    return jnp.concatenate([rows * low, rows * high], axis=0)


def beside(stacked):
    half = stacked.shape[0] // 2
    lane = lax.broadcasted_iota(jnp.int32, (half, PAIR), 1)
    return jnp.where(lane < HD, stacked[:half], stacked[half:])


def qkv(packed, n, pair, step, width):
    rows = slice(n * step, (n + 1) * step)
    return tuple(packed[rows, part * width + pair * PAIR : part * width + (pair + 1) * PAIR] for part in range(3))


def head_pairs(packed, count, length, width):
    step = padded_length(length)
    parts = [qkv(packed, n, pair, step, width) for n in range(count) for pair in range(width // PAIR)]
    return [both_heads(queries) for queries, _, _ in parts], [keys for _, keys, _ in parts], [v for _, _, v in parts]


def block(rows, n, total):
    high = rows.shape[0] // total
    return rows[n * high : (n + 1) * high]


def attention_forward(packed, mixed, count, length, width):
    step = padded_length(length)
    queries, keys, values = head_pairs(packed, count, length, width)
    scores = jnp.concatenate([dot_nt(q, k) for q, k in zip(queries, keys)], axis=0) * HD**-0.5
    lane = lax.broadcasted_iota(jnp.int32, scores.shape, 1)
    scores = jnp.where(lane < length, scores, -1e30)
    grown = jnp.exp(scores - jnp.max(scores, axis=-1, keepdims=True))
    probs = grown * (1.0 / jnp.sum(grown, axis=-1, keepdims=True))
    rounded = probs.astype(BF)
    outs = [beside(dot(block(rounded, at, len(values)), v)).astype(BF) for at, v in enumerate(values)]
    for at, out in enumerate(outs):
        n, pair = divmod(at, width // PAIR)
        mixed[n * step : (n + 1) * step, pair * PAIR : (pair + 1) * PAIR] = out
    return probs


def attention_backward(packed, probs, grad_mixed, grad_packed, count, length, width):
    step = padded_length(length)
    queries, keys, values = head_pairs(packed, count, length, width)
    pairs = width // PAIR
    incoming = [
        both_heads(grad_mixed[n * step : (n + 1) * step, pair * PAIR : (pair + 1) * PAIR])
        for n in range(count)
        for pair in range(pairs)
    ]
    grad_probs = jnp.concatenate([dot_nt(g, v) for g, v in zip(incoming, values)], axis=0)
    inner = jnp.sum(probs * grad_probs, axis=-1, keepdims=True)
    grad_scores = (probs * (grad_probs - inner)).astype(BF)
    rounded = probs.astype(BF)
    total = len(keys)
    parts = [
        (
            beside(dot(block(grad_scores, at, total), keys[at])) * HD**-0.5,
            dot_tn(block(grad_scores, at, total), queries[at]) * HD**-0.5,
            dot_tn(block(rounded, at, total), incoming[at]),
        )
        for at in range(total)
    ]
    for at, three in enumerate(parts):
        n, pair = divmod(at, pairs)
        for part, value in enumerate(three):
            column = part * width + pair * PAIR
            grad_packed[n * step : (n + 1) * step, column : column + PAIR] = value.astype(BF)


def entry_rows(rows, small):
    normed, inverse = norm_parts(rows)
    return (normed * small[PRE_GAIN : PRE_GAIN + 1] + small[PRE_SHIFT : PRE_SHIFT + 1]).astype(BF), normed, inverse


def mid_rows(middle, small):
    normed, inverse = norm_parts(middle)
    return (normed * small[MID_GAIN : MID_GAIN + 1] + small[MID_SHIFT : MID_SHIFT + 1]).astype(BF), normed, inverse


def packed_bias(small):
    query = small[QUERY_BIAS : QUERY_BIAS + 1]
    return jnp.concatenate([query, jnp.zeros_like(query), small[VALUE_BIAS : VALUE_BIAS + 1]], axis=1)


def gelu_parts(hidden):
    bell = 0.5 * (1.0 + lax.erf(hidden * SQRT_HALF))
    return hidden * bell, bell


def gelu_slope(hidden, bell):
    return bell + hidden * jnp.exp(-0.5 * hidden * hidden) * INV_ROOT_TAU


def picked_images(info, images):
    return [
        jnp.where(info[2 + n] == 0, images[0], images[1]) for n in range(images.shape[0])
    ]


def pack_kernel(info, heads_ref, merge_ref, up_ref, *refs):
    many = (len(refs) - 4) // 2
    vectors, (out_ref, half_ref, rows, *held), sems = refs[:many], refs[many : 2 * many + 3], refs[-1]
    part, wide = heads_ref.shape
    half = half_ref.shape[1]
    columns = pl.ds(pl.multiple_of(info[0] * half, half), half)
    copies = [
        pltpu.make_async_copy(heads_ref, out_ref.at[pl.ds(0, part), pl.ds(0, wide)], sems.at[0]),
        pltpu.make_async_copy(merge_ref, out_ref.at[pl.ds(0, part), pl.ds(wide, merge_ref.shape[1])], sems.at[1]),
        pltpu.make_async_copy(up_ref.at[:, columns], half_ref, sems.at[2]),
    ]
    copies += [pltpu.make_async_copy(v, held[n], sems.at[3 + n]) for n, v in enumerate(vectors)]
    for copy in copies:
        copy.start()
    rows[...] = jnp.zeros_like(rows)
    arrive(copies[3:])
    for n, vector in enumerate(held):
        rows[n : n + 1, : vector.shape[1]] = vector[...].astype(F32)
    out_ref[part:, :] = rows[...].astype(BF)
    arrive(copies[:3])


def pick_kernel(info, images, mix_ref, rows_ref, unit_ref, own_ref, sem):
    copy = pltpu.make_async_copy(mix_ref, own_ref, sem)
    copy.start()
    unit_ref[...], _ = norm_parts(pad_images(picked_images(info, images), rows_ref))
    copy.wait()


def attend_kernel(shards, count, length, info, rows_ref, unit_ref, *refs):
    pieces = refs[:shards]
    middle_ref, mid_ref, heads, merge, small, up_bias, packed, mixed, vectors, sems = refs[shards:]
    me = info[0]
    width = rows_ref.shape[1]
    part = width // shards
    first = fetch(pieces, heads, sems, 0, me, part)
    second = fetch(pieces, merge, sems, shards, me, part, heads.shape[1])
    third = []
    for k, piece in enumerate(pieces):
        source = piece.at[pl.ds(part, 16)]
        third.append(pltpu.make_async_copy(source, vectors.at[jnp.bitwise_xor(me, k)], sems.at[2 * shards + k]))
        third[-1].start()
    arrive(third)
    hidden_part = up_bias.shape[1] // shards
    for at in range(shards):
        given = vectors[at].astype(F32)
        small[:, at * part : (at + 1) * part] = given[:8, :part]
        up_bias[:, at * hidden_part : (at + 1) * hidden_part] = given[8:9, :hidden_part]
    arrive(first)
    arrive(second)

    @pl.when(info[1] == 0)
    def _():
        entry = (unit_ref[...] * small[PRE_GAIN : PRE_GAIN + 1] + small[PRE_SHIFT : PRE_SHIFT + 1]).astype(BF)
        packed[...] = (dot(entry, heads[...]) + packed_bias(small)).astype(BF)
        attention_forward(packed, mixed, count, length, width)
        middle = rows_ref[...] + dot(mixed[...], merge[...]) + small[MERGE_BIAS : MERGE_BIAS + 1]
        middle_ref[...] = middle
        mid_ref[...] = mid_rows(middle, small)[0]


def feed_forward_kernel(shards, info, mid_ref, middle_ref, small, up_bias, *refs):
    near, far = refs[: shards // 2], refs[shards // 2 : shards * 3 // 2]
    down_pieces = refs[shards * 3 // 2 : shards * 5 // 2]
    out_ref, up, down, sems = refs[shards * 5 // 2 :]
    me = info[0]
    first = fetch((*near, *zip(far[::2], far[1::2])), up, sems, 0, me, half=info[4])
    second = fetch(down_pieces, down, sems, 2 * shards, me)
    arrive(first)
    arrive(second)

    @pl.when(info[1] == 0)
    def _():
        hidden = dot(mid_ref[...], up[...]) + up_bias[...]
        act = gelu_parts(hidden)[0].astype(BF)
        out = middle_ref[...] + dot(act, down[...]) + small[DOWN_BIAS : DOWN_BIAS + 1]
        unpad(out_ref, out, BF)


def act_gradient_kernel(cotangent, down, grad_act_ref, grad_ref):
    incoming = pad_images([cotangent[n] for n in range(cotangent.shape[0])], grad_ref)
    grad_act_ref[...] = dot_nt(incoming.astype(BF), down[...])


def both_ways_kernel(
    info,
    first_rows,
    arrived,
    cotangent,
    grad_act,
    small,
    up_bias,
    heads,
    merge,
    up,
    down,
    out_ref,
    sent_ref,
    packed,
    probs_ref,
    mixed,
    act_ref,
    slope_ref,
    entry_ref,
    unit_one_ref,
    inverse_one_ref,
    mid_ref,
    unit_two_ref,
    inverse_two_ref,
    rows_ref,
    grad_ref,
    grad_packed,
):
    leading = info[1] == 0
    count, length, width = arrived.shape
    rows = jnp.where(leading, first_rows[...], pad_images([arrived[n] for n in range(count)], rows_ref))
    entry_ref[...], unit_one_ref[...], inverse_one_ref[...] = entry_rows(rows, small)
    packed[...] = (dot(entry_ref[...], heads[...]) + packed_bias(small)).astype(BF)
    probs_ref[...] = attention_forward(packed, mixed, count, length, width)
    middle = rows + dot(mixed[...], merge[...]) + small[MERGE_BIAS : MERGE_BIAS + 1]
    mid_ref[...], unit_two_ref[...], inverse_two_ref[...] = mid_rows(middle, small)
    hidden = dot(mid_ref[...], up[...]) + up_bias[...]
    act, bell = gelu_parts(hidden)
    slope_ref[...] = gelu_slope(hidden, bell)
    act_ref[...] = act.astype(BF)
    out = middle + dot(act_ref[...], down[...]) + small[DOWN_BIAS : DOWN_BIAS + 1]
    unpad(out_ref, out, BF)
    incoming = pad_images([cotangent[n] for n in range(count)], grad_ref)
    grad_hidden = (grad_act[...] * slope_ref[...]).astype(BF)
    grad_mid = dot_nt(grad_hidden, up[...])
    grad_middle = incoming + norm_backward(
        grad_mid, unit_two_ref[...], inverse_two_ref[...], small[MID_GAIN : MID_GAIN + 1]
    )
    grad_mixed = dot_nt(grad_middle.astype(BF), merge[...]).astype(BF)
    attention_backward(packed, probs_ref[...], grad_mixed, grad_packed, count, length, width)
    grad_entry = dot_nt(grad_packed[...], heads[...])
    grad_in = grad_middle + norm_backward(
        grad_entry, unit_one_ref[...], inverse_one_ref[...], small[PRE_GAIN : PRE_GAIN + 1]
    )
    unpad(sent_ref, grad_in, BF)


def own_gradient(info, returned, cotangent, scratch):
    leading = info[1] == 0
    return pad_images(
        [jnp.where(leading, returned[n], cotangent[n]) for n in range(cotangent.shape[0])], scratch
    )


def rest_grad_kernel(
    shards,
    info,
    returned,
    cotangent,
    small,
    heads,
    merge,
    up,
    down,
    packed,
    probs_ref,
    mixed,
    act_ref,
    slope_ref,
    entry_ref,
    unit_one_ref,
    inverse_one_ref,
    mid_ref,
    unit_two_ref,
    inverse_two_ref,
    *refs,
):
    down_outs, up_outs, rest_outs = (refs[n * shards : (n + 1) * shards] for n in range(3))
    grad_in_ref, grad_ref, grad_packed, whole_up, whole_heads, whole_merge, extra = refs[3 * shards :]
    me, leading = info[0], info[1] == 0
    count, length, width = cotangent.shape
    part = width // shards
    incoming = own_gradient(info, returned, cotangent, grad_ref)
    extra[...] = jnp.zeros_like(extra)
    extra[DOWN_BIAS : DOWN_BIAS + 1, :] = column_sum(incoming)
    grad_out = incoming.astype(BF)
    high = act_ref.shape[1] // shards
    for k in range(shards):
        columns = pl.ds(pl.multiple_of(jnp.bitwise_xor(me, k) * high, high), high)
        down_outs[k][:high, :] = dot_tn(act_ref[:, columns], grad_out).astype(BF)
    grad_hidden = (dot_nt(grad_out, down[...]) * slope_ref[...]).astype(BF)
    whole_up[...] = dot_tn(mid_ref[...], grad_hidden).astype(BF)
    wide_sum = column_sum(grad_hidden.astype(F32))
    for n in range(wide_sum.shape[1] // width):
        extra[8 + n : 9 + n, :] = wide_sum[:, n * width : (n + 1) * width]
    grad_mid = dot_nt(grad_hidden, up[...])
    extra[MID_GAIN : MID_GAIN + 1, :] = column_sum(grad_mid * unit_two_ref[...])
    extra[MID_SHIFT : MID_SHIFT + 1, :] = column_sum(grad_mid)
    grad_middle = incoming + norm_backward(
        grad_mid, unit_two_ref[...], inverse_two_ref[...], small[MID_GAIN : MID_GAIN + 1]
    )
    grad_branch = grad_middle.astype(BF)
    extra[MERGE_BIAS : MERGE_BIAS + 1, :] = column_sum(grad_branch.astype(F32))
    whole_merge[...] = dot_tn(mixed[...], grad_branch).astype(BF)
    grad_mixed = dot_nt(grad_branch, merge[...]).astype(BF)
    attention_backward(packed, probs_ref[...], grad_mixed, grad_packed, count, length, width)
    packed_sum = column_sum(grad_packed[...].astype(F32))
    extra[QUERY_BIAS : QUERY_BIAS + 1, :] = packed_sum[:, :width]
    extra[VALUE_BIAS : VALUE_BIAS + 1, :] = packed_sum[:, 2 * width :]
    whole_heads[...] = dot_tn(entry_ref[...], grad_packed[...]).astype(BF)
    grad_entry = dot_nt(grad_packed[...], heads[...])
    extra[PRE_GAIN : PRE_GAIN + 1, :] = column_sum(grad_entry * unit_one_ref[...])
    extra[PRE_SHIFT : PRE_SHIFT + 1, :] = column_sum(grad_entry)
    grad_in = grad_middle + norm_backward(
        grad_entry, unit_one_ref[...], inverse_one_ref[...], small[PRE_GAIN : PRE_GAIN + 1]
    )
    rounded = grad_in.astype(BF).astype(F32)
    unpad(grad_in_ref, jnp.where(leading, grad_in, rounded), F32)
    wide = whole_heads.shape[1]
    for k in range(shards):
        rows = pl.ds(pl.multiple_of(jnp.bitwise_xor(me, k) * part, part), part)
        up_outs[k][...] = whole_up[rows, :]
        rest_outs[k][:, :wide] = whole_heads[rows, :]
        rest_outs[k][:, wide:] = whole_merge[rows, :]
        down_outs[k][high:, :] = extra[...].astype(BF)


def column_blocks_kernel(at, *refs):
    outs = [ref for ref in refs if ref.shape != refs[0].shape]
    wide = outs[0].shape[1]
    for k, out in enumerate(outs):
        columns = pl.ds(pl.multiple_of(jnp.bitwise_xor(at[0], k) * wide, wide), wide)
        out[...] = sum(ref[:, columns].astype(F32) for ref in refs[: len(refs) - len(outs)]).astype(BF)


def call(kernel, name, info, blocks, pieces, outs, scratch, flops, earlier=(), room=VMEM_BYTES):
    space = lambda kind, many: [pl.BlockSpec(memory_space=kind)] * many
    nbytes = sum(a.size * a.dtype.itemsize for a in (*blocks, *pieces, *outs))
    scalars = () if info is None else (info,)
    used = len(scalars) + len(blocks) + len(pieces)
    return pl.pallas_call(
        lambda *refs: kernel(*refs[:used], *refs[used + len(earlier) :]),
        out_shape=outs,
        in_specs=space(pltpu.SMEM, len(scalars)) + space(pltpu.VMEM, len(blocks)) + space(pl.ANY, len(pieces) + len(earlier)),
        out_specs=space(pltpu.VMEM, len(outs)),
        scratch_shapes=scratch,
        compiler_params=pltpu.CompilerParams(vmem_limit_bytes=room),
        cost_estimate=pl.CostEstimate(flops=flops, bytes_accessed=nbytes, transcendentals=0),
        name=name,
    )(*scalars, *blocks, *pieces, *earlier)


def after(value, *others):
    return lax.optimization_barrier((value, *others))[0]


def swapped(block, axis, bit):
    return lax.ppermute(block, axis, [(i, i ^ bit) for i in range(lax.axis_size(axis))])


def bits_of(size):
    return [1 << n for n in range(size.bit_length() - 1)]


def gather_nearer(pieces, axis):
    for bit in bits_of(lax.axis_size(axis))[:-1]:
        pieces = pieces + [swapped(piece, axis, bit) for piece in pieces]
    return pieces


def gather_pieces(shard, axis, *earlier):
    pieces = {0: shard}
    for bit in reversed(bits_of(lax.axis_size(axis))):
        pieces.update({k ^ bit: swapped(piece if k == 0 else after(piece, *earlier), axis, bit) for k, piece in list(pieces.items())})
    return [pieces[k] for k in range(len(pieces))]


def added(*terms):
    return sum(term.astype(F32) for term in terms).astype(BF)


def nearer_sums(pieces, axis):
    terms = {k: (piece,) for k, piece in enumerate(pieces)}
    *nearer, last = bits_of(lax.axis_size(axis))
    for bit in nearer:
        for k in sorted((k for k in terms if not k & bit), reverse=True):
            terms[k] += (swapped(added(*terms.pop(k ^ bit)), axis, bit),)
    return added(*terms[last]), terms[0]


def together(*values):
    return lax.optimization_barrier(values)


def rounded(*terms):
    return lax.reduce_precision(sum(term.astype(F32) for term in terms), 8, 7).astype(BF)


def chosen(at, options):
    while len(options) > 1:
        options = [jnp.where((at & 1) != 0, odd, even) for even, odd in zip(options[::2], options[1::2])]
        at = at >> 1
    return options[0]


def column_blocks(at, terms, count):
    high, wide = terms[0].shape
    shapes = (jax.ShapeDtypeStruct((high, wide // count), BF),) * count
    return call(column_blocks_kernel, "column_blocks", at.reshape(1), terms, (), shapes, [], 1)


def totals_over_line(leaving, kept, axes):
    scattered, axis = axes
    at = lax.axis_index(axis).astype(jnp.int32)
    size = lax.axis_size(axis)
    odd = (at & 1) != 0
    far = lambda block: swapped(block, scattered, lax.axis_size(scattered) // 2)
    others = lambda blocks: [swapped(blocks[k], axis, k) for k in range(1, size)]
    lower = lambda block: block[: block.shape[0] // 2]
    upper = lambda block: block[block.shape[0] // 2 :]
    own_half = lambda block: jnp.where(odd, upper(block), lower(block))
    other_half = lambda block: jnp.where(odd, lower(block), upper(block))
    whole = lambda own, other: jnp.concatenate([jnp.where(odd, other, own), jnp.where(odd, own, other)]).astype(F32)

    down_far, *leaving = together(far(leaving[0]), *leaving[1:])
    down = added(*kept[0], down_far)

    down_near = swapped(other_half(down), axis, 1)
    rest = after(leaving[1], down_near)
    up_far, down_near = after(far(leaving[0]), down_near), down_near
    up, down = added(*kept[1], up_far), added(own_half(down), down_near)

    rest_far, up_near, down_next = together(far(rest), swapped(other_half(up), axis, 1), swapped(down, axis, 2))
    blocks = column_blocks(at, (*kept[2], rest_far), size)
    up, down = added(own_half(up), up_near), rounded(down, down_next)

    down_back = swapped(down, axis, 1)
    up_next, *received = together(swapped(up, axis, 2), *others(blocks))
    own, up_full = rounded(blocks[0], *received), rounded(up, up_next)

    up_total = whole(up_full, swapped(up_full, axis, 1))
    full = [own, *after(tuple(others([own] * size)), up_total)]
    rest_total = [chosen(at, [full[n ^ k] for k in range(size)]).astype(F32) for n in range(size)]
    return whole(down, down_back), up_total, rest_total, up


def totals_over(grads, axes):
    scattered, axis = axes
    first, later = grads[0], grads[1:]
    first_leaving, first_kept = nearer_sums(first, scattered)
    first_leaving, *tied = together(first_leaving, *later)
    leaving, kept = zip((first_leaving, first_kept), *(nearer_sums(pieces, scattered) for pieces in tied))
    if lax.axis_size(axis) == 4:
        return totals_over_line(leaving, kept, axes)
    last = lax.axis_size(scattered) // 2
    sums = tuple(added(*terms, swapped(one, scattered, last)) for one, terms in zip(leaving, kept))
    down, up, rest = (total.astype(F32) for total in lax.psum(sums, axis))
    return down, up, jnp.split(rest, 4, axis=1), sums[1]


def local(
    images,
    slot_image,
    cotangent,
    pre_gain,
    pre_shift,
    heads_weight,
    query_bias,
    value_bias,
    merge_weight,
    merge_bias,
    mid_gain,
    mid_shift,
    up_weight,
    up_bias,
    down_weight,
    down_bias,
):
    me = lax.axis_index("fsdp").astype(jnp.int32)
    section = lax.axis_index("section").astype(jnp.int32)
    shards = lax.axis_size("fsdp")
    half = lax.axis_index("dp").astype(jnp.int32) & 1
    info = jnp.concatenate([jnp.stack([me, section]), slot_image[0], half[None]])
    count, length, width = images.shape
    tall = count * padded_length(length)
    part = width // shards
    wide = heads_weight.shape[2]
    hidden_width = up_weight.shape[2]

    shape = jax.ShapeDtypeStruct
    scratch_rows = pltpu.VMEM((tall, width), F32)
    scratch_packed = pltpu.VMEM((tall, wide), BF)
    scratch_mixed = pltpu.VMEM((tall, width), BF)
    sems = lambda many: pltpu.SemaphoreType.DMA((many * shards,))
    bind = lambda kernel: functools.partial(kernel, shards)
    work = 2 * tall * width
    full_heads, full_merge = shape((width, wide), BF), shape((width, width), BF)
    full_up, full_down = shape((width, hidden_width), BF), shape((hidden_width, width), BF)
    rows_wide, rows_bf, column = shape((tall, width), F32), shape((tall, width), BF), shape((tall, 1), F32)

    mix, up_half = call(
        pack_kernel,
        "pack",
        half.reshape(1),
        (),
        (
            heads_weight[0],
            merge_weight[0],
            up_weight[0],
            pre_gain,
            pre_shift,
            query_bias,
            value_bias,
            merge_bias,
            mid_gain,
            mid_shift,
            down_bias,
            up_bias,
        ),
        (shape((part + 16, wide + width), BF), shape((part, hidden_width // 2), BF)),
        [pltpu.VMEM((16, wide + width), F32)]
        + [pltpu.VMEM((1, part), BF)] * 8
        + [pltpu.VMEM(up_bias.shape, BF), pltpu.SemaphoreType.DMA((12,))],
        1,
        room=56 * 1024 * 1024,
    )
    first_rows, first_unit, own_mix = call(
        pick_kernel,
        "pick",
        info,
        (images,),
        (mix,),
        (rows_wide, rows_wide, shape(mix.shape, BF)),
        [pltpu.SemaphoreType.DMA(())],
        1,
    )
    farthest = shards // 2
    up_far = swapped(up_half, "fsdp", farthest)
    mix_pieces = [own_mix, *gather_pieces(mix, "fsdp", up_far, first_rows)[1:]]
    up_other = swapped(after(up_far, mix_pieces[-1]), "dp", 1)
    up_near = gather_nearer([up_weight[0]], "fsdp")
    up_halves = [gather_nearer([one], "fsdp") for one in (up_far, up_other)]

    middle, mid, heads, merge, small, wide_bias = call(
        functools.partial(attend_kernel, shards, count, length),
        "attend",
        info,
        (first_rows, first_unit),
        mix_pieces,
        (rows_wide, rows_bf, full_heads, full_merge, shape((8, width), F32), shape((1, hidden_width), F32)),
        [
            scratch_packed,
            scratch_mixed,
            pltpu.VMEM((shards, 16, wide + width), BF),
            sems(3),
        ],
        work * (wide + width),
    )
    down_pieces = gather_pieces(down_weight[0], "fsdp", mid, *(one for two in up_halves for one in two))
    first_out, up, down = call(
        bind(feed_forward_kernel),
        "feed_forward",
        info,
        (mid, middle, small, wide_bias),
        (*up_near, *(one for two in zip(*up_halves) for one in two), *down_pieces),
        (shape(images.shape, BF), full_up, full_down),
        [sems(3)],
        2 * work * hidden_width,
    )
    arrived = lax.ppermute(first_out, "section", [(0, 1)])

    (grad_act,) = call(
        act_gradient_kernel,
        "act_gradient",
        None,
        (cotangent, down),
        (),
        (shape((tall, hidden_width), F32),),
        [scratch_rows],
        work * hidden_width,
    )

    layer_out, sent, packed, probs, mixed, act, slope, *kept = call(
        both_ways_kernel,
        "both_ways",
        info,
        (first_rows, arrived, cotangent, grad_act, small, wide_bias, heads, merge, up, down),
        (),
        (
            shape(images.shape, BF),
            shape(images.shape, BF),
            shape((tall, wide), BF),
            shape((2 * tall * (width // PAIR), tall // count), F32),
            rows_bf,
            shape((tall, hidden_width), BF),
            shape((tall, hidden_width), F32),
            rows_bf,
            rows_wide,
            column,
            rows_bf,
            rows_wide,
            column,
        ),
        [scratch_rows, scratch_rows, scratch_packed],
        2 * work * (wide + width + 2 * hidden_width),
    )
    returned = lax.ppermute(sent, "section", [(1, 0)])

    *grads, grad_in = call(
        bind(rest_grad_kernel),
        "rest_grad",
        info,
        (returned, cotangent, small, heads, merge, up, down, packed, probs, mixed, act, slope, *kept),
        (),
        (shape((hidden_width // shards + 16, width), BF),) * shards
        + (shape((part, hidden_width), BF),) * shards
        + (shape((part, wide + width), BF),) * shards
        + (shape(images.shape, F32),),
        [
            scratch_rows,
            scratch_packed,
            pltpu.VMEM((width, hidden_width), BF),
            pltpu.VMEM((width, wide), BF),
            pltpu.VMEM((width, width), BF),
            pltpu.VMEM((16, width), F32),
        ],
        2 * work * (wide + width + 2 * hidden_width),
    )
    down_total, up_total, rest_total, up_sum = totals_over(
        [grads[n * shards : (n + 1) * shards] for n in range(3)], ("fsdp", "dp")
    )
    layer_out, grad_in = after(layer_out, up_sum), after(grad_in, up_sum)

    vectors, down_total = down_total[-16:], down_total[:-16]
    heads_total, merge_total = jnp.concatenate(rest_total[:3], axis=1), rest_total[3]
    vector_total = lax.dynamic_slice(vectors, (0, me * part), (8, part))
    up_bias_total = lax.dynamic_slice(vectors, (8 + me, 0), (1, width))
    row = lambda n: vector_total[n : n + 1]
    return (
        layer_out[None],
        grad_in[None],
        row(PRE_GAIN),
        row(PRE_SHIFT),
        heads_total[None],
        row(QUERY_BIAS),
        row(VALUE_BIAS),
        merge_total[None],
        row(MERGE_BIAS),
        row(MID_GAIN),
        row(MID_SHIFT),
        up_total[None],
        up_bias_total,
        down_total[None],
        row(DOWN_BIAS),
    )


def solution(mesh):
    vector, matrix = P("section", "fsdp"), P("section", "fsdp", None)
    rows = P("section", ("fsdp", "dp"), None, None)
    weights = (
        vector,
        vector,
        matrix,
        vector,
        vector,
        matrix,
        vector,
        vector,
        vector,
        matrix,
        vector,
        matrix,
        vector,
    )
    blocks = P(("fsdp", "dp"), None, None)
    return jax.shard_map(
        local,
        mesh=mesh,
        in_specs=(blocks, P(("fsdp", "dp"), None), blocks, *weights),
        out_specs=(rows, rows, *weights),
        check_vma=False,
    )
```
